32 devices in a mesh: dp: 2 (over core), fsdp: 16 (over z, y, x).
Axes of the slice: x: 2, y: 2, z: 4, core: 2. Of those that a mesh axis runs over, the one named last changes fastest.
Arguments:
- tokens: bfloat16 [2, 8192, 768], P(None, ('dp', 'fsdp')), may hold values from -6 to 6
- cotangent: bfloat16 [2, 8192, 768], P(None, ('dp', 'fsdp')), may hold values from -6 to 6
- routes: int32 [2, 8192, 1], P(None, ('dp', 'fsdp')), may hold values from 0 to 15
- lengths: int32 [2, 32, 2], P(None, ('dp', 'fsdp')), may hold values from 32 to 224, as said below
- norm1_gain: bfloat16 [768], P(('dp', 'fsdp')), may hold values from 0.5 to 1.5
- input_weight: bfloat16 [768, 3072], P(('dp', 'fsdp')), may hold values from -0.21875 to 0.21875
- conv_weight: bfloat16 [1536, 4], P(('dp', 'fsdp')), may hold values from -3 to 3
- conv_bias: bfloat16 [1536], P(('dp', 'fsdp')), may hold values from -1.5 to 1.5
- scan_weight: bfloat16 [1536, 80], P(('dp', 'fsdp')), may hold values from -0.15625 to 0.15625
- step_weight: bfloat16 [1536, 48], P(('dp', 'fsdp')), may hold values from -0.875 to 0.875
- step_bias: bfloat16 [1536], P(('dp', 'fsdp')), may hold values from -4.59375 to -2.296875
- decay_log: bfloat16 [1536, 16], P(('dp', 'fsdp')), may hold values from 0 to 2.765625
- skip_gain: bfloat16 [1536], P(('dp', 'fsdp')), may hold values from 0.5 to 1.5
- out_weight: bfloat16 [1536, 768], P(('dp', 'fsdp')), may hold values from -0.15625 to 0.15625
- norm2_gain: bfloat16 [768], P(('dp', 'fsdp')), may hold values from 0.5 to 1.5
- router_weight: bfloat16 [768, 16], P(('dp', 'fsdp')), may hold values from -0.15625 to 0.15625
- expert_up: bfloat16 [16, 768, 3072], P('fsdp', None, 'dp'), may hold values from -0.21875 to 0.21875
- expert_down: bfloat16 [16, 3072, 768], P('fsdp', 'dp'), may hold values from -1.75 to 1.75
Outputs:
- block_output: bfloat16 [2, 8192, 768], P(None, ('dp', 'fsdp'))
- tokens_grad: float32 [2, 8192, 768], P(None, ('dp', 'fsdp'))
- norm1_gain_grad: float32 [768], P(('dp', 'fsdp'))
- input_weight_grad: float32 [768, 3072], P(('dp', 'fsdp'))
- conv_weight_grad: float32 [1536, 4], P(('dp', 'fsdp'))
- conv_bias_grad: float32 [1536], P(('dp', 'fsdp'))
- scan_weight_grad: float32 [1536, 80], P(('dp', 'fsdp'))
- step_weight_grad: float32 [1536, 48], P(('dp', 'fsdp'))
- step_bias_grad: float32 [1536], P(('dp', 'fsdp'))
- decay_log_grad: float32 [1536, 16], P(('dp', 'fsdp'))
- skip_gain_grad: float32 [1536], P(('dp', 'fsdp'))
- out_weight_grad: float32 [1536, 768], P(('dp', 'fsdp'))
- norm2_gain_grad: float32 [768], P(('dp', 'fsdp'))
- router_weight_grad: float32 [768, 16], P(('dp', 'fsdp'))
- expert_up_grad: float32 [16, 768, 3072], P('fsdp', None, 'dp')
- expert_down_grad: float32 [16, 3072, 768], P('fsdp', 'dp')
The draws below stay inside these ranges and needn't reach their ends.
Inputs may be any that keep to these rules, and one draw needn't show every extreme that they name: `routes`: routes of padding rows are ignored. `lengths`: A pack's two entries sum to 256: first its sample's length, from 128 to 224, then its padding. In every micro-batch some pack has the longest sample and another the shortest.
All inputs are finite; a program needn't handle non-finite values.
Results may differ from the reference program's by a relative error of at most 0.013.
Values may be sent and summed in bfloat16 or wider, within the bound.
No kernel may reach another device: no remote copies, remote signals or barrier semaphores. Data moves between devices by JAX's collectives and lax.ppermute only.
A program may use at most 256 MiB of HBM per device.

```python
import math
import jax
import jax.numpy as jnp
from jax import lax

D = 768
INNER = 1536
DSTATE = 16
RANK = 48
KERNEL = 4
FF = 3072
SPAN = 256
TOK_DEV = 256
MB = 2
SEGS = 2
PACKS = 32
TOKENS = 8192
EXPERTS = 16
CAP = 20


def draw_lengths(key, part):
    key = jax.random.fold_in(key, 7)
    shortest = TOK_DEV // 2
    longest = TOK_DEV - TOK_DEV // 8
    first_key, pick_key, other_key = jax.random.split(key, 3)
    sample = jax.random.randint(first_key, (MB, PACKS), shortest, longest + 1, dtype=jnp.int32)
    rows = jnp.arange(MB, dtype=jnp.int32)
    picked = jax.random.randint(pick_key, (MB,), 0, PACKS, dtype=jnp.int32)
    other = (picked + 1 + jax.random.randint(other_key, (MB,), 0, PACKS - 1, dtype=jnp.int32)) % PACKS
    sample = sample.at[rows, picked].set(longest)
    sample = sample.at[rows, other].set(shortest)
    return jnp.stack([sample, TOK_DEV - sample], axis=-1).astype(jnp.int32)


def block_scale(own_key, shape, shards, smallest, high):
    def one(dim, shards_of):
        steps = jax.random.uniform(jax.random.fold_in(jax.random.fold_in(own_key, 6), dim), (shards_of,), jnp.float32, smallest / len(shards), high / len(shards))
        return jnp.repeat(jnp.exp(steps), shape[dim] // shards_of).reshape((-1,) + (1,) * (len(shape) - dim - 1))

    factor_of = one(*shards[0])
    for cut in shards[1:]:
        factor_of = factor_of * one(*cut)
    return factor_of


def different_ones(own_key, rows, number_of, top, lift):
    ranking = jax.random.permutation(jax.random.fold_in(own_key, 1), number_of)
    boost = ranking
    for power in range(3):
        boost = boost * boost // number_of
    boost = boost * lift // number_of
    lots = jax.random.randint(jax.random.fold_in(own_key, 2), (rows, number_of), 0, 4096) + boost
    holders = jax.random.permutation(jax.random.fold_in(own_key, 3), rows)[jnp.arange(number_of) % rows]
    lots = jnp.where(jnp.arange(rows)[:, None] == holders[None, :], 1 << 14, lots)
    score = lots * number_of + jnp.arange(number_of)
    return lax.top_k(score.astype(jnp.int32), top)[1].astype(jnp.int32)


def bell_draw(key, shape, scale, reach, cuts=(), kind=jnp.bfloat16):
    entries = jax.random.normal(key, shape, jnp.float32) * scale
    if len(cuts) > 0:
        entries = block_scale(key, shape, cuts, -0.22, 0.18) * entries
    return jnp.clip(entries, min=-reach, max=reach).astype(kind)


def setup_inputs(seed: int = 0) -> dict:
    seeds = jax.random.split(jax.random.key(seed), 19)
    return {
        "tokens": bell_draw(seeds[0], (MB, TOKENS, D), 1.0, 6.0, ((1, 32),)),
        "cotangent": bell_draw(seeds[1], (MB, TOKENS, D), 1.0, 6.0, ((1, 32),)),
        "routes": different_ones(seeds[2], MB * TOKENS, EXPERTS, 1, 512).reshape((MB, TOKENS, 1)),
        "lengths": draw_lengths(jax.random.fold_in(seeds[18], 71), 0),
        "norm1_gain": jnp.clip(1.0 + 0.1 * jax.random.normal(seeds[4], (D,), jnp.float32), 0.5, 1.5).astype(jnp.bfloat16),
        "input_weight": bell_draw(seeds[5], (D, 2 * INNER), D ** -0.5, 0.21875, ((0, 32),)),
        "conv_weight": bell_draw(seeds[6], (INNER, KERNEL), KERNEL ** -0.5, 3.0, ((0, 32),)),
        "conv_bias": bell_draw(seeds[7], (INNER,), 0.3, 1.5, ((0, 32),)),
        "scan_weight": bell_draw(seeds[8], (INNER, RANK + 2 * DSTATE), INNER ** -0.5, 0.15625, ((0, 32),)),
        "step_weight": bell_draw(seeds[9], (INNER, RANK), RANK ** -0.5, 0.875, ((0, 32),)),
        "step_bias": jnp.clip(-4.59375 + 2.296875 * jax.random.uniform(seeds[10], (INNER,), jnp.float32) ** block_scale(seeds[10], (INNER,), ((0, 32),), -0.2, 0.2), -4.59375, -2.296875).astype(jnp.bfloat16),
        "decay_log": jnp.clip(2.765625 * jax.random.uniform(seeds[11], (INNER, DSTATE), jnp.float32) ** block_scale(seeds[11], (INNER, DSTATE), ((0, 32),), -0.2, 0.2), 0.0, 2.765625).astype(jnp.bfloat16),
        "skip_gain": jnp.clip(0.5 + 1.0 * jax.random.uniform(seeds[12], (INNER,), jnp.float32) ** block_scale(seeds[12], (INNER,), ((0, 32),), -0.2, 0.2), 0.5, 1.5).astype(jnp.bfloat16),
        "out_weight": bell_draw(seeds[13], (INNER, D), INNER ** -0.5, 0.15625, ((0, 32),)),
        "norm2_gain": jnp.clip(1.0 + 0.1 * jax.random.normal(seeds[14], (D,), jnp.float32), 0.5, 1.5).astype(jnp.bfloat16),
        "router_weight": bell_draw(seeds[15], (D, EXPERTS), (2 * D) ** -0.5, 0.15625, ((0, 32),)),
        "expert_up": bell_draw(seeds[16], (EXPERTS, D, FF), D ** -0.5, 0.21875, ((0, 16), (2, 2))),
        "expert_down": bell_draw(seeds[17], (EXPERTS, FF, D), (max(1, FF // (EXPERTS * EXPERTS))) ** -0.5, 1.75, ((0, 16), (1, 2))),
    }


EPSILON = 1e-05
HIGHEST = lax.Precision.HIGHEST

@jax.custom_vjp
def low(v):
    return lax.optimization_barrier(v.astype(jnp.bfloat16)).astype(jnp.float32)

@jax.custom_vjp
def low_back(v):
    return v

def low_keep(v):
    return (low(v), None)

def low_pass(kept, grad):
    return (grad,)

def back_keep(v):
    return (v, None)

def back_low(kept, grad):
    return (low(grad),)
low.defvjp(low_keep, low_pass)
low_back.defvjp(back_keep, back_low)

def product(left, right):
    return jnp.dot(left, right, precision=HIGHEST, preferred_element_type=jnp.float32)

def segment_rows(lengths_row):
    ends = jnp.cumsum(lengths_row)
    places = jnp.arange(TOK_DEV, dtype=jnp.int32)
    return lax.optimization_barrier(jnp.sum((places[:, None] >= ends[None, :]).astype(jnp.int32), axis=1))

def conv_silu(branch_x, segment, conv_weight, conv_bias):
    width = branch_x.shape[1]
    total = conv_bias[None, :] + conv_weight[:, KERNEL - 1][None, :] * branch_x
    for shift in range(1, KERNEL):
        moved = jnp.concatenate([jnp.zeros((shift, width), jnp.float32), branch_x[:-shift]], axis=0)
        moved_segment = jnp.concatenate([jnp.full((shift,), -1, jnp.int32), segment[:-shift]])
        same = (moved_segment == segment).astype(jnp.float32)
        total = total + conv_weight[:, KERNEL - 1 - shift][None, :] * moved * same[:, None]
    return jax.nn.silu(total)

def selective_scan(scan_in, step_size, bmat, cmat, decay_mat, carried):
    count = TOK_DEV // SPAN

    def one_step(state, item):
        size_t, input_t, bvec, cvec, carry_t = item
        state = jnp.exp(size_t[None, :] * decay_mat) * carry_t * state + bvec[:, None] * (size_t * input_t)[None, :]
        return (state, lax.optimization_barrier(jnp.sum(cvec[:, None] * state, axis=0)))

    @jax.checkpoint
    def one_block(state, block):
        return lax.scan(one_step, state, block)
    blocks = (step_size.reshape(count, SPAN, INNER), scan_in.reshape(count, SPAN, INNER), bmat.reshape(count, SPAN, DSTATE), cmat.reshape(count, SPAN, DSTATE), carried.reshape(count, SPAN))
    final, outputs = lax.scan(one_block, jnp.zeros((DSTATE, INNER), jnp.float32), blocks)
    return outputs.reshape(TOK_DEV, INNER)

def mixer(hidden, segment, weights):
    gain_one, input_weight, conv_weight, conv_bias, scan_weight, step_weight, step_bias, decay_log, skip_gain, out_weight = weights
    normed = hidden * lax.rsqrt(lax.optimization_barrier(jnp.mean(hidden * hidden, axis=-1, keepdims=True)) + EPSILON) * gain_one
    projected = low_back(product(low(normed), input_weight))
    branch_x = projected[:, :INNER]
    branch_z = projected[:, INNER:]
    scan_in = conv_silu(branch_x, segment, conv_weight, conv_bias)
    selected = low_back(product(low(scan_in), scan_weight))
    rank_part = selected[:, :RANK]
    bmat = selected[:, RANK:RANK + DSTATE]
    cmat = selected[:, RANK + DSTATE:]
    step_size = jax.nn.softplus(low_back(product(low(rank_part), step_weight.T)) + step_bias)
    decay_mat = (-jnp.exp(decay_log)).T
    previous = jnp.concatenate([jnp.full((1,), -1, jnp.int32), segment[:-1]])
    carried = (segment == previous).astype(jnp.float32)
    scanned = selective_scan(scan_in, step_size, bmat, cmat, decay_mat, carried) + skip_gain * scan_in
    gated = scanned * jax.nn.silu(branch_z)
    return low_back(product(low(gated), out_weight))

def reference(tokens, cotangent, routes, lengths, norm1_gain, input_weight, conv_weight, conv_bias, scan_weight, step_weight, step_bias, decay_log, skip_gain, out_weight, norm2_gain, router_weight, expert_up, expert_down):
    packs = MB * PACKS
    hidden = tokens.astype(jnp.float32).reshape(packs, TOK_DEV, D)
    upstream = cotangent.astype(jnp.float32).reshape(packs, TOK_DEV, D)
    route = routes.reshape(packs, TOK_DEV).astype(jnp.int32)
    segment = jax.vmap(segment_rows)(lengths.reshape(packs, SEGS))
    live = (segment < SEGS - 1).astype(jnp.int32)
    expert_ids = jnp.arange(EXPERTS, dtype=jnp.int32)
    route_hot = (route[:, :, None] == expert_ids[None, None, :]).astype(jnp.int32)
    live_hot = route_hot * live[:, :, None]
    before = jnp.cumsum(live_hot, axis=1) - live_hot
    slot = lax.optimization_barrier(jnp.sum(before * live_hot, axis=2))
    kept = live * (slot < CAP).astype(jnp.int32)
    rows_all = EXPERTS * packs * CAP
    owner = jnp.arange(packs, dtype=jnp.int32)[:, None]
    target = jnp.where(kept == 1, route * (packs * CAP) + owner * CAP + slot, rows_all).astype(jnp.int32)
    weights = tuple((piece.astype(jnp.float32) for piece in (norm1_gain, input_weight, conv_weight, conv_bias, scan_weight, step_weight, step_bias, decay_log, skip_gain, out_weight, norm2_gain, router_weight, expert_up, expert_down)))
    group = math.gcd(packs, max(1, 4096 // TOK_DEV))

    def forward(hidden, weights):
        mixer_weights = weights[:10]
        gain_two, router_full, up_full, down_full = weights[10:]

        def group_step(carry, item):
            block_hidden, block_segment = item
            return (carry, jax.vmap(mixer, in_axes=(0, 0, None))(block_hidden, block_segment, mixer_weights))
        _, mixed = lax.scan(jax.checkpoint(group_step), jnp.zeros((), jnp.float32), (hidden.reshape(packs // group, group, TOK_DEV, D), segment.reshape(packs // group, group, TOK_DEV)))
        mixed = mixed.reshape(packs, TOK_DEV, D)
        residual = hidden + live[:, :, None].astype(jnp.float32) * mixed
        normed = residual * lax.rsqrt(lax.optimization_barrier(jnp.mean(residual * residual, axis=-1, keepdims=True)) + EPSILON) * gain_two
        routed = low(normed)
        logits = low_back(product(routed.reshape(-1, D), router_full)).reshape(packs, TOK_DEV, EXPERTS)
        probs = jax.nn.softmax(logits, axis=-1)
        gate = lax.optimization_barrier(jnp.sum(probs * route_hot.astype(jnp.float32), axis=-1))
        weight_row = gate * kept.astype(jnp.float32)
        sent = low_back(routed) * kept[:, :, None].astype(jnp.float32)
        buffer = jnp.zeros((rows_all + 1, D), jnp.float32).at[target.reshape(-1)].add(sent.reshape(-1, D))
        expert_rows = buffer[:rows_all].reshape(EXPERTS, packs * CAP, D)

        def expert_step(item):
            rows, up_one, down_one = item
            pre = low_back(product(rows, up_one))
            act = low(jax.nn.gelu(pre))
            return low(low_back(product(act, down_one)))
        results = lax.map(jax.checkpoint(expert_step), (expert_rows, up_full, down_full))
        flat = jnp.concatenate([results.reshape(rows_all, D), jnp.zeros((1, D), jnp.float32)], axis=0)
        back = flat[target.reshape(-1)].reshape(packs, TOK_DEV, D)
        return residual + weight_row[:, :, None] * back
    output, pullback = jax.vjp(forward, hidden, weights)
    hidden_grad, grads = pullback(upstream)
    return (output.reshape(MB, TOKENS, D).astype(jnp.bfloat16), hidden_grad.reshape(MB, TOKENS, D), grads[0], grads[1], grads[2], grads[3], grads[4], grads[5], grads[6], grads[7], grads[8], grads[9], grads[10], grads[11], grads[12], grads[13])
```

```python
import functools
import math

import jax
import jax.numpy as jnp
from jax import lax
from jax.experimental import pallas as pl
from jax.experimental.pallas import tpu as pltpu
from jax.sharding import PartitionSpec as P

EPSILON = 1e-05
LOG2E = 1.4426950408889634
LN2 = 0.6931471805599453
LANES = 128
ROWS = 8


def fold_rows(parts):
    place = lax.broadcasted_iota(jnp.int32, parts[0].shape, 0)
    half = 1
    while half < ROWS:
        lower = (place & half) == 0
        merged = []
        for i in range(0, len(parts), 2):
            a, b = parts[i], parts[i + 1]
            merged.append(jnp.where(lower, a, b) + pltpu.roll(jnp.where(lower, b, a), half, 0))
        parts = merged
        half *= 2
    return parts[0]


def sum_states(parts, how, pick):
    if how == "mxu":
        stack = jnp.concatenate([p.astype(jnp.bfloat16) for p in parts], axis=0)
        return jnp.dot(pick, stack, preferred_element_type=jnp.float32)
    n = parts[0].shape[0]
    halves = []
    for p in parts:
        total = p[:ROWS]
        for i in range(1, n // ROWS):
            total = total + p[i * ROWS:(i + 1) * ROWS]
        halves.append(total)
    return fold_rows(halves)


def fwd_kernel(len_ref, delta_ref, xs_ref, b_ref, c_ref, a_ref, y_ref, h_ref, last_ref, state, *, block, how, group):
    pack, step = pl.program_id(0), pl.program_id(1)
    states, width = a_ref.shape

    @pl.when(step == 0)
    def _():
        state[...] = jnp.zeros_like(state)

    live = step * block < len_ref[pack]

    @pl.when(live)
    def _():
        pick = (lax.broadcasted_iota(jnp.int32, (ROWS, ROWS * states), 1) // states
                == lax.broadcasted_iota(jnp.int32, (ROWS, ROWS * states), 0)).astype(jnp.bfloat16)

        def rows(s, _):
            r = pl.multiple_of(s * ROWS, ROWS)

            def chunk(g, _):
                for u in range(group):
                    lanes = pl.ds(pl.multiple_of((g * group + u) * LANES, LANES), LANES)
                    d = delta_ref[pl.ds(r, ROWS), lanes]
                    dx = d * xs_ref[pl.ds(r, ROWS), lanes]
                    a = a_ref[:, lanes]
                    h = state[:, lanes]
                    parts = []
                    for t in range(ROWS):
                        h_ref[r + t, :, lanes] = h
                        e = jnp.exp2(d[t:t + 1] * a)
                        h = e * h + b_ref[r + t] * dx[t:t + 1]
                        parts.append(c_ref[r + t] * h)
                    state[:, lanes] = h
                    y_ref[pl.ds(r, ROWS), lanes] = sum_states(parts, how, pick)
                return 0

            lax.fori_loop(0, width // (LANES * group), chunk, 0)
            return 0

        lax.fori_loop(0, block // ROWS, rows, 0)

    @pl.when(jnp.logical_not(live))
    def _():
        y_ref[...] = jnp.zeros_like(y_ref)

    last_ref[0] = state[...]


def scan_fwd(lens, delta, xs, bwide, cwide, a2, steps, block=32, how="vpu", group=2):
    rows, width = delta.shape
    states = a2.shape[0]
    packs = rows // steps
    blocks = steps // block
    at = lambda p, i, lens: (p * blocks + i, 0)
    at3 = lambda p, i, lens: (p * blocks + i, 0, 0)
    return pl.pallas_call(
        functools.partial(fwd_kernel, block=block, how=how, group=group),
        grid_spec=pltpu.PrefetchScalarGridSpec(
            num_scalar_prefetch=1,
            grid=(packs, blocks),
            in_specs=[
                pl.BlockSpec((block, width), at),
                pl.BlockSpec((block, width), at),
                pl.BlockSpec((block, states, LANES), at3),
                pl.BlockSpec((block, states, LANES), at3),
                pl.BlockSpec((states, width), lambda p, i, lens: (0, 0)),
            ],
            out_specs=[
                pl.BlockSpec((block, width), at),
                pl.BlockSpec((block, states, width), at3),
                pl.BlockSpec((1, states, width), lambda p, i, lens: (p, 0, 0)),
            ],
            scratch_shapes=[pltpu.VMEM((states, width), jnp.float32)],
        ),
        out_shape=[
            jax.ShapeDtypeStruct((rows, width), jnp.float32),
            jax.ShapeDtypeStruct((rows, states, width), jnp.float32),
            jax.ShapeDtypeStruct((packs, states, width), jnp.float32),
        ],
        compiler_params=pltpu.CompilerParams(vmem_limit_bytes=48 << 20),
        name="scan_forward",
    )(lens, delta, xs, bwide, cwide, a2)


def bwd_kernel(len_ref, delta_ref, xs_ref, gy_ref, b_ref, c_ref, a_ref, h_ref, last_ref,
               gd_ref, gx_ref, gb_ref, gc_ref, ga_ref, mu_s, hn_s, *, block, how, group, blocks):
    pack, back = pl.program_id(0), pl.program_id(1)
    step = blocks - 1 - back
    states, width = a_ref.shape

    @pl.when(back == 0)
    def _():
        mu_s[...] = jnp.zeros_like(mu_s)
        hn_s[...] = last_ref[0]

    @pl.when((back == 0) & (pack == 0))
    def _():
        ga_ref[...] = jnp.zeros_like(ga_ref)

    live = step * block < len_ref[pack]

    gb_ref[...] = jnp.zeros_like(gb_ref)
    gc_ref[...] = jnp.zeros_like(gc_ref)

    @pl.when(live)
    def _():
        pick = (lax.broadcasted_iota(jnp.int32, (ROWS, ROWS * states), 1) // states
                == lax.broadcasted_iota(jnp.int32, (ROWS, ROWS * states), 0)).astype(jnp.bfloat16)

        def rows(s, _):
            r = pl.multiple_of((block // ROWS - 1 - s) * ROWS, ROWS)

            def chunk(g, _):
                each = []
                for u in range(group):
                    lanes = pl.ds(pl.multiple_of((g * group + u) * LANES, LANES), LANES)
                    d = delta_ref[pl.ds(r, ROWS), lanes]
                    x = xs_ref[pl.ds(r, ROWS), lanes]
                    gy = gy_ref[pl.ds(r, ROWS), lanes]
                    each.append(dict(lanes=lanes, d=d, x=x, gy=gy, dx=d * x, a=a_ref[:, lanes], mu=mu_s[:, lanes],
                                     hn=hn_s[:, lanes], ga=ga_ref[:, lanes], sp=[None] * ROWS, gp=[None] * ROWS))
                for t in range(ROWS - 1, -1, -1):
                    b, c = b_ref[r + t], c_ref[r + t]
                    gb = gc = None
                    for v in each:
                        dt = v["d"][t:t + 1]
                        gyt = v["gy"][t:t + 1]
                        hp = h_ref[r + t, :, v["lanes"]]
                        e = jnp.exp2(dt * v["a"])
                        lam = c * gyt + v["mu"]
                        v["sp"][t] = b * lam
                        one_b = lam * v["dx"][t:t + 1]
                        one_c = v["hn"] * gyt
                        gb = one_b if gb is None else gb + one_b
                        gc = one_c if gc is None else gc + one_c
                        mu = e * lam
                        q = mu * hp
                        v["gp"][t] = q * v["a"]
                        v["ga"] = v["ga"] + q * dt
                        v["mu"], v["hn"] = mu, hp
                    gb_ref[r + t] += gb
                    gc_ref[r + t] += gc
                for v in each:
                    lanes = v["lanes"]
                    mu_s[:, lanes], hn_s[:, lanes], ga_ref[:, lanes] = v["mu"], v["hn"], v["ga"]
                    total = sum_states(v["sp"], how, pick)
                    decay = sum_states(v["gp"], how, pick)
                    gd_ref[pl.ds(r, ROWS), lanes] = decay * LN2 + v["x"] * total
                    gx_ref[pl.ds(r, ROWS), lanes] = v["d"] * total
                return 0

            lax.fori_loop(0, width // (LANES * group), chunk, 0)
            return 0

        lax.fori_loop(0, block // ROWS, rows, 0)

    @pl.when(jnp.logical_not(live))
    def _():
        gd_ref[...] = jnp.zeros_like(gd_ref)
        gx_ref[...] = jnp.zeros_like(gx_ref)


def scan_bwd(lens, delta, xs, gy, bwide, cwide, a2, hall, last, steps, block=32, how="vpu", group=2):
    rows, width = delta.shape
    states = a2.shape[0]
    packs = rows // steps
    blocks = steps // block
    at = lambda p, i, lens: (p * blocks + blocks - 1 - i, 0)
    at3 = lambda p, i, lens: (p * blocks + blocks - 1 - i, 0, 0)
    f32 = jnp.float32
    return pl.pallas_call(
        functools.partial(bwd_kernel, block=block, how=how, group=group, blocks=blocks),
        grid_spec=pltpu.PrefetchScalarGridSpec(
            num_scalar_prefetch=1,
            grid=(packs, blocks),
            in_specs=[
                pl.BlockSpec((block, width), at),
                pl.BlockSpec((block, width), at),
                pl.BlockSpec((block, width), at),
                pl.BlockSpec((block, states, LANES), at3),
                pl.BlockSpec((block, states, LANES), at3),
                pl.BlockSpec((states, width), lambda p, i, lens: (0, 0)),
                pl.BlockSpec((block, states, width), at3),
                pl.BlockSpec((1, states, width), lambda p, i, lens: (p, 0, 0)),
            ],
            out_specs=[
                pl.BlockSpec((block, width), at),
                pl.BlockSpec((block, width), at),
                pl.BlockSpec((block, states, LANES), at3),
                pl.BlockSpec((block, states, LANES), at3),
                pl.BlockSpec((states, width), lambda p, i, lens: (0, 0)),
            ],
            scratch_shapes=[pltpu.VMEM((states, width), f32), pltpu.VMEM((states, width), f32)],
        ),
        out_shape=[
            jax.ShapeDtypeStruct((rows, width), f32),
            jax.ShapeDtypeStruct((rows, width), f32),
            jax.ShapeDtypeStruct((rows, states, LANES), f32),
            jax.ShapeDtypeStruct((rows, states, LANES), f32),
            jax.ShapeDtypeStruct((states, width), f32),
        ],
        compiler_params=pltpu.CompilerParams(vmem_limit_bytes=48 << 20),
        name="scan_backward",
    )(lens, delta, xs, gy, bwide, cwide, a2, hall, last)


F32 = jnp.float32
BF16 = jnp.bfloat16


def dot(left, right, dims=((1,), (0,))):
    return lax.dot_general(left, right, (dims, ((), ())), preferred_element_type=F32)


def swap(values, axis, mask):
    count = lax.axis_size(axis)
    return lax.ppermute(values, axis, [(i, i ^ mask) for i in range(count)])


def grow(values, axis, mask, dim):
    got = swap(values, axis, mask)
    upper = (lax.axis_index(axis) & mask) != 0
    return jnp.concatenate([jnp.where(upper, got, values), jnp.where(upper, values, got)], axis=dim)


def gather_rows(values):
    rows, width = values.shape
    bits = lax.axis_size("fsdp").bit_length() - 1
    whole = values.reshape((1,) * bits + (rows, width))
    place = lambda bit: bits - 1 - bit
    for bit in range(2, bits):
        whole = grow(whole, "fsdp", 1 << bit, place(bit))
    first, second = whole[..., : width // 2], whole[..., width // 2 :]
    first = grow(first, "fsdp", 2, place(1))
    second = grow(second, "fsdp", 1, place(0))
    first = grow(first, "fsdp", 1, place(0))
    second = grow(second, "fsdp", 2, place(1))
    whole = jnp.concatenate([first, second], axis=-1).reshape(-1, width)
    mask = 1
    while mask < lax.axis_size("dp"):
        whole = grow(whole, "dp", mask, 0) if mask == 1 else grow(whole.reshape(1, -1, width), "dp", mask, 0).reshape(-1, width)
        mask *= 2
    return whole


def own_block(values, index, count, axis):
    size = values.shape[axis] // count
    return lax.dynamic_slice_in_dim(values, index * size, size, axis)


def scatter_rows(piece):
    me, groups, count = lax.axis_index("dp"), lax.axis_size("dp"), lax.axis_size("fsdp")
    sent = [swap(piece(me ^ k).astype(BF16), "dp", k) for k in range(1, groups)]
    total = piece(me)
    for got in sent:
        total = total + got.astype(F32)
    rows, width = total.shape
    parts = total.astype(BF16).reshape(count, rows // count, width)
    return jnp.sum(lax.all_to_all(parts, "fsdp", 0, 0, tiled=True).astype(F32), axis=0)


def scatter_product(left, right):
    groups = lax.axis_size("dp")
    return scatter_rows(lambda i: dot(own_block(left, i, groups, 1), right, ((0,), (0,))))


def scatter_array(values):
    groups = lax.axis_size("dp")
    return scatter_rows(lambda i: own_block(values, i, groups, 0))


def norm_backward(grad_normed, gain, normed, inv_scale):
    scaled = grad_normed * gain
    grad_in = inv_scale * (scaled - normed * jnp.mean(scaled * normed, axis=-1, keepdims=True))
    return (grad_in, jnp.sum(grad_normed * normed, axis=0))


def shifted(values, by):
    if by == 0:
        return values
    zeros = jnp.zeros(values.shape[:1] + (abs(by),) + values.shape[2:], values.dtype)
    if by > 0:
        return jnp.concatenate([zeros, values[:, :-by]], axis=1)
    return jnp.concatenate([values[:, -by:], zeros], axis=1)


def body(
    tokens,
    cotangent,
    routes,
    lengths,
    norm1_gain,
    input_weight,
    conv_weight,
    conv_bias,
    scan_weight,
    step_weight,
    step_bias,
    decay_log,
    skip_gain,
    out_weight,
    norm2_gain,
    router_weight,
    expert_up,
    expert_down,
):
    micro, steps, model = tokens.shape
    rows = micro * steps
    experts = lax.axis_size("fsdp")
    groups = lax.axis_size("dp")
    devices = experts * groups
    capacity = (5 * steps + 4 * experts - 1) // (4 * experts)
    slots = micro * capacity
    inner = input_weight.shape[1] // 2
    states = decay_log.shape[1]
    rank = step_weight.shape[1]
    taps = conv_weight.shape[1]
    own_model, own_inner = norm1_gain.shape[0], conv_bias.shape[0]

    column = lambda v: v[:, None]
    half = experts // 2
    vectors = jnp.concatenate(
        [
            conv_weight,
            column(conv_bias),
            column(step_bias),
            column(skip_gain),
            decay_log,
            column(jnp.concatenate([norm1_gain, norm2_gain])),
            jnp.concatenate([router_weight[:, :half], router_weight[:, half:]], axis=0),
        ],
        axis=1,
    )
    used = vectors.shape[1]
    matrices = jnp.concatenate([scan_weight, step_weight], axis=1)
    small = jnp.concatenate(
        [matrices, vectors, jnp.zeros((own_inner, matrices.shape[1] - used), BF16)], axis=1
    )
    input_x = gather_rows(input_weight[:, :inner])
    small_full = gather_rows(small)
    input_z = lax.all_gather(input_weight[:, inner:], ("dp", "fsdp"), axis=0, tiled=True)
    output_full = lax.all_gather(out_weight, ("dp", "fsdp"), axis=0, tiled=True)
    ups = [expert_up[0]] + [swap(expert_up[0], "dp", k) for k in range(1, groups)]
    downs = [expert_down[0]] + [swap(expert_down[0], "dp", k) for k in range(1, groups)]

    place = jnp.arange(steps, dtype=jnp.int32)
    sample = lengths[:, 0, 0]
    live = (place[None, :] < sample[:, None]).astype(jnp.int32)
    route = routes[:, :, 0]
    expert_ids = jnp.arange(experts, dtype=jnp.int32)
    route_hot = (route[:, :, None] == expert_ids).astype(BF16)
    live_hot = route_hot * live[:, :, None].astype(BF16)
    earlier = (place[:, None] > place[None, :]).astype(BF16)
    before = lax.dot_general(
        jnp.broadcast_to(earlier, (micro, steps, steps)), live_hot, (((2,), (1,)), ((0,), (0,))),
        preferred_element_type=F32,
    )
    slot = jnp.sum(before * live_hot.astype(F32), axis=2).astype(jnp.int32)
    kept = (live * (slot < capacity).astype(jnp.int32)).reshape(rows)
    live = live.reshape(rows).astype(F32)
    target = (route * slots + jnp.arange(micro, dtype=jnp.int32)[:, None] * capacity + slot).reshape(rows)
    chooser = (
        (jnp.arange(experts * slots, dtype=jnp.int32)[:, None] == target[None, :]) & (kept[None, :] == 1)
    ).astype(BF16)
    kept = kept.astype(F32)
    route_float = route_hot.reshape(rows, experts).astype(F32)

    def to_experts(values):
        sent = dot(chooser, values).astype(BF16).reshape(experts, slots, -1)
        return lax.all_to_all(sent, "fsdp", 0, 0, tiled=True).reshape(experts * slots, -1)

    def from_experts(values):
        back = lax.all_to_all(values.reshape(experts, slots, -1), "fsdp", 0, 0, tiled=True)
        return dot(chooser, back.reshape(experts * slots, -1), ((0,), (0,)))

    cotangent = cotangent.reshape(rows, model)
    upstream_sent = to_experts(cotangent)
    upstream = cotangent.astype(F32)

    hidden = tokens.reshape(rows, model).astype(F32)
    matrices_full = small_full[:, : rank + 2 * states + rank]
    select_full = small_full[:, : rank + 2 * states]
    step_full = small_full[:, rank + 2 * states : 2 * rank + 2 * states]
    vectors_full = small_full[:, 2 * rank + 2 * states :].T
    kernel_full = vectors_full[:taps].astype(F32)
    bias_conv, bias_step, skip_one = [vectors_full[taps + i].astype(F32) for i in range(3)]
    decay_full = vectors_full[taps + 3 : taps + 3 + states].astype(F32)
    gains = vectors_full[taps + 3 + states].reshape(devices, 2, own_model)
    gain_one = gains[:, 0].reshape(model).astype(F32)
    gain_two = gains[:, 1].reshape(model).astype(F32)
    router_full = vectors_full[taps + 4 + states : taps + 4 + states + half].reshape(half, devices, 2, own_model)
    router_full = router_full.transpose(2, 0, 1, 3).reshape(experts, model)

    inv_first = lax.rsqrt(jnp.mean(hidden * hidden, axis=-1, keepdims=True) + EPSILON)
    normed_first = hidden * inv_first
    normed_low = (normed_first * gain_one).astype(BF16)
    branch_x = dot(normed_low, input_x)
    branch_x3 = branch_x.reshape(micro, steps, inner)
    conv_out = bias_conv
    for shift in range(taps):
        conv_out = conv_out + kernel_full[taps - 1 - shift] * shifted(branch_x3, shift)
    conv_out = conv_out.reshape(rows, inner)
    conv_sig = jax.nn.sigmoid(conv_out)
    scan_in = conv_out * conv_sig
    scan_low = scan_in.astype(BF16)
    selected = dot(scan_low, select_full)
    rank_low = selected[:, :rank].astype(BF16)
    bmat = selected[:, rank : rank + states]
    cmat = selected[:, rank + states :]
    step_pre = dot(rank_low, step_full, ((1,), (1,))) + bias_step
    step_size = jax.nn.softplus(step_pre)
    decay_mat = -jnp.exp(decay_full)
    decay_two = decay_mat * LOG2E
    bwide = jnp.broadcast_to(bmat[:, :, None], (rows, states, LANES))
    cwide = jnp.broadcast_to(cmat[:, :, None], (rows, states, LANES))
    scanned, state_all, state_last = scan_fwd(sample, step_size, scan_in, bwide, cwide, decay_two, steps, group=4)
    branch_z = dot(normed_low, input_z)
    mixer_out = scanned + skip_one * scan_in
    sigmoid_z = jax.nn.sigmoid(branch_z)
    silu_z = branch_z * sigmoid_z
    gated_low = (mixer_out * silu_z).astype(BF16)
    mixed = dot(gated_low, output_full)

    residual = hidden + live[:, None] * mixed
    inv_second = lax.rsqrt(jnp.mean(residual * residual, axis=-1, keepdims=True) + EPSILON)
    normed_second = residual * inv_second
    routed = (normed_second * gain_two).astype(BF16)
    probs = jax.nn.softmax(dot(routed, router_full, ((1,), (1,))), axis=-1)
    gate = jnp.sum(probs * route_float, axis=1)
    weight_row = gate * kept
    weight_high = weight_row.astype(BF16)
    weight_low = (weight_row - weight_high.astype(F32)).astype(BF16)
    received = to_experts(
        jnp.concatenate(
            [routed, weight_high[:, None], weight_low[:, None], jnp.zeros((rows, LANES - 2), BF16)], axis=1
        )
    )

    flat_in = received[:, :model]
    flat_weight = received[:, model].astype(F32) + received[:, model + 1].astype(F32)
    flat_grad = (flat_weight[:, None] * upstream_sent.astype(F32)).astype(BF16)
    pres = [dot(flat_in, up) for up in ups]
    acts = [jax.nn.gelu(pre).astype(BF16) for pre in pres]
    result = sum(dot(act, down) for act, down in zip(acts, downs))
    back = from_experts(result.astype(BF16))
    grad_pres = []
    for pre, down in zip(pres, downs):
        grad_act = dot(flat_grad, down, ((1,), (1,)))
        grad_pres.append(jax.vjp(jax.nn.gelu, pre)[1](grad_act)[0].astype(BF16))
    grad_rows = sum(dot(grad_pre, up, ((1,), (1,))) for grad_pre, up in zip(grad_pres, ups))
    grad_back = from_experts(grad_rows.astype(BF16))
    up_grad = dot(flat_in, grad_pres[0], ((0,), (0,)))
    down_grad = dot(acts[0], flat_grad, ((0,), (0,)))
    for k in range(1, groups):
        up_grad = up_grad + swap(dot(flat_in, grad_pres[k], ((0,), (0,))).astype(BF16), "dp", k).astype(F32)
        down_grad = down_grad + swap(dot(acts[k], flat_grad, ((0,), (0,))).astype(BF16), "dp", k).astype(F32)

    block_output = (residual + weight_row[:, None] * back).astype(BF16)
    grad_gate = kept * jnp.sum(upstream * back, axis=1)
    grad_logits = ((grad_gate * gate)[:, None] * (route_float - probs)).astype(BF16)
    router_grad = dot(routed, grad_logits, ((0,), (0,)))
    grad_routed = dot(grad_logits, router_full) + grad_back
    grad_norm_two, gain_two_grad = norm_backward(grad_routed, gain_two, normed_second, inv_second)
    grad_residual = upstream + grad_norm_two
    grad_mixed = (live[:, None] * grad_residual).astype(BF16)
    output_grad = scatter_product(gated_low, grad_mixed)

    grad_gated = dot(grad_mixed, output_full, ((1,), (1,)))
    grad_mixer = grad_gated * silu_z
    grad_z = (grad_gated * mixer_out * sigmoid_z * (1.0 + branch_z * (1.0 - sigmoid_z))).astype(BF16)
    input_z_grad = scatter_product(normed_low, grad_z)
    grad_step, grad_scan_in, grad_bwide, grad_cwide, grad_decay = scan_bwd(
        sample, step_size, scan_in, grad_mixer, bwide, cwide, decay_two, state_all, state_last, steps, group=4
    )
    skip_grad = jnp.sum(grad_mixer * scan_in, axis=0)
    decay_grad = grad_decay * decay_mat
    grad_step_pre = grad_step * jax.nn.sigmoid(step_pre)
    step_bias_grad = jnp.sum(grad_step_pre, axis=0)
    grad_step_low = grad_step_pre.astype(BF16)
    step_grad = dot(grad_step_low, rank_low, ((0,), (0,)))
    grad_rank = dot(grad_step_low, step_full)
    grad_selected = jnp.concatenate(
        [grad_rank, jnp.sum(grad_bwide, axis=-1), jnp.sum(grad_cwide, axis=-1)], axis=1
    ).astype(BF16)
    select_grad = dot(scan_low, grad_selected, ((0,), (0,)))
    grad_values = dot(grad_selected, select_full, ((1,), (1,)))
    grad_xs = grad_values + grad_scan_in + grad_mixer * skip_one
    grad_conv = grad_xs * (conv_sig * (1.0 + conv_out * (1.0 - conv_sig)))
    conv_bias_grad = jnp.sum(grad_conv, axis=0)
    grad_conv3 = grad_conv.reshape(micro, steps, inner)
    kernel_grad = []
    grad_x = 0.0
    for j in range(taps):
        shift = taps - 1 - j
        kernel_grad.append(jnp.sum(grad_conv3 * shifted(branch_x3, shift), axis=(0, 1)))
        grad_x = grad_x + kernel_full[j] * shifted(grad_conv3, -shift)
    grad_x = grad_x.reshape(rows, inner).astype(BF16)
    input_x_grad = scatter_product(normed_low, grad_x)
    grad_normed = dot(grad_x, input_x, ((1,), (1,))) + dot(grad_z, input_z, ((1,), (1,)))
    grad_norm_one, gain_one_grad = norm_backward(grad_normed, gain_one, normed_first, inv_first)
    tokens_grad = grad_residual + grad_norm_one

    gain_grads = jnp.concatenate(
        [gain_one_grad.reshape(devices, 1, own_model), gain_two_grad.reshape(devices, 1, own_model)], axis=1
    ).reshape(1, inner)
    router_grads = router_grad.reshape(devices, own_model, 2, half).transpose(0, 2, 1, 3).reshape(inner, half)
    vector_grads = jnp.concatenate(
        [jnp.stack(kernel_grad + [conv_bias_grad, step_bias_grad, skip_grad]), decay_grad, gain_grads], axis=0
    ).T
    small_grads = scatter_array(
        jnp.concatenate(
            [
                select_grad,
                step_grad,
                vector_grads,
                router_grads,
                jnp.zeros((inner, matrices.shape[1] - used), F32),
            ],
            axis=1,
        )
    )
    at = 2 * rank + 2 * states
    vector_grads = small_grads[:, at:]
    at_gain = taps + 3 + states
    routers = vector_grads[:, at_gain + 1 : at_gain + 1 + half]
    return (
        block_output.reshape(micro, steps, model),
        tokens_grad.reshape(micro, steps, model),
        vector_grads[:own_model, at_gain],
        jnp.concatenate([input_x_grad, input_z_grad], axis=1),
        vector_grads[:, :taps],
        vector_grads[:, taps],
        small_grads[:, : rank + 2 * states],
        small_grads[:, rank + 2 * states : at],
        vector_grads[:, taps + 1],
        vector_grads[:, taps + 3 : at_gain],
        vector_grads[:, taps + 2],
        output_grad,
        vector_grads[own_model:, at_gain],
        jnp.concatenate([routers[:own_model], routers[own_model:]], axis=1),
        up_grad[None],
        down_grad[None],
    )


def solution(mesh):
    rows3 = P(None, ("dp", "fsdp"), None)
    vector = P(("dp", "fsdp"))
    matrix = P(("dp", "fsdp"), None)
    weights = (
        vector, matrix, matrix, vector, matrix, matrix, vector, matrix, vector, matrix, vector, matrix,
        P("fsdp", None, "dp"), P("fsdp", "dp", None),
    )
    return jax.shard_map(
        body,
        mesh=mesh,
        in_specs=(rows3, rows3, rows3, rows3) + weights,
        out_specs=(rows3, rows3) + weights,
        check_vma=False,
    )
```

```python
import functools

import jax
import jax.numpy as jnp
from jax import lax
from jax.experimental import pallas as pl
from jax.experimental.pallas import tpu as pltpu
from jax.sharding import PartitionSpec as P

EPSILON = 1e-05
LOG2E = 1.4426950408889634
LN2 = 0.6931471805599453
LANES = 128
ROWS = 8
F32 = jnp.float32
BF16 = jnp.bfloat16


def dot(left, right, dims=((1,), (0,))):
    return lax.dot_general(left, right, (dims, ((), ())), preferred_element_type=F32)


def fold_rows(parts):
    place = lax.broadcasted_iota(jnp.int32, parts[0].shape, 0)
    half = 1
    while half < ROWS:
        lower = (place & half) == 0
        merged = []
        for i in range(0, len(parts), 2):
            a, b = parts[i], parts[i + 1]
            merged.append(jnp.where(lower, a, b) + pltpu.roll(jnp.where(lower, b, a), half, 0))
        parts = merged
        half *= 2
    return parts[0]


def sum_states(parts):
    halves = []
    for p in parts:
        total = p[:ROWS]
        for i in range(1, p.shape[0] // ROWS):
            total = total + p[i * ROWS : (i + 1) * ROWS]
        halves.append(total)
    return fold_rows(halves)


def lane_chunk(k, count=1):
    return pl.ds(pl.multiple_of(k * LANES * count, LANES), LANES * count)


def split_low(values):
    high = values.astype(BF16)
    return high, (values - high.astype(F32)).astype(BF16)


def widen(selected, first, states, wide_ref):
    steps = selected.shape[0]
    ones = jnp.ones((LANES, LANES), BF16)
    lane = lax.broadcasted_iota(jnp.int32, (states, LANES), 1)
    row = lax.broadcasted_iota(jnp.int32, (states, LANES), 0)
    own = (lane == row + first)[None]
    size = 64
    for at in range(0, steps, size):
        spread = jnp.where(own, selected[at : at + size][:, None, :], 0.0).reshape(size * states, LANES)
        high, low = split_low(spread)
        wide_ref[at * states : (at + size) * states, :] = dot(high, ones) + dot(low, ones)


def narrow(wide_ref, first, states, steps):
    ones = jnp.ones((LANES, LANES), BF16)
    lane = lax.broadcasted_iota(jnp.int32, (states, LANES), 1)
    row = lax.broadcasted_iota(jnp.int32, (states, LANES), 0)
    own = (lane == row + first)[None]
    size = 64
    out = []
    for at in range(0, steps, size):
        high, low = split_low(wide_ref[at * states : (at + size) * states, :])
        sums = (dot(high, ones) + dot(low, ones)).reshape(size, states, LANES)
        out.append(jnp.sum(jnp.where(own, sums, 0.0), axis=1))
    return jnp.concatenate(out, axis=0)


def shift_rows(values, by):
    if by == 0:
        return values
    rows = values.shape[0]
    place = lax.broadcasted_iota(jnp.int32, values.shape, 0)
    inside = place >= by if by > 0 else place < rows + by
    return jnp.where(inside, pltpu.roll(values, by % rows, 0), 0.0)


def conv_of(x, taps_ref, bias, lanes, taps):
    total = bias
    for shift in range(taps):
        total = total + taps_ref[taps - 1 - shift : taps - shift, lanes] * shift_rows(x, shift)
    return total


def forward_kernel(len_ref, u_ref, wx_ref, sela_ref, stepb_ref, vec_ref, a_ref,
                   bx_ref, xs_ref, delta_ref, sel_ref, mix_ref, h_ref, last_ref,
                   state, bw, cw, low, *, block, group, rank, taps):
    pack, step = pl.program_id(0), pl.program_id(1)
    states, width = a_ref.shape
    steps = u_ref.shape[0]
    chunks = width // LANES
    bias_conv, bias_step, skip = taps, taps + 1, taps + 2

    @pl.when(step == 0)
    def _():
        state[...] = jnp.zeros_like(state)

        def project(k, _):
            lanes = lane_chunk(k, 2)
            bx_ref[:, lanes] = dot(u_ref[...], wx_ref[:, lanes])
            return 0

        lax.fori_loop(0, chunks // 2, project, 0)

        def convolve(k, _):
            lanes = lane_chunk(k)
            conv = conv_of(bx_ref[:, lanes], vec_ref, vec_ref[bias_conv : bias_conv + 1, lanes], lanes, taps)
            xs = conv * jax.nn.sigmoid(conv)
            xs_ref[:, lanes] = xs
            low[:, lanes] = xs.astype(BF16)
            return 0

        lax.fori_loop(0, chunks, convolve, 0)
        selected = dot(low[...], sela_ref[...])
        sel_ref[...] = selected
        lane = lax.broadcasted_iota(jnp.int32, selected.shape, 1)
        rank_low = jnp.where(lane < rank, selected, 0.0).astype(BF16)
        widen(selected, rank, states, bw)
        widen(selected, rank + states, states, cw)

        def sizes(k, _):
            lanes = lane_chunk(k, 2)
            pre = dot(rank_low, stepb_ref[lanes, :], ((1,), (1,))) + vec_ref[bias_step : bias_step + 1, lanes]
            delta_ref[:, lanes] = jnp.maximum(pre, 0.0) + jnp.log1p(jnp.exp(-jnp.abs(pre)))
            return 0

        lax.fori_loop(0, chunks // 2, sizes, 0)

    live = step * block < len_ref[pack]

    @pl.when(live)
    def _():
        def rows(s, _):
            r = pl.multiple_of(s * ROWS, ROWS)
            at = pl.multiple_of(step * block + r, ROWS)

            def chunk(g, _):
                for u in range(group):
                    lanes = lane_chunk(g * group + u)
                    d = delta_ref[pl.ds(at, ROWS), lanes]
                    x = xs_ref[pl.ds(at, ROWS), lanes]
                    dx = d * x
                    a = a_ref[:, lanes]
                    h = state[:, lanes]
                    parts = []
                    for t in range(ROWS):
                        here = pl.ds(pl.multiple_of((at + t) * states, states), states)
                        h_ref[r + t, :, lanes] = h
                        h = jnp.exp2(d[t : t + 1] * a) * h + bw[here, :] * dx[t : t + 1]
                        parts.append(cw[here, :] * h)
                    state[:, lanes] = h
                    mix_ref[pl.ds(r, ROWS), lanes] = sum_states(parts) + vec_ref[skip : skip + 1, lanes] * x
                return 0

            lax.fori_loop(0, chunks // group, chunk, 0)
            return 0

        lax.fori_loop(0, block // ROWS, rows, 0)

    @pl.when(jnp.logical_not(live))
    def _():
        mix_ref[...] = jnp.zeros_like(mix_ref)

    last_ref[0] = state[...]


def mixer_forward(sample, u, wx, sela, stepb, vec, a2, packs, rank, taps, block=32, group=4):
    rows, model = u.shape
    steps = rows // packs
    states, width = a2.shape
    blocks = steps // block
    per_pack = lambda p, i, lens: (p, 0)
    fixed = lambda p, i, lens: (0, 0)
    at = lambda p, i, lens: (p * blocks + i, 0)
    whole = lambda v: pl.BlockSpec(v.shape, fixed)
    return pl.pallas_call(
        functools.partial(forward_kernel, block=block, group=group, rank=rank, taps=taps),
        grid_spec=pltpu.PrefetchScalarGridSpec(
            num_scalar_prefetch=1,
            grid=(packs, blocks),
            in_specs=[pl.BlockSpec((steps, model), per_pack), whole(wx), whole(sela), whole(stepb), whole(vec), whole(a2)],
            out_specs=[
                pl.BlockSpec((steps, width), per_pack),
                pl.BlockSpec((steps, width), per_pack),
                pl.BlockSpec((steps, width), per_pack),
                pl.BlockSpec((steps, LANES), per_pack),
                pl.BlockSpec((block, width), at),
                pl.BlockSpec((block, states, width), lambda p, i, lens: (p * blocks + i, 0, 0)),
                pl.BlockSpec((1, states, width), lambda p, i, lens: (p, 0, 0)),
            ],
            scratch_shapes=[
                pltpu.VMEM((states, width), F32),
                pltpu.VMEM((steps * states, LANES), F32),
                pltpu.VMEM((steps * states, LANES), F32),
                pltpu.VMEM((steps, width), BF16),
            ],
        ),
        out_shape=[
            jax.ShapeDtypeStruct((rows, width), F32),
            jax.ShapeDtypeStruct((rows, width), F32),
            jax.ShapeDtypeStruct((rows, width), F32),
            jax.ShapeDtypeStruct((rows, LANES), F32),
            jax.ShapeDtypeStruct((rows, width), F32),
            jax.ShapeDtypeStruct((rows, states, width), F32),
            jax.ShapeDtypeStruct((packs, states, width), F32),
        ],
        compiler_params=pltpu.CompilerParams(vmem_limit_bytes=56 << 20),
        cost_estimate=pl.CostEstimate(flops=0, bytes_accessed=120_000_000, transcendentals=0),
        name="mixer_forward",
    )(sample, u, wx, sela, stepb, vec, a2)


def backward_kernel(len_ref, delta_ref, xs_ref, bx_ref, gm_ref, sel_ref, sela_ref, stepb_ref, vec_ref, a_ref, h_ref, last_ref,
                    wx_ref, x_ref, gain_ref, gu_ref, gh_ref,
                    gx_ref, gsel_ref, gstep_ref, ggain_ref, gtok_ref,
                    mu_s, hn_s, bw, cw, gb, gc, gd, gxs, low, gvec_ref, ga_ref, *, block, group, blocks, rank, taps):
    pack, back = pl.program_id(0), pl.program_id(1)
    step = blocks - 1 - back
    states, width = a_ref.shape
    steps = sel_ref.shape[0]
    chunks = width // LANES
    bias_conv, bias_step, skip = taps, taps + 1, taps + 2

    @pl.when((back == 0) & (pack == 0))
    def _():
        ga_ref[...] = jnp.zeros_like(ga_ref)
        gsel_ref[...] = jnp.zeros_like(gsel_ref)
        gstep_ref[...] = jnp.zeros_like(gstep_ref)
        gvec_ref[...] = jnp.zeros_like(gvec_ref)
        ggain_ref[...] = jnp.zeros_like(ggain_ref)

    @pl.when(back == 0)
    def _():
        mu_s[...] = jnp.zeros_like(mu_s)
        hn_s[...] = last_ref[0]
        gb[...] = jnp.zeros_like(gb)
        gc[...] = jnp.zeros_like(gc)
        selected = sel_ref[...]
        widen(selected, rank, states, bw)
        widen(selected, rank + states, states, cw)

    live = step * block < len_ref[pack]

    @pl.when(live)
    def _():
        def rows(s, _):
            r = pl.multiple_of((block // ROWS - 1 - s) * ROWS, ROWS)
            at = pl.multiple_of(step * block + r, ROWS)

            def chunk(g, _):
                each = []
                for u in range(group):
                    lanes = lane_chunk(g * group + u)
                    d = delta_ref[pl.ds(at, ROWS), lanes]
                    x = xs_ref[pl.ds(at, ROWS), lanes]
                    gy = gm_ref[pl.ds(at, ROWS), lanes]
                    each.append(dict(lanes=lanes, d=d, x=x, gy=gy, dx=d * x, a=a_ref[:, lanes], mu=mu_s[:, lanes],
                                     hn=hn_s[:, lanes], ga=ga_ref[:, lanes], sp=[None] * ROWS, gp=[None] * ROWS))
                for t in range(ROWS - 1, -1, -1):
                    here = pl.ds(pl.multiple_of((at + t) * states, states), states)
                    b, c = bw[here, :], cw[here, :]
                    one_b = one_c = None
                    for v in each:
                        dt = v["d"][t : t + 1]
                        gyt = v["gy"][t : t + 1]
                        hp = h_ref[r + t, :, v["lanes"]]
                        lam = c * gyt + v["mu"]
                        v["sp"][t] = b * lam
                        to_b = lam * v["dx"][t : t + 1]
                        to_c = v["hn"] * gyt
                        one_b = to_b if one_b is None else one_b + to_b
                        one_c = to_c if one_c is None else one_c + to_c
                        mu = jnp.exp2(dt * v["a"]) * lam
                        q = mu * hp
                        v["gp"][t] = q * v["a"]
                        v["ga"] = v["ga"] + q * dt
                        v["mu"], v["hn"] = mu, hp
                    gb[here, :] += one_b
                    gc[here, :] += one_c
                for v in each:
                    lanes = v["lanes"]
                    mu_s[:, lanes], hn_s[:, lanes], ga_ref[:, lanes] = v["mu"], v["hn"], v["ga"]
                    total = sum_states(v["sp"])
                    decay = sum_states(v["gp"])
                    gd[pl.ds(at, ROWS), lanes] = decay * LN2 + v["x"] * total
                    gxs[pl.ds(at, ROWS), lanes] = v["d"] * total
                return 0

            lax.fori_loop(0, chunks // group, chunk, 0)
            return 0

        lax.fori_loop(0, block // ROWS, rows, 0)

    @pl.when(jnp.logical_not(live))
    def _():
        here = pl.ds(pl.multiple_of(step * block, block), block)
        gd[here, :] = jnp.zeros((block, width), F32)
        gxs[here, :] = jnp.zeros((block, width), F32)

    @pl.when(back == blocks - 1)
    def _():
        def add_row(row, lanes, values):
            gvec_ref[row : row + 1, lanes] += jnp.sum(values, axis=0, keepdims=True)

        def sizes(k, _):
            lanes = lane_chunk(k)
            d = delta_ref[:, lanes]
            rise = jnp.where(d < 0.01, d * (1.0 - d * (0.5 - d * (1.0 / 6.0))), 1.0 - jnp.exp(-d))
            grad = gd[:, lanes] * rise
            add_row(bias_step, lanes, grad)
            low[:, lanes] = grad.astype(BF16)
            add_row(skip, lanes, gm_ref[:, lanes] * xs_ref[:, lanes])
            return 0

        lax.fori_loop(0, chunks, sizes, 0)
        selected = sel_ref[...]
        lane = lax.broadcasted_iota(jnp.int32, selected.shape, 1)
        rank_low = jnp.where(lane < rank, selected, 0.0).astype(BF16)
        grad_rank = dot(low[...], stepb_ref[...])
        gstep_ref[...] += dot(low[...], rank_low, ((0,), (0,)))
        grad_sel = narrow(gb, rank, states, steps) + narrow(gc, rank + states, states, steps)
        grad_sel = jnp.where(lane < rank, grad_rank, grad_sel).astype(BF16)

        def values(k, _):
            lanes = lane_chunk(k)
            gm = gm_ref[:, lanes]
            x = bx_ref[:, lanes]
            conv = conv_of(x, vec_ref, vec_ref[bias_conv : bias_conv + 1, lanes], lanes, taps)
            sig = jax.nn.sigmoid(conv)
            low[:, lanes] = (conv * sig).astype(BF16)
            grad = dot(grad_sel, sela_ref[lanes, :], ((1,), (1,)))
            grad = grad + gxs[:, lanes] + gm * vec_ref[skip : skip + 1, lanes]
            grad = grad * (sig * (1.0 + conv * (1.0 - sig)))
            add_row(bias_conv, lanes, grad)
            back_x = None
            for j in range(taps):
                shift = taps - 1 - j
                add_row(j, lanes, grad * shift_rows(x, shift))
                term = vec_ref[j : j + 1, lanes] * shift_rows(grad, -shift)
                back_x = term if back_x is None else back_x + term
            gx_ref[:, lanes] = back_x.astype(BF16)
            return 0

        lax.fori_loop(0, chunks, values, 0)
        gsel_ref[...] += dot(low[...], grad_sel, ((0,), (0,)))

        hidden = x_ref[...].astype(F32)
        inv = lax.rsqrt(jnp.mean(hidden * hidden, axis=1, keepdims=True) + EPSILON)
        normed = hidden * inv
        grad_u = dot(gx_ref[...], wx_ref[...], ((1,), (1,))) + gu_ref[...]
        scaled = grad_u * gain_ref[...]
        ggain_ref[...] += jnp.sum(grad_u * normed, axis=0, keepdims=True)
        gtok_ref[...] = gh_ref[...] + inv * (scaled - normed * jnp.mean(scaled * normed, axis=1, keepdims=True))

    @pl.when((back == blocks - 1) & (pack == pl.num_programs(0) - 1))
    def _():
        used = jnp.concatenate([gvec_ref[...], ga_ref[...] * a_ref[...] * LN2], axis=0)
        before = jnp.zeros((rank, width), F32)
        after = jnp.zeros((LANES - rank - used.shape[0], width), F32)
        gstep_ref[...] += jnp.concatenate([before, used, after], axis=0).T


def mixer_backward(sample, delta, xs, bx, gm, sel, sela, stepb, vec, a2, hall, last, wx, tokens, gain, grad_u, grad_h,
                   packs, rank, taps, block=32, group=4):
    rows, width = delta.shape
    steps = rows // packs
    states = a2.shape[0]
    blocks = steps // block
    per_pack = lambda p, i, lens: (p, 0)
    fixed = lambda p, i, lens: (0, 0)
    whole = lambda v: pl.BlockSpec(v.shape, fixed)
    model = tokens.shape[1]
    mats = pl.BlockSpec((steps, width), per_pack)
    toks = pl.BlockSpec((steps, model), per_pack)
    return pl.pallas_call(
        functools.partial(backward_kernel, block=block, group=group, blocks=blocks, rank=rank, taps=taps),
        grid_spec=pltpu.PrefetchScalarGridSpec(
            num_scalar_prefetch=1,
            grid=(packs, blocks),
            in_specs=[
                mats, mats, mats, mats,
                pl.BlockSpec((steps, LANES), per_pack),
                whole(sela), whole(stepb), whole(vec), whole(a2),
                pl.BlockSpec((block, states, width), lambda p, i, lens: (p * blocks + blocks - 1 - i, 0, 0)),
                pl.BlockSpec((1, states, width), lambda p, i, lens: (p, 0, 0)),
                whole(wx), toks, whole(gain), toks, toks,
            ],
            out_specs=[
                mats,
                pl.BlockSpec((width, LANES), fixed),
                pl.BlockSpec((width, LANES), fixed),
                pl.BlockSpec((1, model), fixed),
                toks,
            ],
            scratch_shapes=[
                pltpu.VMEM((states, width), F32),
                pltpu.VMEM((states, width), F32),
                pltpu.VMEM((steps * states, LANES), F32),
                pltpu.VMEM((steps * states, LANES), F32),
                pltpu.VMEM((steps * states, LANES), F32),
                pltpu.VMEM((steps * states, LANES), F32),
                pltpu.VMEM((steps, width), F32),
                pltpu.VMEM((steps, width), F32),
                pltpu.VMEM((steps, width), BF16),
                pltpu.VMEM((ROWS, width), F32),
                pltpu.VMEM((states, width), F32),
            ],
        ),
        out_shape=[
            jax.ShapeDtypeStruct((rows, width), BF16),
            jax.ShapeDtypeStruct((width, LANES), F32),
            jax.ShapeDtypeStruct((width, LANES), F32),
            jax.ShapeDtypeStruct((1, model), F32),
            jax.ShapeDtypeStruct((rows, model), F32),
        ],
        compiler_params=pltpu.CompilerParams(vmem_limit_bytes=56 << 20),
        cost_estimate=pl.CostEstimate(flops=0, bytes_accessed=190_000_000, transcendentals=0),
        name="mixer_backward",
    )(sample, delta, xs, bx, gm, sel, sela, stepb, vec, a2, hall, last, wx, tokens, gain, grad_u, grad_h)


def expert_kernel(*refs, parts):
    q_ref, gy_ref, router_ref, mine_ref = refs[:4]
    ups, downs = refs[4 : 4 + parts], refs[4 + parts : 4 + 2 * parts]
    outs = refs[4 + 2 * parts :]
    result_ref, gq_ref, gr_ref, grouter_ref = outs[:4]
    acts, grads = outs[4 : 4 + parts], outs[4 + parts : 4 + 2 * parts]
    total, back, gates = outs[4 + 2 * parts :]
    step = pl.program_id(0)

    @pl.when(step == 0)
    def _():
        logits = dot(q_ref[...], router_ref[...], ((1,), (1,)))
        odds = jnp.exp(logits - jnp.max(logits, axis=1, keepdims=True))
        probs = odds / jnp.sum(odds, axis=1, keepdims=True)
        gate = jnp.sum(probs * mine_ref[...], axis=1, keepdims=True)
        gates[...] = gate * (mine_ref[...] - probs)
        gr_ref[...] = (gate * gy_ref[...].astype(F32)).astype(BF16)
        total[...] = jnp.zeros_like(total)
        back[...] = jnp.zeros_like(back)

    q, gr = q_ref[...], gr_ref[...]
    root = 0.7978845608028654
    for k in range(parts):
        pre = dot(q, ups[k][...])
        grad_act = dot(gr, downs[k][...], ((1,), (1,)))
        square = pre * pre
        t = jnp.tanh(root * pre * (1.0 + 0.044715 * square))
        half = 0.5 * (1.0 + t)
        act = (pre * half).astype(BF16)
        slope = half + (0.5 * root) * pre * (1.0 - t * t) * (1.0 + 0.134145 * square)
        grad = (grad_act * slope).astype(BF16)
        acts[k][...] = act
        grads[k][...] = grad
        total[...] += dot(act, downs[k][...])
        back[...] += dot(grad, ups[k][...], ((1,), (1,)))

    @pl.when(step == pl.num_programs(0) - 1)
    def _():
        result = total[...].astype(BF16)
        result_ref[...] = result
        grad_gate = jnp.sum(gy_ref[...].astype(F32) * result.astype(F32), axis=1, keepdims=True)
        grad_logits = (grad_gate * gates[...]).astype(BF16)
        grouter_ref[...] = dot(grad_logits, q_ref[...], ((0,), (0,)))
        gq_ref[...] = (dot(grad_logits, router_ref[...]) + back[...]).astype(BF16)


def expert_pass(q, gy, router, mine, ups, downs):
    rows, model = q.shape
    experts = router.shape[0]
    parts = len(ups)
    hidden = ups[0].shape[1]
    block = 256 if hidden % 256 == 0 else 128
    fixed = lambda i: (0, 0)
    whole = lambda shape: pl.BlockSpec(shape, fixed)
    across = lambda n: pl.BlockSpec((n, block), lambda i: (0, i))
    down = pl.BlockSpec((block, model), lambda i: (i, 0))
    outs = pl.pallas_call(
        functools.partial(expert_kernel, parts=parts),
        grid=(hidden // block,),
        in_specs=[whole(q.shape), whole(gy.shape), whole(router.shape), whole(mine.shape)]
        + [across(model)] * parts
        + [down] * parts,
        out_specs=[whole((rows, model))] * 3 + [whole((experts, model))] + [across(rows)] * (2 * parts),
        out_shape=[jax.ShapeDtypeStruct((rows, model), BF16)] * 3
        + [jax.ShapeDtypeStruct((experts, model), F32)]
        + [jax.ShapeDtypeStruct((rows, hidden), BF16)] * (2 * parts),
        scratch_shapes=[pltpu.VMEM((rows, model), F32), pltpu.VMEM((rows, model), F32), pltpu.VMEM((rows, experts), F32)],
        compiler_params=pltpu.CompilerParams(vmem_limit_bytes=56 << 20),
        cost_estimate=pl.CostEstimate(flops=0, bytes_accessed=70_000_000, transcendentals=0),
        name="expert_pass",
    )(q, gy, router, mine, *ups, *downs)
    return (*outs[:4], outs[4 : 4 + parts], outs[4 + parts :])


def unfold_all(values, count):
    n, rows, width = values.shape
    return values.reshape(n, rows, count, width // count).transpose(0, 2, 1, 3).reshape(-1, width // count)


def swap(values, axis, mask):
    count = lax.axis_size(axis)
    return lax.ppermute(values, axis, [(i, i ^ mask) for i in range(count)])


def grow(values, axis, mask, dim):
    got = swap(values, axis, mask)
    upper = (lax.axis_index(axis) & mask) != 0
    return jnp.concatenate([jnp.where(upper, got, values), jnp.where(upper, values, got)], axis=dim)


def gather_rows(values):
    rows, width = values.shape
    bits = lax.axis_size("fsdp").bit_length() - 1
    place = lambda bit: bits - 1 - bit
    whole = values.reshape((1,) * bits + (rows, width))
    for bit in range(2, bits):
        whole = grow(whole, "fsdp", 1 << bit, place(bit))
    first = grow(whole[..., : width // 2], "fsdp", 2, place(1))
    second = grow(whole[..., width // 2 :], "fsdp", 1, place(0))
    first = grow(first, "fsdp", 1, place(0))
    second = grow(second, "fsdp", 2, place(1))
    whole = jnp.concatenate([first, second], axis=-1).reshape(1, -1, rows, width)
    mask = 1
    while mask < lax.axis_size("dp"):
        whole = grow(whole.reshape(1, -1, rows, width), "dp", mask, 0)
        mask *= 2
    return whole.reshape(-1, rows, width)


def fold(values, count):
    rows = values.shape[-2] // count
    return jnp.concatenate([values[..., j * rows : (j + 1) * rows, :] for j in range(count)], axis=-1)


def unfold(values, count):
    width = values.shape[-1] // count
    return jnp.concatenate([values[..., j * width : (j + 1) * width] for j in range(count)], axis=-2)


def own_block(values, index, count, axis):
    size = values.shape[axis] // count
    return lax.dynamic_slice_in_dim(values, index * size, size, axis)


def scatter_begin(piece):
    me, groups = lax.axis_index("dp"), lax.axis_size("dp")
    sent = [swap(piece(me ^ k).astype(BF16), "dp", k) for k in range(1, groups)]
    total = piece(me).astype(F32)
    for got in sent:
        total = total + got.astype(F32)
    return total.astype(BF16)


def scatter_end(parts):
    return jnp.sum(lax.all_to_all(parts, "fsdp", 0, 0, tiled=True).astype(F32), axis=0)


def rows_of(left, right, i):
    product = dot(own_block(left, i, lax.axis_size("dp"), 1), right, ((0,), (0,)))
    return product.reshape(lax.axis_size("fsdp"), -1, product.shape[1])


def norm_backward(grad_normed, gain, normed, inv_scale):
    scaled = grad_normed * gain
    grad_in = inv_scale * (scaled - normed * jnp.mean(scaled * normed, axis=-1, keepdims=True))
    return (grad_in, jnp.sum(grad_normed * normed, axis=0))


def body(
    tokens,
    cotangent,
    routes,
    lengths,
    norm1_gain,
    input_weight,
    conv_weight,
    conv_bias,
    scan_weight,
    step_weight,
    step_bias,
    decay_log,
    skip_gain,
    out_weight,
    norm2_gain,
    router_weight,
    expert_up,
    expert_down,
):
    micro, steps, model = tokens.shape
    rows = micro * steps
    experts = lax.axis_size("fsdp")
    groups = lax.axis_size("dp")
    devices = experts * groups
    capacity = (5 * steps + 4 * experts - 1) // (4 * experts)
    slots = micro * capacity
    inner = input_weight.shape[1] // 2
    states = decay_log.shape[1]
    rank = step_weight.shape[1]
    taps = conv_weight.shape[1]
    own_model, own_inner = norm1_gain.shape[0], conv_bias.shape[0]

    half = experts // 2
    vectors = jnp.concatenate(
        [
            conv_weight,
            jnp.stack([conv_bias, step_bias, skip_gain, jnp.concatenate([norm1_gain, norm2_gain])]).T,
            decay_log,
            jnp.concatenate([router_weight[:, :half], router_weight[:, half:]], axis=0),
        ],
        axis=1,
    )
    padding = lambda n: jnp.zeros((own_inner, n), BF16)
    small = jnp.concatenate(
        [
            scan_weight,
            padding(LANES - rank - 2 * states),
            step_weight,
            vectors,
            padding(LANES - rank - vectors.shape[1]),
        ],
        axis=1,
    )
    folds = inner // (2 * LANES)
    early = gather_rows(jnp.concatenate([input_weight[:, :inner], fold(small, folds)], axis=0))
    late = jnp.concatenate([input_weight[:, inner : inner + model], input_weight[:, inner + model :], out_weight], axis=0)
    late = lax.all_gather(late, ("dp", "fsdp"), axis=0, tiled=False)
    input_z = [late[:, i * own_model : (i + 1) * own_model].reshape(model, model) for i in range(2)]
    output_full = late[:, 2 * own_model :].reshape(inner, model)
    ups = [expert_up[0]] + [swap(expert_up[0], "dp", k) for k in range(1, groups)]
    downs = [expert_down[0]] + [swap(expert_down[0], "dp", k) for k in range(1, groups)]

    place = jnp.arange(steps, dtype=jnp.int32)
    sample = lengths[:, 0, 0]
    live = (place[None, :] < sample[:, None]).astype(jnp.int32)
    route = routes[:, :, 0]
    expert_ids = jnp.arange(experts, dtype=jnp.int32)
    route_hot = (route[:, :, None] == expert_ids).astype(BF16)
    live_hot = route_hot * live[:, :, None].astype(BF16)
    earlier = (place[:, None] > place[None, :]).astype(BF16)
    before = lax.dot_general(
        jnp.broadcast_to(earlier, (micro, steps, steps)), live_hot, (((2,), (1,)), ((0,), (0,))),
        preferred_element_type=F32,
    )
    slot = jnp.sum(before * live_hot.astype(F32), axis=2).astype(jnp.int32)
    kept = (live * (slot < capacity).astype(jnp.int32)).reshape(rows)
    live = live.reshape(rows).astype(F32)
    target = (route * slots + jnp.arange(micro, dtype=jnp.int32)[:, None] * capacity + slot).reshape(rows)
    chooser = (
        (jnp.arange(experts * slots, dtype=jnp.int32)[:, None] == target[None, :]) & (kept[None, :] == 1)
    ).astype(BF16)
    kept = kept.astype(F32)
    route_float = route_hot.reshape(rows, experts).astype(F32)

    def to_experts(values):
        return lax.all_to_all(values.reshape(experts, slots, -1), "fsdp", 0, 0, tiled=True).reshape(experts * slots, -1)

    def from_experts(values):
        return dot(chooser, values.reshape(experts * slots, -1), ((0,), (0,)))

    def back_home(values):
        return lax.all_to_all(values.reshape(experts, slots, -1), "fsdp", 0, 0, tiled=True)

    cotangent = cotangent.reshape(rows, model)
    upstream = cotangent.astype(F32)

    hidden = tokens.reshape(rows, model).astype(F32)
    inv_first = lax.rsqrt(jnp.mean(hidden * hidden, axis=-1, keepdims=True) + EPSILON)
    normed_first = hidden * inv_first
    early, upstream_rows = lax.optimization_barrier((early, dot(chooser, cotangent).astype(BF16)))
    upstream_sent = to_experts(upstream_rows)
    input_x = early[:, :own_model].reshape(model, inner)
    small_full = unfold_all(early[:, own_model:], folds)
    select_full, step_full = small_full[:, :LANES], small_full[:, LANES:]
    vectors_full = step_full[:, rank:].T
    vectors_first = vectors_full[:ROWS].astype(F32)
    decay_full = vectors_full[taps + 4 : taps + 4 + states].astype(F32)
    gains = vectors_full[taps + 3].reshape(devices, 2, own_model)
    gain_one = gains[:, 0].reshape(model).astype(F32)
    gain_two = gains[:, 1].reshape(model).astype(F32)
    router_full = vectors_full[taps + 4 + states : taps + 4 + states + half].reshape(half, devices, 2, own_model)
    router_full = router_full.transpose(2, 0, 1, 3).reshape(experts, model)

    normed_low = (normed_first * gain_one).astype(BF16)
    decay_mat = -jnp.exp(decay_full)
    decay_two = decay_mat * LOG2E
    branch_x, scan_in, step_size, selected, mixer_out, state_all, state_last = mixer_forward(
        sample, normed_low, input_x, select_full, step_full, vectors_first, decay_two, micro, rank, taps
    )
    mixer_out, upstream_sent = lax.optimization_barrier((mixer_out, upstream_sent))
    branch_z = jnp.concatenate([dot(normed_low, part) for part in input_z], axis=1)
    sigmoid_z = jax.nn.sigmoid(branch_z)
    silu_z = branch_z * sigmoid_z
    gated_low = (mixer_out * silu_z).astype(BF16)
    mixed = dot(gated_low, output_full)

    residual = hidden + live[:, None] * mixed
    inv_second = lax.rsqrt(jnp.mean(residual * residual, axis=-1, keepdims=True) + EPSILON)
    normed_second = residual * inv_second
    routed = (normed_second * gain_two).astype(BF16)
    probs = jax.nn.softmax(dot(routed, router_full, ((1,), (1,))), axis=-1)
    gate = jnp.sum(probs * route_float, axis=1)
    weight_row = gate * kept
    received = to_experts(dot(chooser, routed).astype(BF16))

    mine = (expert_ids == lax.axis_index("fsdp")).astype(F32)[None, :]
    result, grad_rows, flat_grad, router_grad, acts, grad_pres = expert_pass(
        received, upstream_sent, router_full, mine, ups, downs
    )
    grad_rows, result, received, flat_grad = lax.optimization_barrier((grad_rows, result, received, flat_grad))
    grad_back = back_home(grad_rows)
    up_grad = dot(received, grad_pres[0], ((0,), (0,)))
    down_grad = dot(acts[0], flat_grad, ((0,), (0,)))
    for k in range(1, groups):
        up_grad = up_grad + swap(dot(received, grad_pres[k], ((0,), (0,))).astype(BF16), "dp", k).astype(F32)
        down_grad = down_grad + swap(dot(acts[k], flat_grad, ((0,), (0,))).astype(BF16), "dp", k).astype(F32)
    grad_back, result, up_grad, down_grad = lax.optimization_barrier((grad_back, result, up_grad, down_grad))
    result = back_home(result)

    grad_routed = from_experts(grad_back)
    grad_norm_two, gain_two_grad = norm_backward(grad_routed, gain_two, normed_second, inv_second)
    grad_residual = upstream + grad_norm_two
    grad_mixed = (live[:, None] * grad_residual).astype(BF16)

    grad_gated = dot(grad_mixed, output_full, ((1,), (1,)))
    grad_mixer = grad_gated * silu_z
    grad_z = (grad_gated * mixer_out * sigmoid_z * (1.0 + branch_z * (1.0 - sigmoid_z))).astype(BF16)
    late_terms = scatter_begin(
        lambda i: jnp.concatenate(
            [rows_of(normed_low, grad_z, i), fold(rows_of(gated_low, grad_mixed, i), 2)], axis=1
        )
    )
    grad_normed_z = sum(
        dot(grad_z[:, i * model : (i + 1) * model], part, ((1,), (1,))) for i, part in enumerate(input_z)
    )
    grad_mixer, grad_normed_z, late_terms, result = lax.optimization_barrier((grad_mixer, grad_normed_z, late_terms, result))
    late_grads = lax.all_to_all(late_terms, "fsdp", 0, 0, tiled=True)
    grad_x, select_grad, step_grad, gain_one_grad, tokens_grad = mixer_backward(
        sample, step_size, scan_in, branch_x, grad_mixer, selected, select_full, step_full, vectors_first, decay_two,
        state_all, state_last, input_x, tokens.reshape(rows, model), gain_one[None, :], grad_normed_z, grad_residual,
        micro, rank, taps,
    )
    grad_x, late_grads = lax.optimization_barrier((grad_x, late_grads))

    gain_grads = jnp.concatenate(
        [gain_one_grad.reshape(devices, 1, own_model), gain_two_grad.reshape(devices, 1, own_model)], axis=1
    ).reshape(inner, 1)
    router_grads = (
        router_grad.reshape(2, half, devices, own_model).transpose(2, 0, 3, 1).reshape(inner, half)
    )
    at_gain, at_decay, at_router = rank + taps + 3, rank + taps + 4, rank + taps + 4 + states
    lane = jnp.arange(LANES)
    step_grad = jnp.where(lane == at_gain, gain_grads, step_grad) + jnp.pad(
        router_grads, ((0, 0), (at_router, LANES - at_router - half))
    )

    def early_terms(i):
        blocks = [own_block(v, i, groups, 0).reshape(experts, own_inner, LANES) for v in (select_grad, step_grad)]
        return jnp.concatenate([rows_of(normed_low, grad_x, i), fold(jnp.concatenate(blocks, axis=2), folds)], axis=1)

    early_grads = scatter_end(scatter_begin(early_terms))
    late_grads = jnp.sum(late_grads.astype(F32), axis=0)
    block_output = (residual + weight_row[:, None] * from_experts(result)).astype(BF16)
    small_grads = unfold(early_grads[own_model:], folds)
    vector_grads = small_grads[:, LANES:]
    routers = vector_grads[:, at_router : at_router + half]
    return (
        block_output.reshape(micro, steps, model),
        tokens_grad.reshape(micro, steps, model),
        vector_grads[:own_model, at_gain],
        jnp.concatenate([early_grads[:own_model], late_grads[:own_model]], axis=1),
        vector_grads[:, rank : rank + taps],
        vector_grads[:, rank + taps],
        small_grads[:, : rank + 2 * states],
        vector_grads[:, :rank],
        vector_grads[:, rank + taps + 1],
        vector_grads[:, at_decay : at_decay + states],
        vector_grads[:, rank + taps + 2],
        unfold(late_grads[own_model:], 2),
        vector_grads[own_model:, at_gain],
        jnp.concatenate([routers[:own_model], routers[own_model:]], axis=1),
        up_grad[None],
        down_grad[None],
    )


def solution(mesh):
    rows3 = P(None, ("dp", "fsdp"), None)
    vector = P(("dp", "fsdp"))
    matrix = P(("dp", "fsdp"), None)
    weights = (
        vector, matrix, matrix, vector, matrix, matrix, vector, matrix, vector, matrix, vector, matrix,
        P("fsdp", None, "dp"), P("fsdp", "dp", None),
    )
    return jax.shard_map(
        body,
        mesh=mesh,
        in_specs=(rows3, rows3, rows3, rows3) + weights,
        out_specs=(rows3, rows3) + weights,
        check_vma=False,
    )
```

```python
import functools

import jax
import jax.numpy as jnp
from jax import lax
from jax.experimental import pallas as pl
from jax.experimental.pallas import tpu as pltpu
from jax.sharding import PartitionSpec as P

EPSILON = 1e-05
LOG2E = 1.4426950408889634
LN2 = 0.6931471805599453
LANES = 128
ROWS = 8
F32 = jnp.float32
BF16 = jnp.bfloat16


def dot(left, right, dims=((1,), (0,))):
    return lax.dot_general(left, right, (dims, ((), ())), preferred_element_type=F32)


def fold_rows(parts):
    place = lax.broadcasted_iota(jnp.int32, parts[0].shape, 0)
    half = 1
    while half < ROWS:
        lower = (place & half) == 0
        merged = []
        for i in range(0, len(parts), 2):
            a, b = parts[i], parts[i + 1]
            merged.append(jnp.where(lower, a, b) + pltpu.roll(jnp.where(lower, b, a), half, 0))
        parts = merged
        half *= 2
    return parts[0]


def sum_states(parts):
    halves = []
    for p in parts:
        total = p[:ROWS]
        for i in range(1, p.shape[0] // ROWS):
            total = total + p[i * ROWS : (i + 1) * ROWS]
        halves.append(total)
    return fold_rows(halves)


def lane_chunk(k, count=1):
    return pl.ds(pl.multiple_of(k * LANES * count, LANES), LANES * count)


def split_low(values):
    high = values.astype(BF16)
    return high, (values - high.astype(F32)).astype(BF16)


def own_lanes(first, states, size):
    lane = lax.broadcasted_iota(jnp.int32, (size, states, LANES), 2)
    row = lax.broadcasted_iota(jnp.int32, (size, states, LANES), 1)
    return (lane == row + first) | (lane == row + first + states)


def widen(selected, first, states, bw, cw):
    steps = selected.shape[0]
    lane = lax.broadcasted_iota(jnp.int32, (2 * LANES, 2 * LANES), 0) % LANES
    to_c = lax.broadcasted_iota(jnp.int32, (2 * LANES, 2 * LANES), 1) >= LANES
    spread = (to_c == (lane >= first + states)).astype(BF16)
    size = 64
    own = own_lanes(first, states, size)
    for at in range(0, steps, size):
        rows = jnp.where(own, selected[at : at + size][:, None, :], 0.0).reshape(size * states, LANES)
        wide = dot(jnp.concatenate(split_low(rows), axis=1), spread)
        bw[at * states : (at + size) * states, :] = wide[:, :LANES]
        cw[at * states : (at + size) * states, :] = wide[:, LANES:]


def narrow(gb, gc, first, states, steps):
    lane = lax.broadcasted_iota(jnp.int32, (2 * LANES, LANES), 1)
    from_c = lax.broadcasted_iota(jnp.int32, (2 * LANES, LANES), 0) >= LANES
    gather = (from_c == (lane >= first + states)).astype(BF16)
    size = 64
    own = own_lanes(first, states, size)
    out = []
    for at in range(0, steps, size):
        here = slice(at * states, (at + size) * states)
        rows = jnp.concatenate([gb[here, :].astype(BF16), gc[here, :].astype(BF16)], axis=1)
        sums = dot(rows, gather).reshape(size, states, LANES)
        out.append(jnp.sum(jnp.where(own, sums, 0.0), axis=1))
    return jnp.concatenate(out, axis=0)


def conv_of(x_ref, vec_ref, lanes, taps, steps):
    total = vec_ref[taps : taps + 1, lanes]
    for shift in range(taps):
        total = total + vec_ref[taps - 1 - shift : taps - shift, lanes] * x_ref[ROWS - shift : ROWS - shift + steps, lanes]
    return total


def forward_kernel(len_ref, u_ref, wx_ref, sela_ref, stepb_ref, vec_ref, a_ref,
                   bx_ref, xs_ref, delta_ref, sel_ref, mix_ref, h_ref,
                   state, bw, cw, low, *, group, rank, taps):
    states, width = a_ref.shape
    steps = u_ref.shape[0]
    chunks = width // LANES
    bias_step, skip = taps + 1, taps + 2
    state[...] = jnp.zeros_like(state)
    bx_ref[:ROWS, :] = jnp.zeros((ROWS, width), F32)

    def project(k, _):
        lanes = lane_chunk(k, 2)
        bx_ref[ROWS:, lanes] = dot(u_ref[...], wx_ref[:, lanes])
        return 0

    lax.fori_loop(0, chunks // 2, project, 0, unroll=True)

    def convolve(k, _):
        lanes = lane_chunk(k)
        conv = conv_of(bx_ref, vec_ref, lanes, taps, steps)
        xs = conv * jax.nn.sigmoid(conv)
        xs_ref[:, lanes] = xs
        low[:, lanes] = xs.astype(BF16)
        return 0

    lax.fori_loop(0, chunks, convolve, 0, unroll=2)
    selected = dot(low[...], sela_ref[...])
    sel_ref[...] = selected
    lane = lax.broadcasted_iota(jnp.int32, selected.shape, 1)
    rank_low = jnp.where(lane < rank, selected, 0.0).astype(BF16)
    widen(selected, rank, states, bw, cw)

    def sizes(k, _):
        lanes = lane_chunk(k, 2)
        pre = dot(rank_low, stepb_ref[lanes, :], ((1,), (1,))) + vec_ref[bias_step : bias_step + 1, lanes]
        delta_ref[:, lanes] = jnp.maximum(pre, 0.0) + jnp.log1p(jnp.exp(-jnp.abs(pre)))
        return 0

    lax.fori_loop(0, chunks // 2, sizes, 0, unroll=2)

    def rows(s, _):
        at = pl.multiple_of(s * ROWS, ROWS)

        def chunk(g, _):
            for u in range(group):
                lanes = lane_chunk(g * group + u)
                d = delta_ref[pl.ds(at, ROWS), lanes]
                x = xs_ref[pl.ds(at, ROWS), lanes]
                dx = d * x
                a = a_ref[:, lanes]
                h = state[:, lanes]
                h_ref[s, :, lanes] = h
                parts = []
                for t in range(ROWS):
                    here = pl.ds(pl.multiple_of((at + t) * states, states), states)
                    h = jnp.exp2(d[t : t + 1] * a) * h + bw[here, :] * dx[t : t + 1]
                    parts.append(cw[here, :] * h)
                state[:, lanes] = h
                mix_ref[pl.ds(at, ROWS), lanes] = sum_states(parts) + vec_ref[skip : skip + 1, lanes] * x
            return 0

        lax.fori_loop(0, chunks // group, chunk, 0)
        return 0

    used = (len_ref[pl.program_id(0)] + ROWS - 1) // ROWS
    lax.fori_loop(0, used, rows, 0)

    def clear(s, _):
        mix_ref[pl.ds(pl.multiple_of(s * ROWS, ROWS), ROWS), :] = jnp.zeros((ROWS, width), F32)
        return 0

    lax.fori_loop(used, steps // ROWS, clear, 0)


def mixer_forward(sample, u, wx, sela, stepb, vec, a2, packs, rank, taps, group=12):
    rows, model = u.shape
    steps = rows // packs
    states, width = a2.shape
    per_pack = lambda p, lens: (p, 0)
    whole = lambda v: pl.BlockSpec(v.shape, lambda p, lens: (0, 0))
    mats = pl.BlockSpec((steps, width), per_pack)
    return pl.pallas_call(
        functools.partial(forward_kernel, group=group, rank=rank, taps=taps),
        grid_spec=pltpu.PrefetchScalarGridSpec(
            num_scalar_prefetch=1,
            grid=(packs,),
            in_specs=[pl.BlockSpec((steps, model), per_pack), whole(wx), whole(sela), whole(stepb), whole(vec), whole(a2)],
            out_specs=[
                pl.BlockSpec((steps + ROWS, width), per_pack),
                mats,
                mats,
                pl.BlockSpec((steps, LANES), per_pack),
                mats,
                pl.BlockSpec((steps // ROWS, states, width), lambda p, lens: (p, 0, 0)),
            ],
            scratch_shapes=[
                pltpu.VMEM((states, width), F32),
                pltpu.VMEM((steps * states, LANES), F32),
                pltpu.VMEM((steps * states, LANES), F32),
                pltpu.VMEM((steps, width), BF16),
            ],
        ),
        out_shape=[
            jax.ShapeDtypeStruct((rows + packs * ROWS, width), F32),
            jax.ShapeDtypeStruct((rows, width), F32),
            jax.ShapeDtypeStruct((rows, width), F32),
            jax.ShapeDtypeStruct((rows, LANES), F32),
            jax.ShapeDtypeStruct((rows, width), F32),
            jax.ShapeDtypeStruct((rows // ROWS, states, width), F32),
        ],
        compiler_params=pltpu.CompilerParams(vmem_limit_bytes=56 << 20),
        cost_estimate=pl.CostEstimate(flops=0, bytes_accessed=120_000_000, transcendentals=0),
        name="mixer_forward",
    )(sample, u, wx, sela, stepb, vec, a2)


def backward_kernel(len_ref, delta_ref, xs_ref, bx_ref, gm_ref, sel_ref, sela_ref, stepb_ref, vec_ref, a_ref, h_ref,
                    wx_ref, x_ref, gain_ref, gu_ref, gh_ref,
                    gx_ref, gsel_ref, gstep_ref, ggain_ref, gtok_ref,
                    mu_s, bw, cw, gb, gc, gd, gxs, low, gvec_ref, ga_ref, *, group, rank, taps):
    pack = pl.program_id(0)
    states, width = a_ref.shape
    steps = sel_ref.shape[0]
    chunks = width // LANES
    bias_conv, bias_step, skip = taps, taps + 1, taps + 2

    @pl.when(pack == 0)
    def _():
        ga_ref[...] = jnp.zeros_like(ga_ref)
        gsel_ref[...] = jnp.zeros_like(gsel_ref)
        gstep_ref[...] = jnp.zeros_like(gstep_ref)
        gvec_ref[...] = jnp.zeros_like(gvec_ref)
        ggain_ref[...] = jnp.zeros_like(ggain_ref)

    mu_s[...] = jnp.zeros_like(mu_s)
    gb[...] = jnp.zeros_like(gb)
    gc[...] = jnp.zeros_like(gc)
    selected = sel_ref[...]
    widen(selected, rank, states, bw, cw)
    used = (len_ref[pack] + ROWS - 1) // ROWS

    def clear(s, _):
        here = pl.ds(pl.multiple_of(s * ROWS, ROWS), ROWS)
        gd[here, :] = jnp.zeros((ROWS, width), F32)
        gxs[here, :] = jnp.zeros((ROWS, width), F32)
        return 0

    lax.fori_loop(used, steps // ROWS, clear, 0)

    def rows(back, _):
        s = used - 1 - back
        at = pl.multiple_of(s * ROWS, ROWS)
        place = [pl.ds(pl.multiple_of((at + t) * states, states), states) for t in range(ROWS)]

        def chunk(g, _):
            each = []
            for u in range(group):
                lanes = lane_chunk(g * group + u)
                d = delta_ref[pl.ds(at, ROWS), lanes]
                x = xs_ref[pl.ds(at, ROWS), lanes]
                a = a_ref[:, lanes]
                dx = d * x
                h, decay = [h_ref[s, :, lanes]], []
                for t in range(ROWS):
                    decay.append(jnp.exp2(d[t : t + 1] * a))
                    h.append(decay[t] * h[t] + bw[place[t], :] * dx[t : t + 1])
                each.append(dict(lanes=lanes, d=d, x=x, gy=gm_ref[pl.ds(at, ROWS), lanes], dx=dx, a=a, mu=mu_s[:, lanes],
                                 h=h, decay=decay, ga=ga_ref[:, lanes], sp=[None] * ROWS, gp=[None] * ROWS))
            for t in range(ROWS - 1, -1, -1):
                b, c = bw[place[t], :], cw[place[t], :]
                one_b = one_c = None
                for v in each:
                    gyt = v["gy"][t : t + 1]
                    lam = c * gyt + v["mu"]
                    v["sp"][t] = b * lam
                    to_b = lam * v["dx"][t : t + 1]
                    to_c = v["h"][t + 1] * gyt
                    one_b = to_b if one_b is None else one_b + to_b
                    one_c = to_c if one_c is None else one_c + to_c
                    v["mu"] = v["decay"][t] * lam
                    q = v["mu"] * v["h"][t]
                    v["gp"][t] = q * v["a"]
                    v["ga"] = v["ga"] + q * v["d"][t : t + 1]
                gb[place[t], :] += one_b
                gc[place[t], :] += one_c
            for v in each:
                lanes = v["lanes"]
                mu_s[:, lanes], ga_ref[:, lanes] = v["mu"], v["ga"]
                total = sum_states(v["sp"])
                gd[pl.ds(at, ROWS), lanes] = sum_states(v["gp"]) * LN2 + v["x"] * total
                gxs[pl.ds(at, ROWS), lanes] = v["d"] * total
            return 0

        lax.fori_loop(0, chunks // group, chunk, 0)
        return 0

    lax.fori_loop(0, used, rows, 0)

    def add_row(row, lanes, values):
        gvec_ref[row : row + 1, lanes] += jnp.sum(values, axis=0, keepdims=True)

    def sizes(k, _):
        lanes = lane_chunk(k)
        d = delta_ref[:, lanes]
        rise = jnp.where(d < 0.01, d * (1.0 - d * (0.5 - d * (1.0 / 6.0))), 1.0 - jnp.exp(-d))
        grad = gd[:steps, lanes] * rise
        add_row(bias_step, lanes, grad)
        low[:, lanes] = grad.astype(BF16)
        add_row(skip, lanes, gm_ref[:, lanes] * xs_ref[:, lanes])
        return 0

    lax.fori_loop(0, chunks, sizes, 0, unroll=2)
    gd[steps:, :] = jnp.zeros((ROWS, width), F32)
    lane = lax.broadcasted_iota(jnp.int32, selected.shape, 1)
    rank_low = jnp.where(lane < rank, selected, 0.0).astype(BF16)
    grad_rank = dot(low[...], stepb_ref[...])
    gstep_ref[...] += dot(low[...], rank_low, ((0,), (0,)))
    grad_sel = jnp.where(lane < rank, grad_rank, narrow(gb, gc, rank, states, steps)).astype(BF16)

    def values(k, _):
        lanes = lane_chunk(k)
        conv = conv_of(bx_ref, vec_ref, lanes, taps, steps)
        sig = jax.nn.sigmoid(conv)
        low[:, lanes] = (conv * sig).astype(BF16)
        grad = dot(grad_sel, sela_ref[lanes, :], ((1,), (1,)))
        grad = grad + gxs[:, lanes] + gm_ref[:, lanes] * vec_ref[skip : skip + 1, lanes]
        grad = grad * (sig * (1.0 + conv * (1.0 - sig)))
        gd[:steps, lanes] = grad
        add_row(bias_conv, lanes, grad)
        back_x = None
        for j in range(taps):
            shift = taps - 1 - j
            add_row(j, lanes, grad * bx_ref[ROWS - shift : ROWS - shift + steps, lanes])
            term = vec_ref[j : j + 1, lanes] * gd[shift : shift + steps, lanes]
            back_x = term if back_x is None else back_x + term
        gx_ref[:, lanes] = back_x.astype(BF16)
        return 0

    lax.fori_loop(0, chunks, values, 0, unroll=2)
    gsel_ref[...] += dot(low[...], grad_sel, ((0,), (0,)))

    hidden = x_ref[...].astype(F32)
    inv = lax.rsqrt(jnp.mean(hidden * hidden, axis=1, keepdims=True) + EPSILON)
    normed = hidden * inv
    grad_u = dot(gx_ref[...], wx_ref[...], ((1,), (1,))) + gu_ref[...]
    scaled = grad_u * gain_ref[...]
    ggain_ref[...] += jnp.sum(grad_u * normed, axis=0, keepdims=True)
    gtok_ref[...] = gh_ref[...] + inv * (scaled - normed * jnp.mean(scaled * normed, axis=1, keepdims=True))

    @pl.when(pack == pl.num_programs(0) - 1)
    def _():
        rows_of_vectors = jnp.concatenate([gvec_ref[...], ga_ref[...] * a_ref[...] * LN2], axis=0)
        before = jnp.zeros((rank, width), F32)
        after = jnp.zeros((LANES - rank - rows_of_vectors.shape[0], width), F32)
        gstep_ref[...] += jnp.concatenate([before, rows_of_vectors, after], axis=0).T


def mixer_backward(sample, delta, xs, bx, gm, sel, sela, stepb, vec, a2, hall, wx, tokens, gain, grad_u, grad_h,
                   packs, rank, taps, group=2):
    rows, width = delta.shape
    steps = rows // packs
    states, model = a2.shape[0], tokens.shape[1]
    per_pack = lambda p, lens: (p, 0)
    fixed = lambda p, lens: (0, 0)
    whole = lambda v: pl.BlockSpec(v.shape, fixed)
    mats = pl.BlockSpec((steps, width), per_pack)
    toks = pl.BlockSpec((steps, model), per_pack)
    return pl.pallas_call(
        functools.partial(backward_kernel, group=group, rank=rank, taps=taps),
        grid_spec=pltpu.PrefetchScalarGridSpec(
            num_scalar_prefetch=1,
            grid=(packs,),
            in_specs=[
                mats, mats,
                pl.BlockSpec((steps + ROWS, width), per_pack),
                mats,
                pl.BlockSpec((steps, LANES), per_pack),
                whole(sela), whole(stepb), whole(vec), whole(a2),
                pl.BlockSpec((steps // ROWS, states, width), lambda p, lens: (p, 0, 0)),
                whole(wx), toks, whole(gain), toks, toks,
            ],
            out_specs=[
                mats,
                pl.BlockSpec((width, LANES), fixed),
                pl.BlockSpec((width, LANES), fixed),
                pl.BlockSpec((1, model), fixed),
                toks,
            ],
            scratch_shapes=[
                pltpu.VMEM((states, width), F32),
                pltpu.VMEM((steps * states, LANES), F32),
                pltpu.VMEM((steps * states, LANES), F32),
                pltpu.VMEM((steps * states, LANES), F32),
                pltpu.VMEM((steps * states, LANES), F32),
                pltpu.VMEM((steps + ROWS, width), F32),
                pltpu.VMEM((steps, width), F32),
                pltpu.VMEM((steps, width), BF16),
                pltpu.VMEM((ROWS, width), F32),
                pltpu.VMEM((states, width), F32),
            ],
        ),
        out_shape=[
            jax.ShapeDtypeStruct((rows, width), BF16),
            jax.ShapeDtypeStruct((width, LANES), F32),
            jax.ShapeDtypeStruct((width, LANES), F32),
            jax.ShapeDtypeStruct((1, model), F32),
            jax.ShapeDtypeStruct((rows, model), F32),
        ],
        compiler_params=pltpu.CompilerParams(vmem_limit_bytes=60 << 20),
        cost_estimate=pl.CostEstimate(flops=0, bytes_accessed=190_000_000, transcendentals=0),
        name="mixer_backward",
    )(sample, delta, xs, bx, gm, sel, sela, stepb, vec, a2, hall, wx, tokens, gain, grad_u, grad_h)


def expert_kernel(*refs, parts):
    q_ref, gy_ref, router_ref, mine_ref = refs[:4]
    ups, downs = refs[4 : 4 + parts], refs[4 + parts : 4 + 2 * parts]
    outs = refs[4 + 2 * parts :]
    result_ref, gq_ref, gr_ref, grouter_ref = outs[:4]
    acts, grads = outs[4 : 4 + parts], outs[4 + parts : 4 + 2 * parts]
    total, back, gates = outs[4 + 2 * parts :]
    step = pl.program_id(0)

    @pl.when(step == 0)
    def _():
        logits = dot(q_ref[...], router_ref[...], ((1,), (1,)))
        odds = jnp.exp(logits - jnp.max(logits, axis=1, keepdims=True))
        probs = odds / jnp.sum(odds, axis=1, keepdims=True)
        gate = jnp.sum(probs * mine_ref[...], axis=1, keepdims=True)
        gates[...] = gate * (mine_ref[...] - probs)
        gr_ref[...] = (gate * gy_ref[...].astype(F32)).astype(BF16)
        total[...] = jnp.zeros_like(total)
        back[...] = jnp.zeros_like(back)

    q, gr = q_ref[...], gr_ref[...]
    root = 0.7978845608028654
    for k in range(parts):
        pre = dot(q, ups[k][...])
        grad_act = dot(gr, downs[k][...], ((1,), (1,)))
        square = pre * pre
        t = jnp.tanh(root * pre * (1.0 + 0.044715 * square))
        half = 0.5 * (1.0 + t)
        act = (pre * half).astype(BF16)
        slope = half + (0.5 * root) * pre * (1.0 - t * t) * (1.0 + 0.134145 * square)
        grad = (grad_act * slope).astype(BF16)
        acts[k][...] = act
        grads[k][...] = grad
        total[...] += dot(act, downs[k][...])
        back[...] += dot(grad, ups[k][...], ((1,), (1,)))

    @pl.when(step == pl.num_programs(0) - 1)
    def _():
        result = total[...].astype(BF16)
        result_ref[...] = result
        grad_gate = jnp.sum(gy_ref[...].astype(F32) * result.astype(F32), axis=1, keepdims=True)
        grad_logits = (grad_gate * gates[...]).astype(BF16)
        grouter_ref[...] = dot(grad_logits, q_ref[...], ((0,), (0,)))
        gq_ref[...] = (dot(grad_logits, router_ref[...]) + back[...]).astype(BF16)


def expert_pass(q, gy, router, mine, ups, downs):
    rows, model = q.shape
    experts = router.shape[0]
    parts = len(ups)
    hidden = ups[0].shape[1]
    block = 256 if hidden % 256 == 0 else 128
    fixed = lambda i: (0, 0)
    whole = lambda shape: pl.BlockSpec(shape, fixed)
    across = lambda n: pl.BlockSpec((n, block), lambda i: (0, i))
    down = pl.BlockSpec((block, model), lambda i: (i, 0))
    outs = pl.pallas_call(
        functools.partial(expert_kernel, parts=parts),
        grid=(hidden // block,),
        in_specs=[whole(q.shape), whole(gy.shape), whole(router.shape), whole(mine.shape)]
        + [across(model)] * parts
        + [down] * parts,
        out_specs=[whole((rows, model))] * 3 + [whole((experts, model))] + [across(rows)] * (2 * parts),
        out_shape=[jax.ShapeDtypeStruct((rows, model), BF16)] * 3
        + [jax.ShapeDtypeStruct((experts, model), F32)]
        + [jax.ShapeDtypeStruct((rows, hidden), BF16)] * (2 * parts),
        scratch_shapes=[pltpu.VMEM((rows, model), F32), pltpu.VMEM((rows, model), F32), pltpu.VMEM((rows, experts), F32)],
        compiler_params=pltpu.CompilerParams(vmem_limit_bytes=56 << 20),
        cost_estimate=pl.CostEstimate(flops=0, bytes_accessed=70_000_000, transcendentals=0),
        name="expert_pass",
    )(q, gy, router, mine, *ups, *downs)
    return (*outs[:4], outs[4 : 4 + parts], outs[4 + parts :])
def live_rows(length, steps):
    return (lax.broadcasted_iota(jnp.int32, (steps, 1), 0) < length).astype(F32)


def norm_of(values):
    inv = lax.rsqrt(jnp.mean(values * values, axis=1, keepdims=True) + EPSILON)
    return values * inv, inv


def home_forward_kernel(len_ref, u_ref, wl_ref, wr_ref, wout_ref, mix_ref, x_ref, gain_ref, router_ref, hot_ref, choose_ref,
                        z_ref, gated_ref, h1_ref, weight_ref, sent_ref, total):
    pack = pl.program_id(0)
    steps, model = u_ref.shape
    mixed = jnp.zeros((steps, model), F32)
    for half, w_ref in enumerate((wl_ref, wr_ref)):
        here = slice(half * model, (half + 1) * model)
        z = dot(u_ref[...], w_ref[...])
        z_ref[:, here] = z
        gated = (mix_ref[:, here] * (z * jax.nn.sigmoid(z))).astype(BF16)
        gated_ref[:, here] = gated
        mixed = mixed + dot(gated, wout_ref[here, :])
    h1 = x_ref[...].astype(F32) + live_rows(len_ref[pack], steps) * mixed
    h1_ref[...] = h1
    routed = (norm_of(h1)[0] * gain_ref[...]).astype(BF16)
    logits = dot(routed, router_ref[...], ((1,), (1,)))
    odds = jnp.exp(logits - jnp.max(logits, axis=1, keepdims=True))
    probs = odds / jnp.sum(odds, axis=1, keepdims=True)
    weight_ref[...] = jnp.sum(probs * hot_ref[...], axis=1, keepdims=True)
    sent = dot(choose_ref[...], routed)

    @pl.when(pack == 0)
    def _():
        total[...] = sent

    @pl.when(pack > 0)
    def _():
        total[...] += sent

    @pl.when(pack == pl.num_programs(0) - 1)
    def _():
        sent_ref[...] = total[...].astype(BF16)


def home_forward(sample, u, wz, wout, mix, tokens, gain, router, hot, chooser):
    packs = sample.shape[0]
    rows, model = u.shape
    steps, inner, slots = rows // packs, mix.shape[1], chooser.shape[0]
    whole = lambda v: pl.BlockSpec(v.shape, lambda p, lens: (0, 0))
    part = lambda n: pl.BlockSpec((steps, n), lambda p, lens: (p, 0))
    return pl.pallas_call(
        home_forward_kernel,
        grid_spec=pltpu.PrefetchScalarGridSpec(
            num_scalar_prefetch=1,
            grid=(packs,),
            in_specs=[
                part(model), whole(wz[0]), whole(wz[1]), whole(wout), part(inner), part(model), whole(gain), whole(router),
                part(hot.shape[1]), pl.BlockSpec((slots, steps), lambda p, lens: (0, p)),
            ],
            out_specs=[
                part(inner), part(inner), part(model), part(1), pl.BlockSpec((slots, model), lambda p, lens: (0, 0)),
            ],
            scratch_shapes=[pltpu.VMEM((slots, model), F32)],
        ),
        out_shape=[
            jax.ShapeDtypeStruct((rows, inner), F32),
            jax.ShapeDtypeStruct((rows, inner), BF16),
            jax.ShapeDtypeStruct((rows, model), F32),
            jax.ShapeDtypeStruct((rows, 1), F32),
            jax.ShapeDtypeStruct((slots, model), BF16),
        ],
        compiler_params=pltpu.CompilerParams(vmem_limit_bytes=56 << 20),
        name="home_forward",
    )(sample, u, wz[0], wz[1], wout, mix, tokens, gain, router, hot, chooser)


def home_backward_kernel(len_ref, choose_ref, back_ref, h1_ref, gy_ref, gain_ref, wout_ref, z_ref, mix_ref, u_ref, gated_ref,
                         wl_ref, wr_ref,
                         gh_ref, gm_ref, gu_ref, ggain_ref, gwz_ref, gwout_ref, sum_z, sum_out):
    pack = pl.program_id(0)
    steps, model = u_ref.shape

    @pl.when(pack == 0)
    def _():
        ggain_ref[...] = jnp.zeros_like(ggain_ref)
        sum_z[...] = jnp.zeros_like(sum_z)
        sum_out[...] = jnp.zeros_like(sum_out)

    grad = dot(choose_ref[...], back_ref[...], ((0,), (0,)))
    normed, inv = norm_of(h1_ref[...])
    scaled = grad * gain_ref[...]
    ggain_ref[...] += jnp.sum(grad * normed, axis=0, keepdims=True)
    gh = gy_ref[...].astype(F32) + inv * (scaled - normed * jnp.mean(scaled * normed, axis=1, keepdims=True))
    gh_ref[...] = gh
    grad_mixed = (live_rows(len_ref[pack], steps) * gh).astype(BF16)
    grad_u = jnp.zeros((steps, model), F32)
    for half, w_ref in enumerate((wl_ref, wr_ref)):
        here = slice(half * model, (half + 1) * model)
        grad_gated = dot(grad_mixed, wout_ref[here, :], ((1,), (1,)))
        z = z_ref[:, here]
        sig = jax.nn.sigmoid(z)
        gm_ref[:, here] = grad_gated * (z * sig)
        grad_z = (grad_gated * mix_ref[:, here] * sig * (1.0 + z * (1.0 - sig))).astype(BF16)
        grad_u = grad_u + dot(grad_z, w_ref[...], ((1,), (1,)))
        sum_z[:, here] += dot(u_ref[...], grad_z, ((0,), (0,)))
        sum_out[here, :] += dot(gated_ref[:, here], grad_mixed, ((0,), (0,)))
    gu_ref[...] = grad_u

    @pl.when(pack == pl.num_programs(0) - 1)
    def _():
        gwz_ref[...] = sum_z[...].astype(BF16)
        gwout_ref[...] = sum_out[...].astype(BF16)


def home_backward(sample, chooser, back, h1, gy, gain, wout, z, mix, u, gated, wz):
    packs = sample.shape[0]
    rows, model = u.shape
    steps, inner, slots = rows // packs, mix.shape[1], chooser.shape[0]
    fixed = lambda p, lens: (0, 0)
    whole = lambda v: pl.BlockSpec(v.shape, fixed)
    part = lambda n: pl.BlockSpec((steps, n), lambda p, lens: (p, 0))
    return pl.pallas_call(
        home_backward_kernel,
        grid_spec=pltpu.PrefetchScalarGridSpec(
            num_scalar_prefetch=1,
            grid=(packs,),
            in_specs=[
                pl.BlockSpec((slots, steps), lambda p, lens: (0, p)), whole(back), part(model), part(model), whole(gain),
                whole(wout), part(inner), part(inner), part(model), part(inner), whole(wz[0]), whole(wz[1]),
            ],
            out_specs=[
                part(model), part(inner), part(model), whole(gain),
                pl.BlockSpec((model, inner), fixed), pl.BlockSpec((inner, model), fixed),
            ],
            scratch_shapes=[pltpu.VMEM((model, inner), F32), pltpu.VMEM((inner, model), F32)],
        ),
        out_shape=[
            jax.ShapeDtypeStruct((rows, model), F32),
            jax.ShapeDtypeStruct((rows, inner), F32),
            jax.ShapeDtypeStruct((rows, model), F32),
            jax.ShapeDtypeStruct((1, model), F32),
            jax.ShapeDtypeStruct((model, inner), BF16),
            jax.ShapeDtypeStruct((inner, model), BF16),
        ],
        compiler_params=pltpu.CompilerParams(vmem_limit_bytes=60 << 20),
        cost_estimate=pl.CostEstimate(flops=0, bytes_accessed=100_000, transcendentals=0),
        name="home_backward",
    )(sample, chooser, back, h1, gy, gain, wout, z, mix, u, gated, wz[0], wz[1])


def expert_grads_kernel(q_ref, gr_ref, *refs, parts):
    gps, acts, outs = refs[:parts], refs[parts : 2 * parts], refs[2 * parts :]
    for k in range(parts):
        outs[2 * k][...] = dot(q_ref[...], gps[k][...], ((0,), (0,))).astype(BF16)
        outs[2 * k + 1][...] = dot(acts[k][...], gr_ref[...], ((0,), (0,))).astype(BF16)


def expert_grads(q, gr, gps, acts):
    rows, model = q.shape
    hidden, parts = gps[0].shape[1], len(gps)
    block = 256 if hidden % 256 == 0 else 128
    whole = pl.BlockSpec((rows, model), lambda i: (0, 0))
    across = lambda n: pl.BlockSpec((n, block), lambda i: (0, i))
    down = pl.BlockSpec((block, model), lambda i: (i, 0))
    return pl.pallas_call(
        functools.partial(expert_grads_kernel, parts=parts),
        grid=(hidden // block,),
        in_specs=[whole, whole] + [across(rows)] * (2 * parts),
        out_specs=[across(model), down] * parts,
        out_shape=[jax.ShapeDtypeStruct((model, hidden), BF16), jax.ShapeDtypeStruct((hidden, model), BF16)] * parts,
        compiler_params=pltpu.CompilerParams(vmem_limit_bytes=60 << 20),
        cost_estimate=pl.CostEstimate(flops=0, bytes_accessed=100_000, transcendentals=0),
        name="expert_grads",
    )(q, gr, *gps, *acts)


def swap(values, axis, mask):
    count = lax.axis_size(axis)
    return lax.ppermute(values, axis, [(i, i ^ mask) for i in range(count)])


def grow(values, axis, mask, dim):
    got = swap(values, axis, mask)
    upper = (lax.axis_index(axis) & mask) != 0
    return jnp.concatenate([jnp.where(upper, got, values), jnp.where(upper, values, got)], axis=dim)


def gather_stages(width):
    bits = lax.axis_size("fsdp").bit_length() - 1
    place = lambda bit: bits - 1 - bit
    half = width // 2

    def single(bit):
        return lambda values: grow(values, "fsdp", 1 << bit, place(bit))

    def split(values):
        return grow(values[..., :half], "fsdp", 2, place(1)), grow(values[..., half:], "fsdp", 1, place(0))

    def join(pair):
        left, right = grow(pair[0], "fsdp", 1, place(0)), grow(pair[1], "fsdp", 2, place(1))
        return jnp.concatenate([left, right], axis=-1)

    def across(mask):
        return lambda values: grow(values.reshape(1, -1, width), "dp", mask, 0)

    masks = [1 << i for i in range(lax.axis_size("dp").bit_length() - 1)]
    return [single(bit) for bit in range(2, bits)] + [split, join] + [across(mask) for mask in masks]


def gather_both(early, late, lag, beside):
    bits = lax.axis_size("fsdp").bit_length() - 1
    shapes = [(-1, v.shape[1]) for v in (early, late)]
    values = [v.reshape((1,) * bits + v.shape) for v in (early, late)]
    stages = [gather_stages(v.shape[1]) for v in (early, late)]
    count = len(stages[0])
    for at in range(count + lag):
        if lag <= at:
            *values, beside = lax.optimization_barrier((*values, beside))
        if at < count:
            values[0] = stages[0][at](values[0])
        if at >= lag:
            values[1] = stages[1][at - lag](values[1])
    return [v.reshape(shape) for v, shape in zip(values, shapes)] + [beside]


def fold(values, count):
    rows = values.shape[-2] // count
    return jnp.concatenate([values[..., j * rows : (j + 1) * rows, :] for j in range(count)], axis=-1)


def unfold(values, count):
    width = values.shape[-1] // count
    return jnp.concatenate([values[..., j * width : (j + 1) * width] for j in range(count)], axis=-2)


def own_block(values, index, count, axis):
    size = values.shape[axis] // count
    return lax.dynamic_slice_in_dim(values, index * size, size, axis)


def scatter_begin(piece):
    me, groups = lax.axis_index("dp"), lax.axis_size("dp")
    sent = [swap(piece(me ^ k).astype(BF16), "dp", k) for k in range(1, groups)]
    total = piece(me).astype(F32)
    for got in sent:
        total = total + got.astype(F32)
    return total.astype(BF16)


def scatter_end(parts):
    return jnp.sum(lax.all_to_all(parts, "fsdp", 0, 0, tiled=True).astype(F32), axis=0)


def rows_of(left, right, i):
    product = dot(own_block(left, i, lax.axis_size("dp"), 1), right, ((0,), (0,)))
    return product.reshape(lax.axis_size("fsdp"), -1, product.shape[1])


def body(
    tokens,
    cotangent,
    routes,
    lengths,
    norm1_gain,
    input_weight,
    conv_weight,
    conv_bias,
    scan_weight,
    step_weight,
    step_bias,
    decay_log,
    skip_gain,
    out_weight,
    norm2_gain,
    router_weight,
    expert_up,
    expert_down,
):
    micro, steps, model = tokens.shape
    rows = micro * steps
    experts = lax.axis_size("fsdp")
    groups = lax.axis_size("dp")
    devices = experts * groups
    capacity = (5 * steps + 4 * experts - 1) // (4 * experts)
    slots = micro * capacity
    inner = input_weight.shape[1] // 2
    states = decay_log.shape[1]
    rank = step_weight.shape[1]
    taps = conv_weight.shape[1]
    own_model, own_inner = norm1_gain.shape[0], conv_bias.shape[0]

    half = experts // 2
    vectors = jnp.concatenate(
        [
            conv_weight,
            jnp.stack([conv_bias, step_bias, skip_gain, jnp.concatenate([norm1_gain, norm2_gain])]).T,
            decay_log,
            jnp.concatenate([router_weight[:, :half], router_weight[:, half:]], axis=0),
        ],
        axis=1,
    )
    padding = lambda n: jnp.zeros((own_inner, n), BF16)
    small = jnp.concatenate(
        [
            scan_weight,
            padding(LANES - rank - 2 * states),
            step_weight,
            vectors,
            padding(LANES - rank - vectors.shape[1]),
        ],
        axis=1,
    )
    folds = inner // (2 * LANES)
    late = jnp.concatenate([input_weight[:, inner : inner + model], input_weight[:, inner + model :], out_weight], axis=0)
    late = lax.all_gather(late, ("dp", "fsdp"), axis=0, tiled=False)
    input_z = [late[:, i * own_model : (i + 1) * own_model].reshape(model, model) for i in range(2)]
    output_full = late[:, 2 * own_model :].reshape(inner, model)
    ups = [expert_up[0]] + [swap(expert_up[0], "dp", k) for k in range(1, groups)]
    downs = [expert_down[0]] + [swap(expert_down[0], "dp", k) for k in range(1, groups)]

    place = jnp.arange(steps, dtype=jnp.int32)
    sample = lengths[:, 0, 0]
    live = (place[None, :] < sample[:, None]).astype(jnp.int32)
    route = routes[:, :, 0]
    expert_ids = jnp.arange(experts, dtype=jnp.int32)
    route_hot = (route[:, :, None] == expert_ids).astype(BF16)
    live_hot = route_hot * live[:, :, None].astype(BF16)
    earlier = (place[:, None] > place[None, :]).astype(BF16)
    before = lax.dot_general(
        jnp.broadcast_to(earlier, (micro, steps, steps)), live_hot, (((2,), (1,)), ((0,), (0,))),
        preferred_element_type=F32,
    )
    slot = jnp.sum(before * live_hot.astype(F32), axis=2).astype(jnp.int32)
    kept = (live * (slot < capacity).astype(jnp.int32)).reshape(rows)
    target = (route * slots + jnp.arange(micro, dtype=jnp.int32)[:, None] * capacity + slot).reshape(rows)
    chooser = (
        (jnp.arange(experts * slots, dtype=jnp.int32)[:, None] == target[None, :]) & (kept[None, :] == 1)
    ).astype(BF16)
    kept = kept.astype(F32)

    def to_experts(values):
        return lax.all_to_all(values.reshape(experts, slots, -1), "fsdp", 0, 0, tiled=True).reshape(experts * slots, -1)

    def from_experts(values):
        return dot(chooser, values.reshape(experts * slots, -1), ((0,), (0,)))

    def back_home(values):
        return lax.all_to_all(values.reshape(experts, slots, -1), "fsdp", 0, 0, tiled=True)

    cotangent = cotangent.reshape(rows, model)

    hidden = tokens.reshape(rows, model).astype(F32)
    inv_first = lax.rsqrt(jnp.mean(hidden * hidden, axis=-1, keepdims=True) + EPSILON)
    normed_first = hidden * inv_first
    input_x, small_full, upstream_rows = gather_both(
        input_weight[:, :inner], small, 1, dot(chooser, cotangent).astype(BF16)
    )
    upstream_sent = to_experts(upstream_rows)
    select_full, step_full = small_full[:, :LANES], small_full[:, LANES:]
    vectors_full = step_full[:, rank:].T
    vectors_first = vectors_full[:ROWS].astype(F32)
    decay_full = vectors_full[taps + 4 : taps + 4 + states].astype(F32)
    gains = vectors_full[taps + 3].reshape(devices, 2, own_model)
    gain_one = gains[:, 0].reshape(model).astype(F32)
    gain_two = gains[:, 1].reshape(model).astype(F32)
    router_full = vectors_full[taps + 4 + states : taps + 4 + states + half].reshape(half, devices, 2, own_model)
    router_full = router_full.transpose(2, 0, 1, 3).reshape(experts, model)

    normed_low = (normed_first * gain_one).astype(BF16)
    decay_mat = -jnp.exp(decay_full)
    decay_two = decay_mat * LOG2E
    branch_x, scan_in, step_size, selected, mixer_out, states_kept = mixer_forward(
        sample, normed_low, input_x, select_full, step_full, vectors_first, decay_two, micro, rank, taps
    )
    mixer_out, upstream_sent = lax.optimization_barrier((mixer_out, upstream_sent))
    kept_hot = route_hot.reshape(rows, experts).astype(F32) * kept[:, None]
    branch_z, gated_low, residual, weight_row, sent = home_forward(
        sample, normed_low, input_z, output_full, mixer_out, tokens.reshape(rows, model), gain_two[None, :], router_full,
        kept_hot, chooser,
    )
    received = to_experts(sent)

    mine = (expert_ids == lax.axis_index("fsdp")).astype(F32)[None, :]
    result, grad_rows, flat_grad, router_grad, acts, grad_pres = expert_pass(
        received, upstream_sent, router_full, mine, ups, downs
    )
    grad_rows, result, received, flat_grad = lax.optimization_barrier((grad_rows, result, received, flat_grad))
    grad_back = back_home(grad_rows)
    matrix_grads = expert_grads(received, flat_grad, grad_pres, acts)
    grad_back, matrix_grads = lax.optimization_barrier((grad_back, matrix_grads))
    up_own, down_own, *others = matrix_grads
    others = [swap(other, "dp", k // 2 + 1) for k, other in enumerate(others)]

    grad_residual, grad_mixer, grad_normed_z, gain_two_grad, input_z_grad, output_grad = home_backward(
        sample, chooser, grad_back.reshape(experts * slots, model), residual, cotangent, gain_two[None, :], output_full,
        branch_z, mixer_out, normed_low, gated_low, input_z,
    )
    late_terms = jnp.concatenate(
        [
            input_z_grad.reshape(devices, own_model, inner),
            fold(output_grad.reshape(devices, own_inner, model), 2),
        ],
        axis=1,
    ).reshape(-1, inner)
    late_grads = lax.psum_scatter(late_terms, ("dp", "fsdp"), scatter_dimension=0, tiled=True)
    grad_mixer, result, others = lax.optimization_barrier((grad_mixer, result, others))
    result = back_home(result)
    grad_x, select_grad, step_grad, gain_one_grad, tokens_grad = mixer_backward(
        sample, step_size, scan_in, branch_x, grad_mixer, selected, select_full, step_full, vectors_first, decay_two,
        states_kept, input_x, tokens.reshape(rows, model), gain_one[None, :], grad_normed_z, grad_residual,
        micro, rank, taps,
    )
    grad_x, result = lax.optimization_barrier((grad_x, result))

    gain_grads = jnp.concatenate(
        [gain_one_grad.reshape(devices, 1, own_model), gain_two_grad.reshape(devices, 1, own_model)], axis=1
    ).reshape(inner, 1)
    router_grads = (
        router_grad.reshape(2, half, devices, own_model).transpose(2, 0, 3, 1).reshape(inner, half)
    )
    at_gain, at_decay, at_router = rank + taps + 3, rank + taps + 4, rank + taps + 4 + states
    lane = jnp.arange(LANES)
    step_grad = jnp.where(lane == at_gain, gain_grads, step_grad) + jnp.pad(
        router_grads, ((0, 0), (at_router, LANES - at_router - half))
    )

    def early_terms(i):
        blocks = [own_block(v, i, groups, 0).reshape(experts, own_inner, LANES) for v in (select_grad, step_grad)]
        return jnp.concatenate([rows_of(normed_low, grad_x, i), fold(jnp.concatenate(blocks, axis=2), folds)], axis=1)

    early_parts, others, result = lax.optimization_barrier((scatter_begin(early_terms), others, result))
    early_grads = scatter_end(early_parts)
    up_grad, down_grad = up_own.astype(F32), down_own.astype(F32)
    for k in range(groups - 1):
        up_grad = up_grad + others[2 * k].astype(F32)
        down_grad = down_grad + others[2 * k + 1].astype(F32)
    late_grads = late_grads.astype(F32)
    block_output = (residual + weight_row * from_experts(result)).astype(BF16)
    small_grads = unfold(early_grads[own_model:], folds)
    vector_grads = small_grads[:, LANES:]
    routers = vector_grads[:, at_router : at_router + half]
    return (
        block_output.reshape(micro, steps, model),
        tokens_grad.reshape(micro, steps, model),
        vector_grads[:own_model, at_gain],
        jnp.concatenate([early_grads[:own_model], late_grads[:own_model]], axis=1),
        vector_grads[:, rank : rank + taps],
        vector_grads[:, rank + taps],
        small_grads[:, : rank + 2 * states],
        vector_grads[:, :rank],
        vector_grads[:, rank + taps + 1],
        vector_grads[:, at_decay : at_decay + states],
        vector_grads[:, rank + taps + 2],
        unfold(late_grads[own_model:], 2),
        vector_grads[own_model:, at_gain],
        jnp.concatenate([routers[:own_model], routers[own_model:]], axis=1),
        up_grad[None],
        down_grad[None],
    )


def solution(mesh):
    rows3 = P(None, ("dp", "fsdp"), None)
    vector = P(("dp", "fsdp"))
    matrix = P(("dp", "fsdp"), None)
    weights = (
        vector, matrix, matrix, vector, matrix, matrix, vector, matrix, vector, matrix, vector, matrix,
        P("fsdp", None, "dp"), P("fsdp", "dp", None),
    )
    return jax.shard_map(
        body,
        mesh=mesh,
        in_specs=(rows3, rows3, rows3, rows3) + weights,
        out_specs=(rows3, rows3) + weights,
        check_vma=False,
    )
```

```python
import functools

import jax
import jax.numpy as jnp
from jax import lax
from jax.experimental import pallas as pl
from jax.experimental.pallas import tpu as pltpu
from jax.sharding import PartitionSpec as P

EPSILON = 1e-05
LOG2E = 1.4426950408889634
LN2 = 0.6931471805599453
LANES = 128
ROWS = 8
F32 = jnp.float32
BF16 = jnp.bfloat16


def dot(left, right, dims=((1,), (0,))):
    return lax.dot_general(left, right, (dims, ((), ())), preferred_element_type=F32)


def fold_rows(parts):
    place = lax.broadcasted_iota(jnp.int32, parts[0].shape, 0)
    half = 1
    while half < ROWS:
        lower = (place & half) == 0
        merged = []
        for i in range(0, len(parts), 2):
            a, b = parts[i], parts[i + 1]
            merged.append(jnp.where(lower, a, b) + pltpu.roll(jnp.where(lower, b, a), half, 0))
        parts = merged
        half *= 2
    return parts[0]


def sum_states(parts):
    halves = []
    for p in parts:
        total = p[:ROWS]
        for i in range(1, p.shape[0] // ROWS):
            total = total + p[i * ROWS : (i + 1) * ROWS]
        halves.append(total)
    return fold_rows(halves)


def lane_chunk(k, count=1):
    return pl.ds(pl.multiple_of(k * LANES * count, LANES), LANES * count)


def split_low(values):
    high = values.astype(BF16)
    return high, (values - high.astype(F32)).astype(BF16)


def own_lanes(first, states, size):
    lane = lax.broadcasted_iota(jnp.int32, (size, states, LANES), 2)
    row = lax.broadcasted_iota(jnp.int32, (size, states, LANES), 1)
    return (lane == row + first) | (lane == row + first + states)


def widen(selected, first, states, bw, cw):
    steps = selected.shape[0]
    lane = lax.broadcasted_iota(jnp.int32, (2 * LANES, 2 * LANES), 0) % LANES
    to_c = lax.broadcasted_iota(jnp.int32, (2 * LANES, 2 * LANES), 1) >= LANES
    spread = (to_c == (lane >= first + states)).astype(BF16)
    size = 64
    own = own_lanes(first, states, size)
    for at in range(0, steps, size):
        rows = jnp.where(own, selected[at : at + size][:, None, :], 0.0).reshape(size * states, LANES)
        wide = dot(jnp.concatenate(split_low(rows), axis=1), spread)
        bw[at * states : (at + size) * states, :] = wide[:, :LANES]
        cw[at * states : (at + size) * states, :] = wide[:, LANES:]


def narrow(gb, gc, first, states, steps):
    lane = lax.broadcasted_iota(jnp.int32, (2 * LANES, LANES), 1)
    from_c = lax.broadcasted_iota(jnp.int32, (2 * LANES, LANES), 0) >= LANES
    gather = (from_c == (lane >= first + states)).astype(BF16)
    size = 64
    own = own_lanes(first, states, size)
    out = []
    for at in range(0, steps, size):
        here = slice(at * states, (at + size) * states)
        rows = jnp.concatenate([gb[here, :].astype(BF16), gc[here, :].astype(BF16)], axis=1)
        sums = dot(rows, gather).reshape(size, states, LANES)
        out.append(jnp.sum(jnp.where(own, sums, 0.0), axis=1))
    return jnp.concatenate(out, axis=0)


def conv_of(x_ref, vec_ref, lanes, taps, steps):
    total = vec_ref[taps : taps + 1, lanes]
    for shift in range(taps):
        total = total + vec_ref[taps - 1 - shift : taps - shift, lanes] * x_ref[ROWS - shift : ROWS - shift + steps, lanes]
    return total


def lane_halves(small):
    return [pl.BlockSpec((small.shape[0], LANES), lambda p, lens, half=half: (0, half)) for half in range(2)]


def forward_kernel(len_ref, u_ref, wx_ref, sela_ref, stepb_ref, vec_ref, a_ref,
                   bx_ref, xs_ref, delta_ref, sel_ref, mix_ref, h_ref,
                   state, bw, cw, low, *, group, rank, taps):
    states, width = a_ref.shape
    steps = u_ref.shape[0]
    chunks = width // LANES
    bias_step, skip = taps + 1, taps + 2
    state[...] = jnp.zeros_like(state)
    bx_ref[:ROWS, :] = jnp.zeros((ROWS, width), F32)

    def project(k, _):
        lanes = lane_chunk(k, 2)
        bx_ref[ROWS:, lanes] = dot(u_ref[...], wx_ref[:, lanes])
        return 0

    lax.fori_loop(0, chunks // 2, project, 0, unroll=True)

    def convolve(k, _):
        lanes = lane_chunk(k)
        conv = conv_of(bx_ref, vec_ref, lanes, taps, steps)
        xs = conv * jax.nn.sigmoid(conv)
        xs_ref[:, lanes] = xs
        low[:, lanes] = xs.astype(BF16)
        return 0

    lax.fori_loop(0, chunks, convolve, 0, unroll=2)
    selected = dot(low[...], sela_ref[...])
    sel_ref[...] = selected
    lane = lax.broadcasted_iota(jnp.int32, selected.shape, 1)
    rank_low = jnp.where(lane < rank, selected, 0.0).astype(BF16)
    widen(selected, rank, states, bw, cw)

    def sizes(k, _):
        lanes = lane_chunk(k, 2)
        pre = dot(rank_low, stepb_ref[lanes, :], ((1,), (1,))) + vec_ref[bias_step : bias_step + 1, lanes]
        delta_ref[:, lanes] = jnp.maximum(pre, 0.0) + jnp.log1p(jnp.exp(-jnp.abs(pre)))
        return 0

    lax.fori_loop(0, chunks // 2, sizes, 0, unroll=2)

    def rows(s, _):
        at = pl.multiple_of(s * ROWS, ROWS)

        def chunk(g, _):
            for u in range(group):
                lanes = lane_chunk(g * group + u)
                d = delta_ref[pl.ds(at, ROWS), lanes]
                x = xs_ref[pl.ds(at, ROWS), lanes]
                dx = d * x
                a = a_ref[:, lanes]
                h = state[:, lanes]
                h_ref[s, :, lanes] = h
                parts = []
                for t in range(ROWS):
                    here = pl.ds(pl.multiple_of((at + t) * states, states), states)
                    h = jnp.exp2(d[t : t + 1] * a) * h + bw[here, :] * dx[t : t + 1]
                    parts.append(cw[here, :] * h)
                state[:, lanes] = h
                mix_ref[pl.ds(at, ROWS), lanes] = sum_states(parts) + vec_ref[skip : skip + 1, lanes] * x
            return 0

        lax.fori_loop(0, chunks // group, chunk, 0)
        return 0

    used = (len_ref[pl.program_id(0)] + ROWS - 1) // ROWS
    lax.fori_loop(0, used, rows, 0)

    def clear(s, _):
        mix_ref[pl.ds(pl.multiple_of(s * ROWS, ROWS), ROWS), :] = jnp.zeros((ROWS, width), F32)
        return 0

    lax.fori_loop(used, steps // ROWS, clear, 0)


def mixer_forward(sample, u, wx, small, vec, a2, packs, rank, taps, group=12):
    rows, model = u.shape
    steps = rows // packs
    states, width = a2.shape
    per_pack = lambda p, lens: (p, 0)
    whole = lambda v: pl.BlockSpec(v.shape, lambda p, lens: (0, 0))
    mats = pl.BlockSpec((steps, width), per_pack)
    return pl.pallas_call(
        functools.partial(forward_kernel, group=group, rank=rank, taps=taps),
        grid_spec=pltpu.PrefetchScalarGridSpec(
            num_scalar_prefetch=1,
            grid=(packs,),
            in_specs=[pl.BlockSpec((steps, model), per_pack), whole(wx), *lane_halves(small), whole(vec), whole(a2)],
            out_specs=[
                pl.BlockSpec((steps + ROWS, width), per_pack),
                mats,
                mats,
                pl.BlockSpec((steps, LANES), per_pack),
                mats,
                pl.BlockSpec((steps // ROWS, states, width), lambda p, lens: (p, 0, 0)),
            ],
            scratch_shapes=[
                pltpu.VMEM((states, width), F32),
                pltpu.VMEM((steps * states, LANES), F32),
                pltpu.VMEM((steps * states, LANES), F32),
                pltpu.VMEM((steps, width), BF16),
            ],
        ),
        out_shape=[
            jax.ShapeDtypeStruct((rows + packs * ROWS, width), F32),
            jax.ShapeDtypeStruct((rows, width), F32),
            jax.ShapeDtypeStruct((rows, width), F32),
            jax.ShapeDtypeStruct((rows, LANES), F32),
            jax.ShapeDtypeStruct((rows, width), F32),
            jax.ShapeDtypeStruct((rows // ROWS, states, width), F32),
        ],
        compiler_params=pltpu.CompilerParams(vmem_limit_bytes=56 << 20),
        cost_estimate=pl.CostEstimate(flops=0, bytes_accessed=120_000_000, transcendentals=0),
        name="mixer_forward",
    )(sample, u, wx, small, small, vec, a2)


def step_slopes(d):
    small = d < 0.01
    slope = 1.0 - d * (0.5 - d * (1.0 / 6.0))
    rise = 1.0 - jnp.exp(-d)
    return jnp.where(small, d * slope, rise), jnp.where(small, slope, rise / jnp.where(small, 1.0, d))


def backward_kernel(len_ref, delta_ref, xs_ref, bx_ref, gm_ref, sel_ref, sela_ref, stepb_ref, vec_ref, a_ref, h_ref,
                    wx_ref, x_ref, gain_ref, gu_ref, gh_ref, u_ref, extra_ref, second_ref, *refs,
                    group, rank, taps, at_gain, own, groups):
    if own:
        outs, refs = refs[:groups], refs[groups:]
        gtok_ref, gxw_ref, gsel_ref, gstep_ref, ggain_ref = refs[:5]
    else:
        gtok_ref, gxw_ref, gsel_ref, gstep_ref, ggain_ref = refs[:5]
    mu_s, bw, cw, gb, gc, gd, gxs, low, gx_ref, gvec_ref, ga_ref, tile = refs[-12:]
    pack = pl.program_id(0)
    states, width = a_ref.shape
    steps = sel_ref.shape[0]
    chunks = width // LANES
    bias_conv, bias_step, skip = taps, taps + 1, taps + 2

    @pl.when(pack == 0)
    def _():
        ga_ref[...] = jnp.zeros_like(ga_ref)
        gsel_ref[...] = jnp.zeros_like(gsel_ref)
        gstep_ref[...] = extra_ref[...]
        gxw_ref[...] = jnp.zeros_like(gxw_ref)
        gvec_ref[...] = jnp.zeros_like(gvec_ref)
        ggain_ref[...] = jnp.zeros_like(ggain_ref)

    mu_s[...] = jnp.zeros_like(mu_s)
    gb[...] = jnp.zeros_like(gb)
    gc[...] = jnp.zeros_like(gc)
    selected = sel_ref[...]
    widen(selected, rank, states, bw, cw)
    used = (len_ref[pack] + ROWS - 1) // ROWS

    def clear(s, _):
        here = pl.ds(pl.multiple_of(s * ROWS, ROWS), ROWS)
        gd[here, :] = jnp.zeros((ROWS, width), F32)
        gxs[here, :] = jnp.zeros((ROWS, width), F32)
        return 0

    lax.fori_loop(used, steps // ROWS, clear, 0)

    def rows(back, _):
        s = used - 1 - back
        at = pl.multiple_of(s * ROWS, ROWS)
        place = [pl.ds(pl.multiple_of((at + t) * states, states), states) for t in range(ROWS)]

        def chunk(g, _):
            each = []
            for u in range(group):
                lanes = lane_chunk(g * group + u)
                d = delta_ref[pl.ds(at, ROWS), lanes]
                x = xs_ref[pl.ds(at, ROWS), lanes]
                a = a_ref[:, lanes]
                dx = d * x
                tile[3 * u] = d
                tile[3 * u + 1] = dx
                tile[3 * u + 2] = gm_ref[pl.ds(at, ROWS), lanes]
                h, power, decay = [h_ref[s, :, lanes]], [], []
                for t in range(ROWS):
                    power.append(tile[3 * u, t : t + 1, :] * a)
                    decay.append(jnp.exp2(power[t]))
                    h.append(decay[t] * h[t] + bw[place[t], :] * tile[3 * u + 1, t : t + 1, :])
                each.append(dict(lanes=lanes, d=d, x=x, mu=mu_s[:, lanes], h=h, power=power, decay=decay,
                                 ga=ga_ref[:, lanes], sp=[None] * ROWS, gp=[None] * ROWS))
            for t in range(ROWS - 1, -1, -1):
                b, c = bw[place[t], :], cw[place[t], :]
                one_b = one_c = None
                for u, v in enumerate(each):
                    gyt = tile[3 * u + 2, t : t + 1, :]
                    lam = c * gyt + v["mu"]
                    v["sp"][t] = b * lam
                    to_b = lam * tile[3 * u + 1, t : t + 1, :]
                    to_c = v["h"][t + 1] * gyt
                    one_b = to_b if one_b is None else one_b + to_b
                    one_c = to_c if one_c is None else one_c + to_c
                    v["mu"] = v["decay"][t] * lam
                    v["gp"][t] = v["mu"] * v["h"][t] * v["power"][t]
                    v["ga"] = v["ga"] + v["gp"][t]
                gb[place[t], :] += one_b
                gc[place[t], :] += one_c
            for v in each:
                lanes = v["lanes"]
                mu_s[:, lanes], ga_ref[:, lanes] = v["mu"], v["ga"]
                total = sum_states(v["sp"])
                rise, slope = step_slopes(v["d"])
                gd[pl.ds(at, ROWS), lanes] = sum_states(v["gp"]) * (slope * LN2) + v["x"] * total * rise
                gxs[pl.ds(at, ROWS), lanes] = v["d"] * total
            return 0

        lax.fori_loop(0, chunks // group, chunk, 0)
        return 0

    lax.fori_loop(0, used, rows, 0)

    def add_row(row, lanes, values):
        gvec_ref[row : row + 1, lanes] += jnp.sum(values, axis=0, keepdims=True)

    def sizes(k, _):
        lanes = lane_chunk(k)
        grad = gd[:steps, lanes]
        add_row(bias_step, lanes, grad)
        low[:, lanes] = grad.astype(BF16)
        add_row(skip, lanes, gm_ref[:, lanes] * xs_ref[:, lanes])
        return 0

    lax.fori_loop(0, chunks, sizes, 0, unroll=2)
    gd[steps:, :] = jnp.zeros((ROWS, width), F32)
    lane = lax.broadcasted_iota(jnp.int32, selected.shape, 1)
    rank_low = jnp.where(lane < rank, selected, 0.0).astype(BF16)
    grad_rank = dot(low[...], stepb_ref[...])
    gstep_ref[...] += dot(low[...], rank_low, ((0,), (0,)))
    grad_sel = jnp.where(lane < rank, grad_rank, narrow(gb, gc, rank, states, steps)).astype(BF16)

    def values(k, _):
        lanes = lane_chunk(k)
        conv = conv_of(bx_ref, vec_ref, lanes, taps, steps)
        sig = jax.nn.sigmoid(conv)
        low[:, lanes] = (conv * sig).astype(BF16)
        grad = dot(grad_sel, sela_ref[lanes, :], ((1,), (1,)))
        grad = grad + gxs[:, lanes] + gm_ref[:, lanes] * vec_ref[skip : skip + 1, lanes]
        grad = grad * (sig * (1.0 + conv * (1.0 - sig)))
        gd[:steps, lanes] = grad
        add_row(bias_conv, lanes, grad)
        back_x = None
        for j in range(taps):
            shift = taps - 1 - j
            add_row(j, lanes, grad * bx_ref[ROWS - shift : ROWS - shift + steps, lanes])
            term = vec_ref[j : j + 1, lanes] * gd[shift : shift + steps, lanes]
            back_x = term if back_x is None else back_x + term
        gx_ref[:, lanes] = back_x.astype(BF16)
        return 0

    lax.fori_loop(0, chunks, values, 0, unroll=2)
    gsel_ref[...] += dot(low[...], grad_sel, ((0,), (0,)))

    def product(k, _):
        lanes = lane_chunk(k, 4)
        gxw_ref[:, lanes] += dot(u_ref[...], gx_ref[:, lanes], ((0,), (0,)))
        return 0

    lax.fori_loop(0, chunks // 4, product, 0, unroll=True)
    hidden = x_ref[...].astype(F32)
    inv = lax.rsqrt(jnp.mean(hidden * hidden, axis=1, keepdims=True) + EPSILON)
    normed = hidden * inv
    grad_u = dot(gx_ref[...], wx_ref[...], ((1,), (1,))) + gu_ref[...]
    scaled = grad_u * gain_ref[...]
    if own:
        ones = jnp.ones((steps, LANES), BF16)
        high, rest = split_low(grad_u * normed)
        ggain_ref[...] += dot(high, ones, ((0,), (0,))) + dot(rest, ones, ((0,), (0,)))
    else:
        ggain_ref[...] += jnp.sum(grad_u * normed, axis=0, keepdims=True)
    gtok_ref[...] = gh_ref[...] + inv * (scaled - normed * jnp.mean(scaled * normed, axis=1, keepdims=True))

    @pl.when(pack == pl.num_programs(0) - 1)
    def _():
        rows_of_vectors = jnp.concatenate([gvec_ref[...], ga_ref[...] * LN2], axis=0)
        before = jnp.zeros((rank, width), F32)
        after = jnp.zeros((LANES - rank - rows_of_vectors.shape[0], width), F32)
        gstep_ref[...] += jnp.concatenate([before, rows_of_vectors, after], axis=0).T
        if own:
            lane = lax.broadcasted_iota(jnp.int32, (own, LANES), 1)
            folds = width // (2 * LANES)
            run = 2 * own // folds

            size = own + run
            count = width // (2 * own) // groups

            def gather(slot, f):
                i = (len_ref[pl.num_programs(0)] ^ slot) * count + f
                mine = pl.ds(pl.multiple_of(own * i, ROWS), own)
                for part, ref in enumerate((ggain_ref, second_ref)):
                    here = pl.ds(pl.multiple_of(2 * own * i + own * part, ROWS), own)
                    gstep_ref[here, :] += jnp.where(lane == at_gain, ref[mine, :], 0.0)
                parts = []
                for j in range(folds):
                    here = pl.ds(pl.multiple_of(2 * own * i + run * j, ROWS), run)
                    parts += [gsel_ref[here, :], gstep_ref[here, :]]
                block = jnp.concatenate([gxw_ref[mine, :], jnp.concatenate(parts, axis=1)], axis=0)
                outs[slot][pl.ds(pl.multiple_of(size * f, size), size), :] = block.astype(BF16)
                return 0

            for slot in range(groups):
                lax.fori_loop(0, count, lambda f, _, slot=slot: gather(slot, f), 0)


def whole_tiles(own, width):
    return own % ROWS == 0 and 4 * own * LANES % (ROWS * width) == 0


def mixer_backward(sample, delta, xs, bx, gm, sel, small, vec, a2, hall, wx, tokens, gain, grad_u, grad_h, u, extra, second,
                   packs, rank, taps, at_gain, own, groups, group=3):
    rows, width = delta.shape
    steps = rows // packs
    states, model = a2.shape[0], tokens.shape[1]
    per_pack = lambda p, lens: (p, 0)
    fixed = lambda p, lens: (0, 0)
    whole = lambda v: pl.BlockSpec(v.shape, fixed)
    mats = pl.BlockSpec((steps, width), per_pack)
    toks = pl.BlockSpec((steps, model), per_pack)
    own = own if whole_tiles(own, width) else 0
    sums = [(model, width), (width, LANES), (width, LANES), (model, LANES) if own else (1, model)]
    size = own + 4 * own * LANES // width
    outs = [jax.ShapeDtypeStruct((rows, model), F32)]
    out_specs = [toks]
    scratch = [
        pltpu.VMEM((states, width), F32),
        pltpu.VMEM((steps * states, LANES), F32),
        pltpu.VMEM((steps * states, LANES), F32),
        pltpu.VMEM((steps * states, LANES), F32),
        pltpu.VMEM((steps * states, LANES), F32),
        pltpu.VMEM((steps + ROWS, width), F32),
        pltpu.VMEM((steps, width), F32),
        pltpu.VMEM((steps, width), BF16),
        pltpu.VMEM((steps, width), BF16),
        pltpu.VMEM((ROWS, width), F32),
        pltpu.VMEM((states, width), F32),
        pltpu.VMEM((3 * group, ROWS, LANES), F32),
    ]
    if own:
        outs = [jax.ShapeDtypeStruct((model // own // groups * size, width), BF16)] * groups + outs
        out_specs = [pl.BlockSpec(outs[0].shape, fixed)] * groups + out_specs
        scratch = [pltpu.VMEM(shape, F32) for shape in sums] + scratch
    else:
        outs += [jax.ShapeDtypeStruct(shape, F32) for shape in sums]
        out_specs += [pl.BlockSpec(shape, fixed) for shape in sums]
    return pl.pallas_call(
        functools.partial(backward_kernel, group=group, rank=rank, taps=taps, at_gain=at_gain, own=own, groups=groups),
        grid_spec=pltpu.PrefetchScalarGridSpec(
            num_scalar_prefetch=1,
            grid=(packs,),
            in_specs=[
                mats, mats,
                pl.BlockSpec((steps + ROWS, width), per_pack),
                mats,
                pl.BlockSpec((steps, LANES), per_pack),
                *lane_halves(small), whole(vec), whole(a2),
                pl.BlockSpec((steps // ROWS, states, width), lambda p, lens: (p, 0, 0)),
                whole(wx), toks, whole(gain), toks, toks, toks, whole(extra), whole(second),
            ],
            out_specs=out_specs,
            scratch_shapes=scratch,
        ),
        out_shape=outs,
        compiler_params=pltpu.CompilerParams(vmem_limit_bytes=62 << 20),
        cost_estimate=pl.CostEstimate(flops=0, bytes_accessed=100_000, transcendentals=0),
        name="mixer_backward",
    )(sample, delta, xs, bx, gm, sel, small, small, vec, a2, hall, wx, tokens, gain, grad_u, grad_h, u, extra, second)


def expert_kernel(*refs, parts):
    q_ref, gy_ref, router_ref, mine_ref = refs[:4]
    ups, downs = refs[4 : 4 + parts], refs[4 + parts : 4 + 2 * parts]
    outs = refs[4 + 2 * parts :]
    result_ref, gq_ref, gr_ref, grouter_ref = outs[:4]
    acts, grads = outs[4 : 4 + parts], outs[4 + parts : 4 + 2 * parts]
    total, back, gates = outs[4 + 2 * parts :]
    step = pl.program_id(0)

    @pl.when(step == 0)
    def _():
        logits = dot(q_ref[...], router_ref[...], ((1,), (1,)))
        odds = jnp.exp(logits - jnp.max(logits, axis=1, keepdims=True))
        probs = odds / jnp.sum(odds, axis=1, keepdims=True)
        gate = jnp.sum(probs * mine_ref[...], axis=1, keepdims=True)
        gates[...] = gate * (mine_ref[...] - probs)
        gr_ref[...] = (gate * gy_ref[...].astype(F32)).astype(BF16)
        total[...] = jnp.zeros_like(total)
        back[...] = jnp.zeros_like(back)

    q, gr = q_ref[...], gr_ref[...]
    root = 0.7978845608028654
    pres = [dot(q, up[...]) for up in ups]
    grad_acts = [dot(gr, down[...], ((1,), (1,))) for down in downs]
    for k, (pre, grad_act) in enumerate(zip(pres, grad_acts)):
        square = pre * pre
        t = jnp.tanh(root * pre * (1.0 + 0.044715 * square))
        half = 0.5 * (1.0 + t)
        act = (pre * half).astype(BF16)
        slope = half + (0.5 * root) * pre * (1.0 - t * t) * (1.0 + 0.134145 * square)
        grad = (grad_act * slope).astype(BF16)
        acts[k][...] = act
        grads[k][...] = grad
        total[...] += dot(act, downs[k][...])
        back[...] += dot(grad, ups[k][...], ((1,), (1,)))

    @pl.when(step == pl.num_programs(0) - 1)
    def _():
        result = total[...].astype(BF16)
        result_ref[...] = result
        grad_gate = jnp.sum(gy_ref[...].astype(F32) * result.astype(F32), axis=1, keepdims=True)
        grad_logits = (grad_gate * gates[...]).astype(BF16)
        grouter_ref[...] = dot(grad_logits, q_ref[...], ((0,), (0,)))
        gq_ref[...] = (dot(grad_logits, router_ref[...]) + back[...]).astype(BF16)


def expert_pass(q, gy, router, mine, ups, downs):
    rows, model = q.shape
    experts = router.shape[0]
    parts = len(ups)
    hidden = ups[0].shape[1]
    block = 256 if hidden % 256 == 0 else 128
    fixed = lambda i: (0, 0)
    whole = lambda shape: pl.BlockSpec(shape, fixed)
    across = lambda n: pl.BlockSpec((n, block), lambda i: (0, i))
    down = pl.BlockSpec((block, model), lambda i: (i, 0))
    outs = pl.pallas_call(
        functools.partial(expert_kernel, parts=parts),
        grid=(hidden // block,),
        in_specs=[whole(q.shape), whole(gy.shape), whole(router.shape), whole(mine.shape)]
        + [across(model)] * parts
        + [down] * parts,
        out_specs=[whole((rows, model))] * 3 + [whole((experts, model))] + [across(rows)] * (2 * parts),
        out_shape=[jax.ShapeDtypeStruct((rows, model), BF16)] * 3
        + [jax.ShapeDtypeStruct((experts, model), F32)]
        + [jax.ShapeDtypeStruct((rows, hidden), BF16)] * (2 * parts),
        scratch_shapes=[pltpu.VMEM((rows, model), F32), pltpu.VMEM((rows, model), F32), pltpu.VMEM((rows, experts), F32)],
        compiler_params=pltpu.CompilerParams(vmem_limit_bytes=56 << 20),
        cost_estimate=pl.CostEstimate(flops=0, bytes_accessed=70_000_000, transcendentals=0),
        name="expert_pass",
    )(q, gy, router, mine, *ups, *downs)
    return (*outs[:4], outs[4 : 4 + parts], outs[4 + parts :])
def rows_from(ref, here):
    if len(ref.shape) == 2:
        return ref[here, :]
    run = ref.shape[1]
    return ref[here.start // run : here.stop // run].reshape(here.stop - here.start, ref.shape[2])


def late_out(late, own):
    devices, count, model = late.shape
    if own % 16 == 0:
        return late, pl.BlockSpec((devices, own, model), lambda p, lens: (0, 1, 0))
    out = late[:, count - own :].reshape(devices * own, model)
    return out, pl.BlockSpec(out.shape, lambda p, lens: (0, 0))


def live_rows(length, steps):
    return (lax.broadcasted_iota(jnp.int32, (steps, 1), 0) < length).astype(F32)


def norm_of(values):
    inv = lax.rsqrt(jnp.mean(values * values, axis=1, keepdims=True) + EPSILON)
    return values * inv, inv


def home_forward_kernel(len_ref, u_ref, wl_ref, wr_ref, wout_ref, mix_ref, x_ref, gain_ref, router_ref, hot_ref, choose_ref,
                        z_ref, gated_ref, h1_ref, weight_ref, sent_ref, total):
    pack = pl.program_id(0)
    steps, model = u_ref.shape
    mixed = jnp.zeros((steps, model), F32)
    for half, w_ref in enumerate((wl_ref, wr_ref)):
        here = slice(half * model, (half + 1) * model)
        z = dot(u_ref[...], w_ref[...])
        z_ref[:, here] = z
        gated = (mix_ref[:, here] * (z * jax.nn.sigmoid(z))).astype(BF16)
        gated_ref[:, here] = gated
        mixed = mixed + dot(gated, rows_from(wout_ref, here))
    h1 = x_ref[...].astype(F32) + live_rows(len_ref[pack], steps) * mixed
    h1_ref[...] = h1
    routed = (norm_of(h1)[0] * gain_ref[...]).astype(BF16)
    logits = dot(routed, router_ref[...], ((1,), (1,)))
    odds = jnp.exp(logits - jnp.max(logits, axis=1, keepdims=True))
    probs = odds / jnp.sum(odds, axis=1, keepdims=True)
    weight_ref[...] = jnp.sum(probs * hot_ref[...], axis=1, keepdims=True)
    sent = dot(choose_ref[...], routed)

    @pl.when(pack == 0)
    def _():
        total[...] = sent

    @pl.when(pack > 0)
    def _():
        total[...] += sent

    @pl.when(pack == pl.num_programs(0) - 1)
    def _():
        sent_ref[...] = total[...].astype(BF16)


def home_forward(sample, u, wz, late, own, mix, tokens, gain, router, hot, chooser):
    wout, wout_spec = late_out(late, own)
    packs = sample.shape[0]
    rows, model = u.shape
    steps, inner, slots = rows // packs, mix.shape[1], chooser.shape[0]
    whole = lambda v: pl.BlockSpec(v.shape, lambda p, lens: (0, 0))
    part = lambda n: pl.BlockSpec((steps, n), lambda p, lens: (p, 0))
    return pl.pallas_call(
        home_forward_kernel,
        grid_spec=pltpu.PrefetchScalarGridSpec(
            num_scalar_prefetch=1,
            grid=(packs,),
            in_specs=[
                part(model), whole(wz[0]), whole(wz[1]), wout_spec, part(inner), part(model), whole(gain), whole(router),
                part(hot.shape[1]), pl.BlockSpec((slots, steps), lambda p, lens: (0, p)),
            ],
            out_specs=[
                part(inner), part(inner), part(model), part(1), pl.BlockSpec((slots, model), lambda p, lens: (0, 0)),
            ],
            scratch_shapes=[pltpu.VMEM((slots, model), F32)],
        ),
        out_shape=[
            jax.ShapeDtypeStruct((rows, inner), F32),
            jax.ShapeDtypeStruct((rows, inner), BF16),
            jax.ShapeDtypeStruct((rows, model), F32),
            jax.ShapeDtypeStruct((rows, 1), F32),
            jax.ShapeDtypeStruct((slots, model), BF16),
        ],
        compiler_params=pltpu.CompilerParams(vmem_limit_bytes=56 << 20),
        name="home_forward",
    )(sample, u, wz[0], wz[1], wout, mix, tokens, gain, router, hot, chooser)


def home_backward_kernel(len_ref, choose_ref, back_ref, h1_ref, gy_ref, gain_ref, wout_ref, z_ref, mix_ref, u_ref, gated_ref,
                         wl_ref, wr_ref,
                         gh_ref, gm_ref, gu_ref, ggain_ref, *refs, own):
    *outs, sum_z, sum_out = refs
    pack = pl.program_id(0)
    steps, model = u_ref.shape

    @pl.when(pack == 0)
    def _():
        ggain_ref[...] = jnp.zeros_like(ggain_ref)
        sum_z[...] = jnp.zeros_like(sum_z)
        sum_out[...] = jnp.zeros_like(sum_out)

    grad = dot(choose_ref[...], back_ref[...], ((0,), (0,)))
    normed, inv = norm_of(h1_ref[...])
    scaled = grad * gain_ref[...]
    if len(outs) == 1:
        ones = jnp.ones((steps, LANES), BF16)
        high, rest = split_low(grad * normed)
        ggain_ref[...] += dot(high, ones, ((0,), (0,))) + dot(rest, ones, ((0,), (0,)))
    else:
        ggain_ref[...] += jnp.sum(grad * normed, axis=0, keepdims=True)
    gh = gy_ref[...].astype(F32) + inv * (scaled - normed * jnp.mean(scaled * normed, axis=1, keepdims=True))
    gh_ref[...] = gh
    grad_mixed = (live_rows(len_ref[pack], steps) * gh).astype(BF16)
    grad_u = jnp.zeros((steps, model), F32)
    for half, w_ref in enumerate((wl_ref, wr_ref)):
        here = slice(half * model, (half + 1) * model)
        grad_gated = dot(grad_mixed, rows_from(wout_ref, here), ((1,), (1,)))
        z = z_ref[:, here]
        sig = jax.nn.sigmoid(z)
        gm_ref[:, here] = grad_gated * (z * sig)
        grad_z = (grad_gated * mix_ref[:, here] * sig * (1.0 + z * (1.0 - sig))).astype(BF16)
        grad_u = grad_u + dot(grad_z, w_ref[...], ((1,), (1,)))
        sum_z[:, here] += dot(u_ref[...], grad_z, ((0,), (0,)))
        sum_out[here, :] += dot(gated_ref[:, here], grad_mixed, ((0,), (0,)))
    gu_ref[...] = grad_u

    @pl.when(pack == pl.num_programs(0) - 1)
    def _():
        if len(outs) == 2:
            outs[0][...] = sum_z[...].astype(BF16)
            outs[1][...] = sum_out[...].astype(BF16)
            return

        def gather(i, _):
            mine = pl.ds(pl.multiple_of(own * i, ROWS), own)
            left = pl.ds(pl.multiple_of(2 * own * i, ROWS), own)
            right = pl.ds(pl.multiple_of(2 * own * i + own, ROWS), own)
            block = jnp.concatenate(
                [sum_z[mine, :], jnp.concatenate([sum_out[left, :], sum_out[right, :]], axis=1)], axis=0
            )
            outs[0][pl.ds(pl.multiple_of(2 * own * i, 2 * own), 2 * own), :] = block.astype(BF16)
            return 0

        lax.fori_loop(0, model // own, gather, 0)


def home_backward(sample, chooser, back, h1, gy, gain, late, own, z, mix, u, gated, wz):
    wout, wout_spec = late_out(late, own)
    packs = sample.shape[0]
    rows, model = u.shape
    steps, inner, slots = rows // packs, mix.shape[1], chooser.shape[0]
    fixed = lambda p, lens: (0, 0)
    whole = lambda v: pl.BlockSpec(v.shape, fixed)
    part = lambda n: pl.BlockSpec((steps, n), lambda p, lens: (p, 0))
    shard = own // 2
    packed = whole_tiles(shard, inner)
    sums = [(inner, inner)] if packed else [(model, inner), (inner, model)]
    gains = (model, LANES) if packed else (1, model)
    return pl.pallas_call(
        functools.partial(home_backward_kernel, own=shard),
        grid_spec=pltpu.PrefetchScalarGridSpec(
            num_scalar_prefetch=1,
            grid=(packs,),
            in_specs=[
                pl.BlockSpec((slots, steps), lambda p, lens: (0, p)), whole(back), part(model), part(model), whole(gain),
                wout_spec, part(inner), part(inner), part(model), part(inner), whole(wz[0]), whole(wz[1]),
            ],
            out_specs=[
                part(model), part(inner), part(model), pl.BlockSpec(gains, fixed),
                *[pl.BlockSpec(shape, fixed) for shape in sums],
            ],
            scratch_shapes=[pltpu.VMEM((model, inner), F32), pltpu.VMEM((inner, model), F32)],
        ),
        out_shape=[
            jax.ShapeDtypeStruct((rows, model), F32),
            jax.ShapeDtypeStruct((rows, inner), F32),
            jax.ShapeDtypeStruct((rows, model), F32),
            jax.ShapeDtypeStruct(gains, F32),
            *[jax.ShapeDtypeStruct(shape, BF16) for shape in sums],
        ],
        compiler_params=pltpu.CompilerParams(vmem_limit_bytes=60 << 20),
        cost_estimate=pl.CostEstimate(flops=0, bytes_accessed=100_000, transcendentals=0),
        name="home_backward",
    )(sample, chooser, back, h1, gy, gain, wout, z, mix, u, gated, wz[0], wz[1])


def expert_grads_kernel(q_ref, gr_ref, *refs, parts):
    gps, acts, outs = refs[:parts], refs[parts : 2 * parts], refs[2 * parts :]
    for k in range(parts):
        outs[2 * k][...] = dot(q_ref[...], gps[k][...], ((0,), (0,))).astype(BF16)
        outs[2 * k + 1][...] = dot(acts[k][...], gr_ref[...], ((0,), (0,))).astype(BF16)


def expert_grads(q, gr, gps, acts):
    rows, model = q.shape
    hidden, parts = gps[0].shape[1], len(gps)
    block = 256 if hidden % 256 == 0 else 128
    whole = pl.BlockSpec((rows, model), lambda i: (0, 0))
    across = lambda n: pl.BlockSpec((n, block), lambda i: (0, i))
    down = pl.BlockSpec((block, model), lambda i: (i, 0))
    return pl.pallas_call(
        functools.partial(expert_grads_kernel, parts=parts),
        grid=(hidden // block,),
        in_specs=[whole, whole] + [across(rows)] * (2 * parts),
        out_specs=[across(model), down] * parts,
        out_shape=[jax.ShapeDtypeStruct((model, hidden), BF16), jax.ShapeDtypeStruct((hidden, model), BF16)] * parts,
        compiler_params=pltpu.CompilerParams(vmem_limit_bytes=60 << 20),
        cost_estimate=pl.CostEstimate(flops=0, bytes_accessed=100_000, transcendentals=0),
        name="expert_grads",
    )(q, gr, *gps, *acts)


def swap(values, axis, mask):
    count = lax.axis_size(axis)
    return lax.ppermute(values, axis, [(i, i ^ mask) for i in range(count)])


def grow(values, axis, mask, dim):
    got = swap(values, axis, mask)
    upper = (lax.axis_index(axis) & mask) != 0
    return jnp.concatenate([jnp.where(upper, got, values), jnp.where(upper, values, got)], axis=dim)


def gather_stages(width):
    count = lax.axis_size("fsdp")
    bits = count.bit_length() - 1
    place = lambda bit: bits - 1 - bit
    half = width // 2

    def upper(values):
        shape = values.shape
        every = jnp.stack([values] + [swap(values, "fsdp", mask) for mask in range(4, count, 4)])
        every = every.reshape((2,) * (bits - 2) + shape)
        for bit in range(2, bits):
            flipped = (lax.axis_index("fsdp") & (1 << bit)) != 0
            every = jnp.where(flipped, jnp.flip(every, place(bit)), every)
        return every.reshape((2,) * (bits - 2) + (1, 1) + shape)

    def split(values):
        return grow(values[..., :half], "fsdp", 2, place(1)), grow(values[..., half:], "fsdp", 1, place(0))

    def join(pair):
        left, right = grow(pair[0], "fsdp", 1, place(0)), grow(pair[1], "fsdp", 2, place(1))
        return jnp.concatenate([left, right], axis=-1)

    def across(mask):
        return lambda values: grow(values.reshape(1, -1, width), "dp", mask, 0)

    masks = [1 << i for i in range(lax.axis_size("dp").bit_length() - 1)]
    return [upper, split, join] + [across(mask) for mask in masks]


def gather_both(first, second, beside):
    shapes = [(-1, v.shape[1]) for v in (first, second)]
    values = [first, second]
    steps = [gather_stages(v.shape[1]) for v in values]
    count = len(steps[0])
    for at in range(count + 1):
        if at:
            *values, beside = lax.optimization_barrier((*values, beside))
        if at < count:
            values[0] = steps[0][at](values[0])
        if at:
            values[1] = steps[1][at - 1](values[1])
    return [v.reshape(shape) for v, shape in zip(values, shapes)] + [beside]


def fold(values, count):
    rows = values.shape[-2] // count
    return jnp.concatenate([values[..., j * rows : (j + 1) * rows, :] for j in range(count)], axis=-1)


def unfold(values, count):
    width = values.shape[-1] // count
    return jnp.concatenate([values[..., j * width : (j + 1) * width] for j in range(count)], axis=-2)


def own_block(values, index, count, axis):
    size = values.shape[axis] // count
    return lax.dynamic_slice_in_dim(values, index * size, size, axis)


def scatter_begin(pieces):
    sent = [swap(piece.astype(BF16), "dp", k + 1) for k, piece in enumerate(pieces[1:])]
    total = pieces[0].astype(F32)
    for got in sent:
        total = total + got.astype(F32)
    return total.astype(BF16)


def scatter_end(parts):
    return jnp.sum(lax.all_to_all(parts, "fsdp", 0, 0, tiled=True).astype(F32), axis=0)


def body(
    tokens,
    cotangent,
    routes,
    lengths,
    norm1_gain,
    input_weight,
    conv_weight,
    conv_bias,
    scan_weight,
    step_weight,
    step_bias,
    decay_log,
    skip_gain,
    out_weight,
    norm2_gain,
    router_weight,
    expert_up,
    expert_down,
):
    micro, steps, model = tokens.shape
    rows = micro * steps
    experts = lax.axis_size("fsdp")
    groups = lax.axis_size("dp")
    devices = experts * groups
    capacity = (5 * steps + 4 * experts - 1) // (4 * experts)
    slots = micro * capacity
    inner = input_weight.shape[1] // 2
    states = decay_log.shape[1]
    rank = step_weight.shape[1]
    taps = conv_weight.shape[1]
    own_model, own_inner = norm1_gain.shape[0], conv_bias.shape[0]

    packed = whole_tiles(own_model, inner)

    def gains_in(first, second):
        pair = [v.reshape(devices, 1, own_model) for v in (first, second)]
        column = jnp.concatenate(pair, axis=1).reshape(inner, 1)
        return jnp.where(jnp.arange(LANES) == rank + taps + 3, column, 0.0)

    half = experts // 2
    vectors = jnp.concatenate(
        [
            conv_weight,
            jnp.stack([conv_bias, step_bias, skip_gain, jnp.concatenate([norm1_gain, norm2_gain])]).T,
            decay_log,
            jnp.concatenate([router_weight[:, :half], router_weight[:, half:]], axis=0),
        ],
        axis=1,
    )
    padding = lambda n: jnp.zeros((own_inner, n), BF16)
    small = jnp.concatenate(
        [
            scan_weight,
            padding(LANES - rank - 2 * states),
            step_weight,
            vectors,
            padding(LANES - rank - vectors.shape[1]),
        ],
        axis=1,
    )
    folds = inner // (2 * LANES)
    late = jnp.concatenate([input_weight[:, inner : inner + model], input_weight[:, inner + model :], out_weight], axis=0)
    late = lax.all_gather(late, ("dp", "fsdp"), axis=0, tiled=False)
    input_z = [late[:, i * own_model : (i + 1) * own_model].reshape(model, model) for i in range(2)]
    ups = [expert_up[0]] + [swap(expert_up[0], "dp", k) for k in range(1, groups)]
    downs = [expert_down[0]] + [swap(expert_down[0], "dp", k) for k in range(1, groups)]

    place = jnp.arange(steps, dtype=jnp.int32)
    sample = lengths[:, 0, 0]
    live = (place[None, :] < sample[:, None]).astype(jnp.int32)
    route = routes[:, :, 0]
    expert_ids = jnp.arange(experts, dtype=jnp.int32)
    route_hot = (route[:, :, None] == expert_ids).astype(BF16)
    live_hot = route_hot * live[:, :, None].astype(BF16)
    earlier = (place[:, None] > place[None, :]).astype(BF16)
    before = lax.dot_general(
        jnp.broadcast_to(earlier, (micro, steps, steps)), live_hot, (((2,), (1,)), ((0,), (0,))),
        preferred_element_type=F32,
    )
    slot = jnp.sum(before * live_hot.astype(F32), axis=2).astype(jnp.int32)
    kept = (live * (slot < capacity).astype(jnp.int32)).reshape(rows)
    target = (route * slots + jnp.arange(micro, dtype=jnp.int32)[:, None] * capacity + slot).reshape(rows)
    chooser = (
        (jnp.arange(experts * slots, dtype=jnp.int32)[:, None] == target[None, :]) & (kept[None, :] == 1)
    ).astype(BF16)
    kept = kept.astype(F32)

    def to_experts(values):
        return lax.all_to_all(values.reshape(experts, slots, -1), "fsdp", 0, 0, tiled=True).reshape(experts * slots, -1)

    def from_experts(values):
        return dot(chooser, values.reshape(experts * slots, -1), ((0,), (0,)))

    def back_home(values):
        return lax.all_to_all(values.reshape(experts, slots, -1), "fsdp", 0, 0, tiled=True)

    cotangent = cotangent.reshape(rows, model)

    hidden = tokens.reshape(rows, model).astype(F32)
    inv_first = lax.rsqrt(jnp.mean(hidden * hidden, axis=-1, keepdims=True) + EPSILON)
    normed_first = hidden * inv_first
    input_x, small_full, upstream_rows = gather_both(
        input_weight[:, :inner], small, dot(chooser, cotangent).astype(BF16)
    )
    upstream_sent = to_experts(upstream_rows)
    vectors_full = small_full[:, LANES + rank :].T
    vectors_first = vectors_full[:ROWS].astype(F32)
    decay_full = vectors_full[taps + 4 : taps + 4 + states].astype(F32)
    gains = vectors_full[taps + 3].reshape(devices, 2, own_model)
    gain_one = gains[:, 0].reshape(model).astype(F32)
    gain_two = gains[:, 1].reshape(model).astype(F32)
    router_full = vectors_full[taps + 4 + states : taps + 4 + states + half].reshape(half, devices, 2, own_model)
    router_full = router_full.transpose(2, 0, 1, 3).reshape(experts, model)

    normed_low = (normed_first * gain_one).astype(BF16)
    decay_mat = -jnp.exp(decay_full)
    decay_two = decay_mat * LOG2E
    branch_x, scan_in, step_size, selected, mixer_out, states_kept = mixer_forward(
        sample, normed_low, input_x, small_full, vectors_first, decay_two, micro, rank, taps
    )
    mixer_out, upstream_sent = lax.optimization_barrier((mixer_out, upstream_sent))
    kept_hot = route_hot.reshape(rows, experts).astype(F32) * kept[:, None]
    branch_z, gated_low, residual, weight_row, sent = home_forward(
        sample, normed_low, input_z, late, own_inner, mixer_out, tokens.reshape(rows, model), gain_two[None, :], router_full,
        kept_hot, chooser,
    )
    received = to_experts(sent)

    mine = (expert_ids == lax.axis_index("fsdp")).astype(F32)[None, :]
    result, grad_rows, flat_grad, router_grad, acts, grad_pres = expert_pass(
        received, upstream_sent, router_full, mine, ups, downs
    )
    grad_rows, result, received, flat_grad = lax.optimization_barrier((grad_rows, result, received, flat_grad))
    grad_back = back_home(grad_rows)
    matrix_grads = expert_grads(received, flat_grad, grad_pres, acts)
    at_gain, at_decay, at_router = rank + taps + 3, rank + taps + 4, rank + taps + 4 + states
    lane = jnp.arange(LANES)
    router_grads = router_grad.reshape(2, half, devices, own_model).transpose(2, 0, 3, 1).reshape(inner, half)
    extra = jnp.pad(router_grads, ((0, 0), (at_router, LANES - at_router - half)))
    gain_row = gain_one[None, :]
    grad_back, matrix_grads, extra, gain_row, result = lax.optimization_barrier(
        (grad_back, matrix_grads, extra, gain_row, result)
    )
    result = back_home(result)
    up_own, down_own, *others = matrix_grads
    others = [swap(other, "dp", k // 2 + 1) for k, other in enumerate(others)]

    grad_residual, grad_mixer, grad_normed_z, gain_two_grad, *late_terms = home_backward(
        sample, chooser, grad_back.reshape(experts * slots, model), residual, cotangent, gain_two[None, :], late,
        own_inner, branch_z, mixer_out, normed_low, gated_low, input_z,
    )
    if not packed:
        blocks = [v.reshape(devices, -1, v.shape[1]) for v in late_terms]
        late_terms = [jnp.concatenate([blocks[0], fold(blocks[1], 2)], axis=1).reshape(-1, inner)]
    late_grads = lax.psum_scatter(late_terms[0], ("dp", "fsdp"), scatter_dimension=0, tiled=True)
    if not packed:
        extra = extra + gains_in(jnp.zeros_like(gain_two_grad), gain_two_grad)
    grad_mixer, others = lax.optimization_barrier((grad_mixer, others))
    mixer_grads = mixer_backward(
        jnp.append(sample, lax.axis_index("dp")), step_size, scan_in, branch_x, grad_mixer, selected, small_full, vectors_first, decay_two,
        states_kept, input_x, tokens.reshape(rows, model), gain_row, grad_normed_z, grad_residual, normed_low, extra,
        gain_two_grad, micro, rank, taps, at_gain, own_model, groups,
    )
    if packed:
        *early_terms, tokens_grad = mixer_grads
        early_terms = [terms.reshape(experts, -1, inner) for terms in early_terms]
    else:
        tokens_grad, input_x_grad, select_grad, step_grad, gain_one_grad = mixer_grads
        step_grad = step_grad + gains_in(gain_one_grad, jnp.zeros_like(gain_one_grad))
        blocks = jnp.concatenate([select_grad, step_grad], axis=1).reshape(devices, own_inner, 2 * LANES)
        blocks = jnp.concatenate([input_x_grad.reshape(devices, own_model, inner), fold(blocks, folds)], axis=1)
        blocks = blocks.reshape(groups, experts, -1, inner)
        me = lax.axis_index("dp")
        early_terms = [lax.dynamic_index_in_dim(blocks, me ^ k, 0, False) for k in range(groups)]
    early_terms, result = lax.optimization_barrier((early_terms, result))
    early_terms = scatter_begin(early_terms)
    early_terms, others, result = lax.optimization_barrier((early_terms, others, result))
    early_grads = scatter_end(early_terms)
    up_grad, down_grad = up_own.astype(F32), down_own.astype(F32)
    for k in range(groups - 1):
        up_grad = up_grad + others[2 * k].astype(F32)
        down_grad = down_grad + others[2 * k + 1].astype(F32)
    late_grads = late_grads.astype(F32)
    block_output = (residual + weight_row * from_experts(result)).astype(BF16)
    small_grads = unfold(early_grads[own_model:], folds)
    vector_grads = small_grads[:, LANES:]
    routers = vector_grads[:, at_router : at_router + half]
    return (
        block_output.reshape(micro, steps, model),
        tokens_grad.reshape(micro, steps, model),
        vector_grads[:own_model, at_gain],
        jnp.concatenate([early_grads[:own_model], late_grads[:own_model]], axis=1),
        vector_grads[:, rank : rank + taps],
        vector_grads[:, rank + taps],
        small_grads[:, : rank + 2 * states],
        vector_grads[:, :rank],
        vector_grads[:, rank + taps + 1],
        vector_grads[:, at_decay : at_decay + states],
        vector_grads[:, rank + taps + 2],
        unfold(late_grads[own_model:], 2),
        vector_grads[own_model:, at_gain],
        jnp.concatenate([routers[:own_model], routers[own_model:]], axis=1),
        up_grad[None],
        down_grad[None],
    )


def solution(mesh):
    rows3 = P(None, ("dp", "fsdp"), None)
    vector = P(("dp", "fsdp"))
    matrix = P(("dp", "fsdp"), None)
    weights = (
        vector, matrix, matrix, vector, matrix, matrix, vector, matrix, vector, matrix, vector, matrix,
        P("fsdp", None, "dp"), P("fsdp", "dp", None),
    )
    return jax.shard_map(
        body,
        mesh=mesh,
        in_specs=(rows3, rows3, rows3, rows3) + weights,
        out_specs=(rows3, rows3) + weights,
        check_vma=False,
    )
```

```python
import functools

import jax
import jax.numpy as jnp
from jax import lax
from jax.experimental import pallas as pl
from jax.experimental.pallas import tpu as pltpu
from jax.sharding import PartitionSpec as P

EPSILON = 1e-05
LOG2E = 1.4426950408889634
LN2 = 0.6931471805599453
LANES = 128
ROWS = 8
F32 = jnp.float32
BF16 = jnp.bfloat16


def dot(left, right, dims=((1,), (0,))):
    return lax.dot_general(left, right, (dims, ((), ())), preferred_element_type=F32)


def fold_rows(parts):
    place = lax.broadcasted_iota(jnp.int32, parts[0].shape, 0)
    half = 1
    while half < ROWS:
        lower = (place & half) == 0
        merged = []
        for i in range(0, len(parts), 2):
            a, b = parts[i], parts[i + 1]
            merged.append(jnp.where(lower, a, b) + pltpu.roll(jnp.where(lower, b, a), half, 0))
        parts = merged
        half *= 2
    return parts[0]


def sum_states(parts):
    halves = []
    for p in parts:
        total = p[:ROWS]
        for i in range(1, p.shape[0] // ROWS):
            total = total + p[i * ROWS : (i + 1) * ROWS]
        halves.append(total)
    return fold_rows(halves)


def lane_chunk(k, count=1):
    return pl.ds(pl.multiple_of(k * LANES * count, LANES), LANES * count)


def split_low(values):
    high = values.astype(BF16)
    return high, (values - high.astype(F32)).astype(BF16)


def own_lanes(first, states, size):
    lane = lax.broadcasted_iota(jnp.int32, (size, states, LANES), 2)
    row = lax.broadcasted_iota(jnp.int32, (size, states, LANES), 1)
    return (lane == row + first) | (lane == row + first + states)


def widen(selected, first, states, bw, cw):
    steps = selected.shape[0]
    lane = lax.broadcasted_iota(jnp.int32, (2 * LANES, 2 * LANES), 0) % LANES
    to_c = lax.broadcasted_iota(jnp.int32, (2 * LANES, 2 * LANES), 1) >= LANES
    spread = (to_c == (lane >= first + states)).astype(BF16)
    size = 64
    own = own_lanes(first, states, size)
    for at in range(0, steps, size):
        rows = jnp.where(own, selected[at : at + size][:, None, :], 0.0).reshape(size * states, LANES)
        wide = dot(jnp.concatenate(split_low(rows), axis=1), spread)
        bw[at * states : (at + size) * states, :] = wide[:, :LANES]
        cw[at * states : (at + size) * states, :] = wide[:, LANES:]


def narrow(gb, gc, first, states, steps):
    lane = lax.broadcasted_iota(jnp.int32, (2 * LANES, LANES), 1)
    from_c = lax.broadcasted_iota(jnp.int32, (2 * LANES, LANES), 0) >= LANES
    gather = (from_c == (lane >= first + states)).astype(BF16)
    size = 64
    own = own_lanes(first, states, size)
    out = []
    for at in range(0, steps, size):
        here = slice(at * states, (at + size) * states)
        rows = jnp.concatenate([gb[here, :].astype(BF16), gc[here, :].astype(BF16)], axis=1)
        sums = dot(rows, gather).reshape(size, states, LANES)
        out.append(jnp.sum(jnp.where(own, sums, 0.0), axis=1))
    return jnp.concatenate(out, axis=0)


def conv_of(x_ref, vec_ref, lanes, taps, steps):
    total = vec_ref[taps : taps + 1, lanes]
    for shift in range(taps):
        total = total + vec_ref[taps - 1 - shift : taps - shift, lanes] * x_ref[ROWS - shift : ROWS - shift + steps, lanes]
    return total


def lane_halves(small):
    return [pl.BlockSpec((small.shape[0], LANES), lambda p, lens, half=half: (0, half)) for half in range(2)]


def unpack_small(small_ref, taps, rank, states, own, half, vec_ref, a_ref, gain_ref, router_ref):
    width = small_ref.shape[0]
    columns = small_ref[...].astype(F32)
    rows = columns.T
    first = rank + taps + 4
    vec_ref[...] = rows[rank : rank + ROWS]
    a_ref[...] = -jnp.exp(rows[first : first + states]) * LOG2E
    devices = columns.reshape(width // (2 * own), 2 * own, LANES)
    for part in range(2):
        rows = devices[:, part * own : (part + 1) * own].reshape(width // 2, LANES).T
        gain_ref[part : part + 1, :] = rows[first - 1 : first]
        router_ref[part * half : (part + 1) * half, :] = rows[first + states : first + states + half].astype(BF16)


def forward_kernel(len_ref, x_ref, wx_ref, sela_ref, stepb_ref, *refs, group, rank, taps, own, half):
    if own:
        *refs, vec_ref, a_ref, gain_ref, router_ref, u_ref = refs

        @pl.when(pl.program_id(0) == 0)
        def _():
            unpack_small(stepb_ref, taps, rank, a_ref.shape[0], own, half, vec_ref, a_ref, gain_ref, router_ref)

        hidden = x_ref[...].astype(F32)
        inv = lax.rsqrt(jnp.mean(hidden * hidden, axis=1, keepdims=True) + EPSILON)
        u_ref[...] = (hidden * inv * gain_ref[:1, :]).astype(BF16)
    else:
        vec_ref, a_ref, *refs = refs
        u_ref = x_ref
    bx_ref, xs_ref, delta_ref, sel_ref, mix_ref, h_ref, state, bw, cw, low = refs
    states, width = a_ref.shape
    steps = u_ref.shape[0]
    chunks = width // LANES
    bias_step, skip = taps + 1, taps + 2
    state[...] = jnp.zeros_like(state)
    bx_ref[:ROWS, :] = jnp.zeros((ROWS, width), F32)

    def project(k, _):
        lanes = lane_chunk(k, 2)
        bx_ref[ROWS:, lanes] = dot(u_ref[...], wx_ref[:, lanes])
        return 0

    lax.fori_loop(0, chunks // 2, project, 0, unroll=True)

    def convolve(k, _):
        lanes = lane_chunk(k)
        conv = conv_of(bx_ref, vec_ref, lanes, taps, steps)
        xs = conv * jax.nn.sigmoid(conv)
        xs_ref[:, lanes] = xs
        low[:, lanes] = xs.astype(BF16)
        return 0

    lax.fori_loop(0, chunks, convolve, 0, unroll=2)
    selected = dot(low[...], sela_ref[...])
    sel_ref[...] = selected
    lane = lax.broadcasted_iota(jnp.int32, selected.shape, 1)
    rank_low = jnp.where(lane < rank, selected, 0.0).astype(BF16)
    widen(selected, rank, states, bw, cw)

    def sizes(k, _):
        lanes = lane_chunk(k, 2)
        pre = dot(rank_low, stepb_ref[lanes, :], ((1,), (1,))) + vec_ref[bias_step : bias_step + 1, lanes]
        delta_ref[:, lanes] = jnp.maximum(pre, 0.0) + jnp.log1p(jnp.exp(-jnp.abs(pre)))
        return 0

    lax.fori_loop(0, chunks // 2, sizes, 0, unroll=2)

    def rows(s, _):
        at = pl.multiple_of(s * ROWS, ROWS)

        def chunk(g, _):
            for u in range(group):
                lanes = lane_chunk(g * group + u)
                d = delta_ref[pl.ds(at, ROWS), lanes]
                x = xs_ref[pl.ds(at, ROWS), lanes]
                dx = d * x
                a = a_ref[:, lanes]
                h = state[:, lanes]
                h_ref[s, :, lanes] = h
                parts = []
                for t in range(ROWS):
                    here = pl.ds(pl.multiple_of((at + t) * states, states), states)
                    h = jnp.exp2(d[t : t + 1] * a) * h + bw[here, :] * dx[t : t + 1]
                    parts.append(cw[here, :] * h)
                state[:, lanes] = h
                mix_ref[pl.ds(at, ROWS), lanes] = sum_states(parts) + vec_ref[skip : skip + 1, lanes] * x
            return 0

        lax.fori_loop(0, chunks // group, chunk, 0)
        return 0

    used = (len_ref[pl.program_id(0)] + ROWS - 1) // ROWS
    lax.fori_loop(0, used, rows, 0)

    def clear(s, _):
        mix_ref[pl.ds(pl.multiple_of(s * ROWS, ROWS), ROWS), :] = jnp.zeros((ROWS, width), F32)
        return 0

    lax.fori_loop(used, steps // ROWS, clear, 0)


def mixer_forward(sample, x, wx, small, vec, a2, packs, rank, taps, states, own, half, group=12):
    rows, model = x.shape
    steps, width = rows // packs, wx.shape[1]
    per_pack = lambda p, lens: (p, 0)
    fixed = lambda p, lens: (0, 0)
    whole = lambda v: pl.BlockSpec(v.shape, fixed)
    mats = pl.BlockSpec((steps, width), per_pack)
    toks = pl.BlockSpec((steps, model), per_pack)
    given = [] if own else [vec, a2]
    outs = [
        jax.ShapeDtypeStruct((rows + packs * ROWS, width), F32),
        jax.ShapeDtypeStruct((rows, width), F32),
        jax.ShapeDtypeStruct((rows, width), F32),
        jax.ShapeDtypeStruct((rows, LANES), F32),
        jax.ShapeDtypeStruct((rows, width), F32),
        jax.ShapeDtypeStruct((rows // ROWS, states, width), F32),
    ]
    out_specs = [
        pl.BlockSpec((steps + ROWS, width), per_pack),
        mats,
        mats,
        pl.BlockSpec((steps, LANES), per_pack),
        mats,
        pl.BlockSpec((steps // ROWS, states, width), lambda p, lens: (p, 0, 0)),
    ]
    scratch = [
        pltpu.VMEM((states, width), F32),
        pltpu.VMEM((steps * states, LANES), F32),
        pltpu.VMEM((steps * states, LANES), F32),
        pltpu.VMEM((steps, width), BF16),
    ]
    count = len(outs)
    if own:
        more = [((ROWS, width), F32), ((states, width), F32), ((2, model), F32), ((2 * half, model), BF16)]
        outs += [jax.ShapeDtypeStruct(*one) for one in more] + [jax.ShapeDtypeStruct((rows, model), BF16)]
        out_specs += [pl.BlockSpec(shape, fixed) for shape, _ in more] + [toks]

    def kernel(len_ref, x_ref, wx_ref, sela_ref, stepb_ref, *refs):
        at = len(given) + count
        refs = refs[:at] + refs[len(given) + len(outs) :] + refs[at : len(given) + len(outs)]
        forward_kernel(
            len_ref, x_ref, wx_ref, sela_ref, stepb_ref, *refs, group=group, rank=rank, taps=taps, own=own, half=half
        )

    return pl.pallas_call(
        kernel,
        grid_spec=pltpu.PrefetchScalarGridSpec(
            num_scalar_prefetch=1,
            grid=(packs,),
            in_specs=[toks, whole(wx), *lane_halves(small), *[whole(v) for v in given]],
            out_specs=out_specs,
            scratch_shapes=scratch,
        ),
        out_shape=outs,
        compiler_params=pltpu.CompilerParams(vmem_limit_bytes=56 << 20),
        cost_estimate=pl.CostEstimate(flops=0, bytes_accessed=120_000_000, transcendentals=0),
        name="mixer_forward",
    )(sample, x, wx, small, small, *given)


def step_slopes(d):
    small = d < 0.01
    slope = 1.0 - d * (0.5 - d * (1.0 / 6.0))
    rise = 1.0 - jnp.exp(-d)
    return jnp.where(small, d * slope, rise), jnp.where(small, slope, rise / jnp.where(small, 1.0, d))


def backward_kernel(len_ref, delta_ref, xs_ref, bx_ref, gm_ref, sel_ref, sela_ref, stepb_ref, vec_ref, a_ref, h_ref,
                    wx_ref, x_ref, gain_ref, gu_ref, gh_ref, u_ref, extra_ref, second_ref, *refs,
                    group, rank, taps, at_gain, own, groups):
    if own:
        outs, refs = refs[:groups], refs[groups:]
        gtok_ref, gxw_ref, gsel_ref, gstep_ref, ggain_ref = refs[:5]
    else:
        gtok_ref, gxw_ref, gsel_ref, gstep_ref, ggain_ref = refs[:5]
    mu_s, bw, cw, gb, gc, gd, gxs, low, gx_ref, gvec_ref, ga_ref, tile = refs[-12:]
    pack = pl.program_id(0)
    states, width = a_ref.shape
    steps = sel_ref.shape[0]
    chunks = width // LANES
    bias_conv, bias_step, skip = taps, taps + 1, taps + 2

    @pl.when(pack == 0)
    def _():
        ga_ref[...] = jnp.zeros_like(ga_ref)
        gsel_ref[...] = jnp.zeros_like(gsel_ref)
        gstep_ref[...] = extra_ref[...]
        gxw_ref[...] = jnp.zeros_like(gxw_ref)
        gvec_ref[...] = jnp.zeros_like(gvec_ref)
        ggain_ref[...] = jnp.zeros_like(ggain_ref)

    mu_s[...] = jnp.zeros_like(mu_s)
    gb[...] = jnp.zeros_like(gb)
    gc[...] = jnp.zeros_like(gc)
    selected = sel_ref[...]
    widen(selected, rank, states, bw, cw)
    used = (len_ref[pack] + ROWS - 1) // ROWS

    def clear(s, _):
        here = pl.ds(pl.multiple_of(s * ROWS, ROWS), ROWS)
        gd[here, :] = jnp.zeros((ROWS, width), F32)
        gxs[here, :] = jnp.zeros((ROWS, width), F32)
        return 0

    lax.fori_loop(used, steps // ROWS, clear, 0)

    def rows(back, _):
        s = used - 1 - back
        at = pl.multiple_of(s * ROWS, ROWS)
        place = [pl.ds(pl.multiple_of((at + t) * states, states), states) for t in range(ROWS)]

        def chunk(g, _):
            each = []
            for u in range(group):
                lanes = lane_chunk(g * group + u)
                d = delta_ref[pl.ds(at, ROWS), lanes]
                x = xs_ref[pl.ds(at, ROWS), lanes]
                a = a_ref[:, lanes]
                dx = d * x
                tile[3 * u] = d
                tile[3 * u + 1] = dx
                tile[3 * u + 2] = gm_ref[pl.ds(at, ROWS), lanes]
                h, power, decay = [h_ref[s, :, lanes]], [], []
                for t in range(ROWS):
                    power.append(tile[3 * u, t : t + 1, :] * a)
                    decay.append(jnp.exp2(power[t]))
                    h.append(decay[t] * h[t] + bw[place[t], :] * tile[3 * u + 1, t : t + 1, :])
                each.append(dict(lanes=lanes, d=d, x=x, mu=mu_s[:, lanes], h=h, power=power, decay=decay,
                                 ga=ga_ref[:, lanes], sp=[None] * ROWS, gp=[None] * ROWS))
            for t in range(ROWS - 1, -1, -1):
                b, c = bw[place[t], :], cw[place[t], :]
                one_b = one_c = None
                for u, v in enumerate(each):
                    gyt = tile[3 * u + 2, t : t + 1, :]
                    lam = c * gyt + v["mu"]
                    v["sp"][t] = b * lam
                    to_b = lam * tile[3 * u + 1, t : t + 1, :]
                    to_c = v["h"][t + 1] * gyt
                    one_b = to_b if one_b is None else one_b + to_b
                    one_c = to_c if one_c is None else one_c + to_c
                    v["mu"] = v["decay"][t] * lam
                    v["gp"][t] = v["mu"] * v["h"][t] * v["power"][t]
                    v["ga"] = v["ga"] + v["gp"][t]
                gb[place[t], :] += one_b
                gc[place[t], :] += one_c
            for v in each:
                lanes = v["lanes"]
                mu_s[:, lanes], ga_ref[:, lanes] = v["mu"], v["ga"]
                total = sum_states(v["sp"])
                rise, slope = step_slopes(v["d"])
                gd[pl.ds(at, ROWS), lanes] = sum_states(v["gp"]) * (slope * LN2) + v["x"] * total * rise
                gxs[pl.ds(at, ROWS), lanes] = v["d"] * total
            return 0

        lax.fori_loop(0, chunks // group, chunk, 0)
        return 0

    lax.fori_loop(0, used, rows, 0)

    def add_row(row, lanes, values):
        gvec_ref[row : row + 1, lanes] += jnp.sum(values, axis=0, keepdims=True)

    def sizes(k, _):
        lanes = lane_chunk(k)
        grad = gd[:steps, lanes]
        add_row(bias_step, lanes, grad)
        low[:, lanes] = grad.astype(BF16)
        add_row(skip, lanes, gm_ref[:, lanes] * xs_ref[:, lanes])
        return 0

    lax.fori_loop(0, chunks, sizes, 0, unroll=2)
    gd[steps:, :] = jnp.zeros((ROWS, width), F32)
    lane = lax.broadcasted_iota(jnp.int32, selected.shape, 1)
    rank_low = jnp.where(lane < rank, selected, 0.0).astype(BF16)
    grad_rank = dot(low[...], stepb_ref[...])
    gstep_ref[...] += dot(low[...], rank_low, ((0,), (0,)))
    grad_sel = jnp.where(lane < rank, grad_rank, narrow(gb, gc, rank, states, steps)).astype(BF16)

    def values(k, _):
        lanes = lane_chunk(k)
        conv = conv_of(bx_ref, vec_ref, lanes, taps, steps)
        sig = jax.nn.sigmoid(conv)
        low[:, lanes] = (conv * sig).astype(BF16)
        grad = dot(grad_sel, sela_ref[lanes, :], ((1,), (1,)))
        grad = grad + gxs[:, lanes] + gm_ref[:, lanes] * vec_ref[skip : skip + 1, lanes]
        grad = grad * (sig * (1.0 + conv * (1.0 - sig)))
        gd[:steps, lanes] = grad
        add_row(bias_conv, lanes, grad)
        back_x = None
        for j in range(taps):
            shift = taps - 1 - j
            add_row(j, lanes, grad * bx_ref[ROWS - shift : ROWS - shift + steps, lanes])
            term = vec_ref[j : j + 1, lanes] * gd[shift : shift + steps, lanes]
            back_x = term if back_x is None else back_x + term
        gx_ref[:, lanes] = back_x.astype(BF16)
        return 0

    lax.fori_loop(0, chunks, values, 0, unroll=2)
    gsel_ref[...] += dot(low[...], grad_sel, ((0,), (0,)))

    def product(k, _):
        lanes = lane_chunk(k, 4)
        gxw_ref[:, lanes] += dot(u_ref[...], gx_ref[:, lanes], ((0,), (0,)))
        return 0

    lax.fori_loop(0, chunks // 4, product, 0, unroll=True)
    hidden = x_ref[...].astype(F32)
    inv = lax.rsqrt(jnp.mean(hidden * hidden, axis=1, keepdims=True) + EPSILON)
    normed = hidden * inv
    grad_u = dot(gx_ref[...], wx_ref[...], ((1,), (1,))) + gu_ref[...]
    scaled = grad_u * gain_ref[...]
    if own:
        ones = jnp.ones((steps, LANES), BF16)
        high, rest = split_low(grad_u * normed)
        ggain_ref[...] += dot(high, ones, ((0,), (0,))) + dot(rest, ones, ((0,), (0,)))
    else:
        ggain_ref[...] += jnp.sum(grad_u * normed, axis=0, keepdims=True)
    gtok_ref[...] = gh_ref[...] + inv * (scaled - normed * jnp.mean(scaled * normed, axis=1, keepdims=True))

    @pl.when(pack == pl.num_programs(0) - 1)
    def _():
        rows_of_vectors = jnp.concatenate([gvec_ref[...], ga_ref[...] * LN2], axis=0)
        before = jnp.zeros((rank, width), F32)
        after = jnp.zeros((LANES - rank - rows_of_vectors.shape[0], width), F32)
        gstep_ref[...] += jnp.concatenate([before, rows_of_vectors, after], axis=0).T
        if own:
            lane = lax.broadcasted_iota(jnp.int32, (own, LANES), 1)
            folds = width // (2 * LANES)
            run = 2 * own // folds

            size = own + run
            count = width // (2 * own) // groups

            def gather(slot, f):
                i = (len_ref[pl.num_programs(0)] ^ slot) * count + f
                mine = pl.ds(pl.multiple_of(own * i, ROWS), own)
                for part, ref in enumerate((ggain_ref, second_ref)):
                    here = pl.ds(pl.multiple_of(2 * own * i + own * part, ROWS), own)
                    gstep_ref[here, :] += jnp.where(lane == at_gain, ref[mine, :], 0.0)
                parts = []
                for j in range(folds):
                    here = pl.ds(pl.multiple_of(2 * own * i + run * j, ROWS), run)
                    parts += [gsel_ref[here, :], gstep_ref[here, :]]
                block = jnp.concatenate([gxw_ref[mine, :], jnp.concatenate(parts, axis=1)], axis=0)
                outs[slot][pl.ds(pl.multiple_of(size * f, size), size), :] = block.astype(BF16)
                return 0

            for slot in range(groups):
                lax.fori_loop(0, count, lambda f, _, slot=slot: gather(slot, f), 0)


def whole_tiles(own, width):
    return own % ROWS == 0 and 4 * own * LANES % (ROWS * width) == 0


def mixer_backward(sample, delta, xs, bx, gm, sel, small, vec, a2, hall, wx, tokens, gain, grad_u, grad_h, u, extra, second,
                   packs, rank, taps, at_gain, own, groups, group=3):
    rows, width = delta.shape
    steps = rows // packs
    states, model = a2.shape[0], tokens.shape[1]
    per_pack = lambda p, lens: (p, 0)
    fixed = lambda p, lens: (0, 0)
    whole = lambda v: pl.BlockSpec(v.shape, fixed)
    mats = pl.BlockSpec((steps, width), per_pack)
    toks = pl.BlockSpec((steps, model), per_pack)
    own = own if whole_tiles(own, width) else 0
    sums = [(model, width), (width, LANES), (width, LANES), (model, LANES) if own else (1, model)]
    size = own + 4 * own * LANES // width
    outs = [jax.ShapeDtypeStruct((rows, model), F32)]
    out_specs = [toks]
    scratch = [
        pltpu.VMEM((states, width), F32),
        pltpu.VMEM((steps * states, LANES), F32),
        pltpu.VMEM((steps * states, LANES), F32),
        pltpu.VMEM((steps * states, LANES), F32),
        pltpu.VMEM((steps * states, LANES), F32),
        pltpu.VMEM((steps + ROWS, width), F32),
        pltpu.VMEM((steps, width), F32),
        pltpu.VMEM((steps, width), BF16),
        pltpu.VMEM((steps, width), BF16),
        pltpu.VMEM((ROWS, width), F32),
        pltpu.VMEM((states, width), F32),
        pltpu.VMEM((3 * group, ROWS, LANES), F32),
    ]
    if own:
        outs = [jax.ShapeDtypeStruct((model // own // groups * size, width), BF16)] * groups + outs
        out_specs = [pl.BlockSpec(outs[0].shape, fixed)] * groups + out_specs
        scratch = [pltpu.VMEM(shape, F32) for shape in sums] + scratch
    else:
        outs += [jax.ShapeDtypeStruct(shape, F32) for shape in sums]
        out_specs += [pl.BlockSpec(shape, fixed) for shape in sums]
    return pl.pallas_call(
        functools.partial(backward_kernel, group=group, rank=rank, taps=taps, at_gain=at_gain, own=own, groups=groups),
        grid_spec=pltpu.PrefetchScalarGridSpec(
            num_scalar_prefetch=1,
            grid=(packs,),
            in_specs=[
                mats, mats,
                pl.BlockSpec((steps + ROWS, width), per_pack),
                mats,
                pl.BlockSpec((steps, LANES), per_pack),
                *lane_halves(small), whole(vec), whole(a2),
                pl.BlockSpec((steps // ROWS, states, width), lambda p, lens: (p, 0, 0)),
                whole(wx), toks, whole(gain), toks, toks, toks, whole(extra), whole(second),
            ],
            out_specs=out_specs,
            scratch_shapes=scratch,
        ),
        out_shape=outs,
        compiler_params=pltpu.CompilerParams(vmem_limit_bytes=62 << 20),
        cost_estimate=pl.CostEstimate(flops=0, bytes_accessed=100_000, transcendentals=0),
        name="mixer_backward",
    )(sample, delta, xs, bx, gm, sel, small, small, vec, a2, hall, wx, tokens, gain, grad_u, grad_h, u, extra, second)


def expert_kernel(*refs, parts):
    q_ref, gy_ref, router_ref, mine_ref = refs[:4]
    ups, downs = refs[4 : 4 + parts], refs[4 + parts : 4 + 2 * parts]
    outs = refs[4 + 2 * parts :]
    result_ref, gq_ref, gr_ref, grouter_ref = outs[:4]
    acts, grads = outs[4 : 4 + parts], outs[4 + parts : 4 + 2 * parts]
    total, back, gates = outs[4 + 2 * parts :]
    step = pl.program_id(0)

    @pl.when(step == 0)
    def _():
        logits = dot(q_ref[...], router_ref[...], ((1,), (1,)))
        odds = jnp.exp(logits - jnp.max(logits, axis=1, keepdims=True))
        probs = odds / jnp.sum(odds, axis=1, keepdims=True)
        gate = jnp.sum(probs * mine_ref[...], axis=1, keepdims=True)
        gates[...] = gate * (mine_ref[...] - probs)
        gr_ref[...] = (gate * gy_ref[...].astype(F32)).astype(BF16)
        total[...] = jnp.zeros_like(total)
        back[...] = jnp.zeros_like(back)

    q, gr = q_ref[...], gr_ref[...]
    root = 0.7978845608028654
    pres = [dot(q, up[...]) for up in ups]
    grad_acts = [dot(gr, down[...], ((1,), (1,))) for down in downs]
    for k, (pre, grad_act) in enumerate(zip(pres, grad_acts)):
        square = pre * pre
        t = jnp.tanh(root * pre * (1.0 + 0.044715 * square))
        half = 0.5 * (1.0 + t)
        act = (pre * half).astype(BF16)
        slope = half + (0.5 * root) * pre * (1.0 - t * t) * (1.0 + 0.134145 * square)
        grad = (grad_act * slope).astype(BF16)
        acts[k][...] = act
        grads[k][...] = grad
        total[...] += dot(act, downs[k][...])
        back[...] += dot(grad, ups[k][...], ((1,), (1,)))

    @pl.when(step == pl.num_programs(0) - 1)
    def _():
        result = total[...].astype(BF16)
        result_ref[...] = result
        grad_gate = jnp.sum(gy_ref[...].astype(F32) * result.astype(F32), axis=1, keepdims=True)
        grad_logits = (grad_gate * gates[...]).astype(BF16)
        grouter_ref[...] = dot(grad_logits, q_ref[...], ((0,), (0,)))
        gq_ref[...] = (dot(grad_logits, router_ref[...]) + back[...]).astype(BF16)


def expert_pass(q, gy, router, mine, ups, downs):
    rows, model = q.shape
    experts = router.shape[0]
    parts = len(ups)
    hidden = ups[0].shape[1]
    block = 256 if hidden % 256 == 0 else 128
    fixed = lambda i: (0, 0)
    whole = lambda shape: pl.BlockSpec(shape, fixed)
    across = lambda n: pl.BlockSpec((n, block), lambda i: (0, i))
    down = pl.BlockSpec((block, model), lambda i: (i, 0))
    outs = pl.pallas_call(
        functools.partial(expert_kernel, parts=parts),
        grid=(hidden // block,),
        in_specs=[whole(q.shape), whole(gy.shape), whole(router.shape), whole(mine.shape)]
        + [across(model)] * parts
        + [down] * parts,
        out_specs=[whole((rows, model))] * 3 + [whole((experts, model))] + [across(rows)] * (2 * parts),
        out_shape=[jax.ShapeDtypeStruct((rows, model), BF16)] * 3
        + [jax.ShapeDtypeStruct((experts, model), F32)]
        + [jax.ShapeDtypeStruct((rows, hidden), BF16)] * (2 * parts),
        scratch_shapes=[pltpu.VMEM((rows, model), F32), pltpu.VMEM((rows, model), F32), pltpu.VMEM((rows, experts), F32)],
        compiler_params=pltpu.CompilerParams(vmem_limit_bytes=56 << 20),
        cost_estimate=pl.CostEstimate(flops=0, bytes_accessed=70_000_000, transcendentals=0),
        name="expert_pass",
    )(q, gy, router, mine, *ups, *downs)
    return (*outs[:4], outs[4 : 4 + parts], outs[4 + parts :])
def rows_from(ref, here):
    if len(ref.shape) == 2:
        return ref[here, :]
    run = ref.shape[1]
    return ref[here.start // run : here.stop // run].reshape(here.stop - here.start, ref.shape[2])


def late_specs(late, own):
    devices, count, model = late.shape
    if own % 16 == 0:
        block = (devices, own, model)
        return [late, late], [pl.BlockSpec(block, lambda p, lens, at=at: (0, at, 0)) for at in range(2)]
    rows = [late[:, at : at + size].reshape(-1, model) for at, size in ((0, own // 2), (own // 2, own // 2), (own, own))]
    return rows, [pl.BlockSpec(v.shape, lambda p, lens: (0, 0)) for v in rows]


def gate_halves(refs, scratch):
    if len(refs) == 3:
        return refs[:2], refs[2]

    @pl.when(pl.program_id(0) == 0)
    def _():
        devices, run, model = refs[0].shape
        step = 4
        for at in range(0, devices, step):
            both = refs[0][at : at + step].astype(F32)
            for half, ref in enumerate(scratch):
                one = both[:, half * (run // 2) : (half + 1) * (run // 2)]
                ref[at * (run // 2) : (at + step) * (run // 2), :] = one.reshape(step * (run // 2), model).astype(BF16)

    return scratch, refs[1]


def gate_scratch(operands, model):
    return [pltpu.VMEM((model, model), BF16)] * 2 if len(operands) == 2 else []


def live_rows(length, steps):
    return (lax.broadcasted_iota(jnp.int32, (steps, 1), 0) < length).astype(F32)


def norm_of(values):
    inv = lax.rsqrt(jnp.mean(values * values, axis=1, keepdims=True) + EPSILON)
    return values * inv, inv


def home_forward_kernel(len_ref, u_ref, mix_ref, x_ref, gain_ref, router_ref, hot_ref, choose_ref, *refs, count):
    late, refs = refs[:count], refs[count:]
    z_ref, gated_ref, h1_ref, weight_ref, sent_ref, total, *scratch = refs
    gates, wout_ref = gate_halves(late, scratch)
    pack = pl.program_id(0)
    steps, model = u_ref.shape
    mixed = jnp.zeros((steps, model), F32)
    for half, w_ref in enumerate(gates):
        here = slice(half * model, (half + 1) * model)
        z = dot(u_ref[...], w_ref[...])
        z_ref[:, here] = z
        gated = (mix_ref[:, here] * (z * jax.nn.sigmoid(z))).astype(BF16)
        gated_ref[:, here] = gated
        mixed = mixed + dot(gated, rows_from(wout_ref, here))
    h1 = x_ref[...].astype(F32) + live_rows(len_ref[pack], steps) * mixed
    h1_ref[...] = h1
    routed = (norm_of(h1)[0] * gain_ref[1:2, :]).astype(BF16)
    logits = dot(routed, router_ref[...], ((1,), (1,)))
    odds = jnp.exp(logits - jnp.max(logits, axis=1, keepdims=True))
    probs = odds / jnp.sum(odds, axis=1, keepdims=True)
    weight_ref[...] = jnp.sum(probs * hot_ref[...], axis=1, keepdims=True)
    sent = dot(choose_ref[...], routed)

    @pl.when(pack == 0)
    def _():
        total[...] = sent

    @pl.when(pack > 0)
    def _():
        total[...] += sent

    @pl.when(pack == pl.num_programs(0) - 1)
    def _():
        sent_ref[...] = total[...].astype(BF16)


def home_forward(sample, u, late, own, mix, tokens, gain, router, hot, chooser):
    operands, specs = late_specs(late, own)
    packs = sample.shape[0]
    rows, model = u.shape
    steps, inner, slots = rows // packs, mix.shape[1], chooser.shape[0]
    whole = lambda v: pl.BlockSpec(v.shape, lambda p, lens: (0, 0))
    part = lambda n: pl.BlockSpec((steps, n), lambda p, lens: (p, 0))
    return pl.pallas_call(
        functools.partial(home_forward_kernel, count=len(operands)),
        grid_spec=pltpu.PrefetchScalarGridSpec(
            num_scalar_prefetch=1,
            grid=(packs,),
            in_specs=[
                part(model), part(inner), part(model), whole(gain), whole(router),
                part(hot.shape[1]), pl.BlockSpec((slots, steps), lambda p, lens: (0, p)), *specs,
            ],
            out_specs=[
                part(inner), part(inner), part(model), part(1), pl.BlockSpec((slots, model), lambda p, lens: (0, 0)),
            ],
            scratch_shapes=[pltpu.VMEM((slots, model), F32), *gate_scratch(operands, model)],
        ),
        out_shape=[
            jax.ShapeDtypeStruct((rows, inner), F32),
            jax.ShapeDtypeStruct((rows, inner), BF16),
            jax.ShapeDtypeStruct((rows, model), F32),
            jax.ShapeDtypeStruct((rows, 1), F32),
            jax.ShapeDtypeStruct((slots, model), BF16),
        ],
        compiler_params=pltpu.CompilerParams(vmem_limit_bytes=56 << 20),
        name="home_forward",
    )(sample, u, mix, tokens, gain, router, hot, chooser, *operands)


def home_backward_kernel(len_ref, choose_ref, back_ref, h1_ref, gy_ref, gain_ref, z_ref, mix_ref, u_ref, gated_ref, *refs,
                         own, count, sums):
    late, refs = refs[:count], refs[count:]
    gh_ref, gm_ref, gu_ref, ggain_ref, *refs = refs
    outs, (sum_z, sum_out, *scratch) = refs[:sums], refs[sums:]
    gates, wout_ref = gate_halves(late, scratch)
    pack = pl.program_id(0)
    steps, model = u_ref.shape

    @pl.when(pack == 0)
    def _():
        ggain_ref[...] = jnp.zeros_like(ggain_ref)
        sum_z[...] = jnp.zeros_like(sum_z)
        sum_out[...] = jnp.zeros_like(sum_out)

    grad = dot(choose_ref[...], back_ref[...], ((0,), (0,)))
    normed, inv = norm_of(h1_ref[...])
    scaled = grad * gain_ref[1:2, :]
    if len(outs) == 1:
        ones = jnp.ones((steps, LANES), BF16)
        high, rest = split_low(grad * normed)
        ggain_ref[...] += dot(high, ones, ((0,), (0,))) + dot(rest, ones, ((0,), (0,)))
    else:
        ggain_ref[...] += jnp.sum(grad * normed, axis=0, keepdims=True)
    gh = gy_ref[...].astype(F32) + inv * (scaled - normed * jnp.mean(scaled * normed, axis=1, keepdims=True))
    gh_ref[...] = gh
    grad_mixed = (live_rows(len_ref[pack], steps) * gh).astype(BF16)
    grad_u = jnp.zeros((steps, model), F32)
    for half, w_ref in enumerate(gates):
        here = slice(half * model, (half + 1) * model)
        grad_gated = dot(grad_mixed, rows_from(wout_ref, here), ((1,), (1,)))
        z = z_ref[:, here]
        sig = jax.nn.sigmoid(z)
        gm_ref[:, here] = grad_gated * (z * sig)
        grad_z = (grad_gated * mix_ref[:, here] * sig * (1.0 + z * (1.0 - sig))).astype(BF16)
        grad_u = grad_u + dot(grad_z, w_ref[...], ((1,), (1,)))
        sum_z[:, here] += dot(u_ref[...], grad_z, ((0,), (0,)))
        sum_out[here, :] += dot(gated_ref[:, here], grad_mixed, ((0,), (0,)))
    gu_ref[...] = grad_u

    @pl.when(pack == pl.num_programs(0) - 1)
    def _():
        if len(outs) == 2:
            outs[0][...] = sum_z[...].astype(BF16)
            outs[1][...] = sum_out[...].astype(BF16)
            return

        def gather(i, _):
            mine = pl.ds(pl.multiple_of(own * i, ROWS), own)
            left = pl.ds(pl.multiple_of(2 * own * i, ROWS), own)
            right = pl.ds(pl.multiple_of(2 * own * i + own, ROWS), own)
            block = jnp.concatenate(
                [sum_z[mine, :], jnp.concatenate([sum_out[left, :], sum_out[right, :]], axis=1)], axis=0
            )
            outs[0][pl.ds(pl.multiple_of(2 * own * i, 2 * own), 2 * own), :] = block.astype(BF16)
            return 0

        lax.fori_loop(0, model // own, gather, 0)


def home_backward(sample, chooser, back, h1, gy, gain, late, own, z, mix, u, gated):
    operands, specs = late_specs(late, own)
    packs = sample.shape[0]
    rows, model = u.shape
    steps, inner, slots = rows // packs, mix.shape[1], chooser.shape[0]
    fixed = lambda p, lens: (0, 0)
    whole = lambda v: pl.BlockSpec(v.shape, fixed)
    part = lambda n: pl.BlockSpec((steps, n), lambda p, lens: (p, 0))
    shard = own // 2
    packed = whole_tiles(shard, inner)
    sums = [(inner, inner)] if packed else [(model, inner), (inner, model)]
    gains = (model, LANES) if packed else (1, model)
    return pl.pallas_call(
        functools.partial(home_backward_kernel, own=shard, count=len(operands), sums=len(sums)),
        grid_spec=pltpu.PrefetchScalarGridSpec(
            num_scalar_prefetch=1,
            grid=(packs,),
            in_specs=[
                pl.BlockSpec((slots, steps), lambda p, lens: (0, p)), whole(back), part(model), part(model), whole(gain),
                part(inner), part(inner), part(model), part(inner), *specs,
            ],
            out_specs=[
                part(model), part(inner), part(model), pl.BlockSpec(gains, fixed),
                *[pl.BlockSpec(shape, fixed) for shape in sums],
            ],
            scratch_shapes=[
                pltpu.VMEM((model, inner), F32), pltpu.VMEM((inner, model), F32), *gate_scratch(operands, model),
            ],
        ),
        out_shape=[
            jax.ShapeDtypeStruct((rows, model), F32),
            jax.ShapeDtypeStruct((rows, inner), F32),
            jax.ShapeDtypeStruct((rows, model), F32),
            jax.ShapeDtypeStruct(gains, F32),
            *[jax.ShapeDtypeStruct(shape, BF16) for shape in sums],
        ],
        compiler_params=pltpu.CompilerParams(vmem_limit_bytes=60 << 20),
        cost_estimate=pl.CostEstimate(flops=0, bytes_accessed=100_000, transcendentals=0),
        name="home_backward",
    )(sample, chooser, back, h1, gy, gain, z, mix, u, gated, *operands)


def expert_grads_kernel(q_ref, gr_ref, *refs, parts):
    gps, acts, outs = refs[:parts], refs[parts : 2 * parts], refs[2 * parts :]
    for k in range(parts):
        outs[2 * k][...] = dot(q_ref[...], gps[k][...], ((0,), (0,))).astype(BF16)
        outs[2 * k + 1][...] = dot(acts[k][...], gr_ref[...], ((0,), (0,))).astype(BF16)


def expert_grads(q, gr, gps, acts):
    rows, model = q.shape
    hidden, parts = gps[0].shape[1], len(gps)
    block = 256 if hidden % 256 == 0 else 128
    whole = pl.BlockSpec((rows, model), lambda i: (0, 0))
    across = lambda n: pl.BlockSpec((n, block), lambda i: (0, i))
    down = pl.BlockSpec((block, model), lambda i: (i, 0))
    return pl.pallas_call(
        functools.partial(expert_grads_kernel, parts=parts),
        grid=(hidden // block,),
        in_specs=[whole, whole] + [across(rows)] * (2 * parts),
        out_specs=[across(model), down] * parts,
        out_shape=[jax.ShapeDtypeStruct((model, hidden), BF16), jax.ShapeDtypeStruct((hidden, model), BF16)] * parts,
        compiler_params=pltpu.CompilerParams(vmem_limit_bytes=60 << 20),
        cost_estimate=pl.CostEstimate(flops=0, bytes_accessed=100_000, transcendentals=0),
        name="expert_grads",
    )(q, gr, *gps, *acts)


def finish_kernel(parts_ref, late_ref, in_ref, out_ref, scan_ref, step_ref, conv_ref, decay_ref, router_ref, *vector_refs,
                  own, rank, taps, states, half):
    total = parts_ref[0].astype(F32)
    for i in range(1, parts_ref.shape[0]):
        total = total + parts_ref[i].astype(F32)
    late = late_ref[...].astype(F32)
    width = total.shape[1]
    model = out_ref.shape[1]
    in_ref[:, :width] = total[:own]
    in_ref[:, width:] = late[:own]
    out_ref[:own, :] = late[own:, :model]
    out_ref[own:, :] = late[own:, model:]
    small = [total[own:, at : at + 2 * LANES] for at in range(0, width, 2 * LANES)]
    first = jnp.concatenate([v[:, :LANES] for v in small], axis=0)
    second = jnp.concatenate([v[:, LANES:] for v in small], axis=0)
    scan_ref[...] = first[:, : rank + 2 * states]
    step_ref[...] = second[:, :rank]
    rows = jnp.concatenate([second, jnp.zeros((LANES - 2 * own, LANES), F32)], axis=0).T
    at = rank + taps + 4
    conv_ref[...] = rows[rank : rank + taps, : 2 * own]
    decay_ref[...] = rows[at : at + states, : 2 * own]
    routers = rows[at + states : at + states + half]
    router_ref[:half, :] = routers[:, :own]
    router_ref[half:, :] = pltpu.roll(routers, LANES - own, 1)[:, :own]
    for i, ref in enumerate(vector_refs[:3]):
        ref[...] = rows[rank + taps + i, : 2 * own]
    gains = rows[at - 1 : at]
    vector_refs[3][...] = gains[0, :own]
    vector_refs[4][...] = pltpu.roll(gains, LANES - own, 1)[0, :own]


def finish(parts, late, own, rank, taps, states, half):
    width = late.shape[1]
    shapes = [
        (own, 2 * width), (2 * own, width // 2), (2 * own, rank + 2 * states), (2 * own, rank), (taps, 2 * own),
        (states, 2 * own), (2 * half, own), (2 * own,), (2 * own,), (2 * own,), (own,), (own,),
    ]
    return pl.pallas_call(
        functools.partial(finish_kernel, own=own, rank=rank, taps=taps, states=states, half=half),
        out_shape=[jax.ShapeDtypeStruct(shape, F32) for shape in shapes],
        name="finish",
    )(parts, late)


def swap(values, axis, mask):
    count = lax.axis_size(axis)
    return lax.ppermute(values, axis, [(i, i ^ mask) for i in range(count)])


def grow(values, axis, mask, dim):
    got = swap(values, axis, mask)
    upper = (lax.axis_index(axis) & mask) != 0
    return jnp.concatenate([jnp.where(upper, got, values), jnp.where(upper, values, got)], axis=dim)


def gather_stages(width):
    count = lax.axis_size("fsdp")
    bits = count.bit_length() - 1
    place = lambda bit: bits - 1 - bit
    half = width // 2

    def upper(values):
        shape = values.shape
        every = jnp.stack([values] + [swap(values, "fsdp", mask) for mask in range(4, count, 4)])
        every = every.reshape((2,) * (bits - 2) + shape)
        for bit in range(2, bits):
            flipped = (lax.axis_index("fsdp") & (1 << bit)) != 0
            every = jnp.where(flipped, jnp.flip(every, place(bit)), every)
        return every.reshape((2,) * (bits - 2) + (1, 1) + shape)

    def split(values):
        return grow(values[..., :half], "fsdp", 2, place(1)), grow(values[..., half:], "fsdp", 1, place(0))

    def join(pair):
        left, right = grow(pair[0], "fsdp", 1, place(0)), grow(pair[1], "fsdp", 2, place(1))
        return jnp.concatenate([left, right], axis=-1)

    def across(mask):
        return lambda values: grow(values.reshape(1, -1, width), "dp", mask, 0)

    masks = [1 << i for i in range(lax.axis_size("dp").bit_length() - 1)]
    return [upper, split, join] + [across(mask) for mask in masks]


def gather_both(first, second, beside):
    shapes = [(-1, v.shape[1]) for v in (first, second)]
    values = [first, second]
    steps = [gather_stages(v.shape[1]) for v in values]
    count = len(steps[0])
    for at in range(count + 1):
        if at:
            *values, beside = lax.optimization_barrier((*values, beside))
        if at < count:
            values[0] = steps[0][at](values[0])
        if at:
            values[1] = steps[1][at - 1](values[1])
    return [v.reshape(shape) for v, shape in zip(values, shapes)] + [beside]


def fold(values, count):
    rows = values.shape[-2] // count
    return jnp.concatenate([values[..., j * rows : (j + 1) * rows, :] for j in range(count)], axis=-1)


def unfold(values, count):
    width = values.shape[-1] // count
    return jnp.concatenate([values[..., j * width : (j + 1) * width] for j in range(count)], axis=-2)


def own_block(values, index, count, axis):
    size = values.shape[axis] // count
    return lax.dynamic_slice_in_dim(values, index * size, size, axis)


def scatter_begin(pieces):
    sent = [swap(piece.astype(BF16), "dp", k + 1) for k, piece in enumerate(pieces[1:])]
    total = pieces[0].astype(F32)
    for got in sent:
        total = total + got.astype(F32)
    return total.astype(BF16)


def body(
    tokens,
    cotangent,
    routes,
    lengths,
    norm1_gain,
    input_weight,
    conv_weight,
    conv_bias,
    scan_weight,
    step_weight,
    step_bias,
    decay_log,
    skip_gain,
    out_weight,
    norm2_gain,
    router_weight,
    expert_up,
    expert_down,
):
    micro, steps, model = tokens.shape
    rows = micro * steps
    experts = lax.axis_size("fsdp")
    groups = lax.axis_size("dp")
    devices = experts * groups
    capacity = (5 * steps + 4 * experts - 1) // (4 * experts)
    slots = micro * capacity
    inner = input_weight.shape[1] // 2
    states = decay_log.shape[1]
    rank = step_weight.shape[1]
    taps = conv_weight.shape[1]
    own_model, own_inner = norm1_gain.shape[0], conv_bias.shape[0]

    packed = whole_tiles(own_model, inner)

    def gains_in(first, second):
        pair = [v.reshape(devices, 1, own_model) for v in (first, second)]
        column = jnp.concatenate(pair, axis=1).reshape(inner, 1)
        return jnp.where(jnp.arange(LANES) == rank + taps + 3, column, 0.0)

    half = experts // 2
    vectors = jnp.concatenate(
        [
            conv_weight,
            jnp.stack([conv_bias, step_bias, skip_gain, jnp.concatenate([norm1_gain, norm2_gain])]).T,
            decay_log,
            jnp.concatenate([router_weight[:, :half], router_weight[:, half:]], axis=0),
        ],
        axis=1,
    )
    padding = lambda n: jnp.zeros((own_inner, n), BF16)
    small = jnp.concatenate(
        [
            scan_weight,
            padding(LANES - rank - 2 * states),
            step_weight,
            vectors,
            padding(LANES - rank - vectors.shape[1]),
        ],
        axis=1,
    )
    folds = inner // (2 * LANES)
    late = jnp.concatenate([input_weight[:, inner : inner + model], input_weight[:, inner + model :], out_weight], axis=0)
    late = lax.all_gather(late, ("dp", "fsdp"), axis=0, tiled=False)
    ups = [expert_up[0]] + [swap(expert_up[0], "dp", k) for k in range(1, groups)]
    downs = [expert_down[0]] + [swap(expert_down[0], "dp", k) for k in range(1, groups)]

    place = jnp.arange(steps, dtype=jnp.int32)
    sample = lengths[:, 0, 0]
    live = (place[None, :] < sample[:, None]).astype(jnp.int32)
    route = routes[:, :, 0]
    expert_ids = jnp.arange(experts, dtype=jnp.int32)
    route_hot = (route[:, :, None] == expert_ids).astype(BF16)
    live_hot = route_hot * live[:, :, None].astype(BF16)
    earlier = (place[:, None] > place[None, :]).astype(BF16)
    before = lax.dot_general(
        jnp.broadcast_to(earlier, (micro, steps, steps)), live_hot, (((2,), (1,)), ((0,), (0,))),
        preferred_element_type=F32,
    )
    slot = jnp.sum(before * live_hot.astype(F32), axis=2).astype(jnp.int32)
    kept = (live * (slot < capacity).astype(jnp.int32)).reshape(rows)
    target = (route * slots + jnp.arange(micro, dtype=jnp.int32)[:, None] * capacity + slot).reshape(rows)
    chooser = (
        (jnp.arange(experts * slots, dtype=jnp.int32)[:, None] == target[None, :]) & (kept[None, :] == 1)
    ).astype(BF16)
    kept = kept.astype(F32)

    def to_experts(values):
        return lax.all_to_all(values.reshape(experts, slots, -1), "fsdp", 0, 0, tiled=True).reshape(experts * slots, -1)

    def from_experts(values):
        return dot(chooser, values.reshape(experts * slots, -1), ((0,), (0,)))

    def back_home(values):
        return lax.all_to_all(values.reshape(experts, slots, -1), "fsdp", 0, 0, tiled=True)

    cotangent = cotangent.reshape(rows, model)

    input_x, small_full, upstream_rows = gather_both(
        input_weight[:, :inner], small, dot(chooser, cotangent).astype(BF16)
    )
    upstream_sent = to_experts(upstream_rows)
    tokens = tokens.reshape(rows, model)
    mixer_in = [sample, tokens, input_x, small_full, None, None]
    if not packed:
        vectors_full = small_full[:, LANES + rank :].T
        vectors_first = vectors_full[:ROWS].astype(F32)
        decay_two = -jnp.exp(vectors_full[taps + 4 : taps + 4 + states].astype(F32)) * LOG2E
        gains = vectors_full[taps + 3].reshape(devices, 2, own_model).transpose(1, 0, 2).reshape(2, model).astype(F32)
        router_full = vectors_full[taps + 4 + states : taps + 4 + states + half].reshape(half, devices, 2, own_model)
        router_full = router_full.transpose(2, 0, 1, 3).reshape(experts, model)
        hidden = tokens.astype(F32)
        inv_first = lax.rsqrt(jnp.mean(hidden * hidden, axis=-1, keepdims=True) + EPSILON)
        normed_low = (hidden * inv_first * gains[:1]).astype(BF16)
        mixer_in = [sample, normed_low, input_x, small_full, vectors_first, decay_two]
    mixer_outs = mixer_forward(*mixer_in, micro, rank, taps, states, own_model if packed else 0, half)
    branch_x, scan_in, step_size, selected, mixer_out, states_kept = mixer_outs[:6]
    if packed:
        vectors_first, decay_two, gains, router_full, normed_low = mixer_outs[6:]
    mixer_out, upstream_sent = lax.optimization_barrier((mixer_out, upstream_sent))
    kept_hot = route_hot.reshape(rows, experts).astype(F32) * kept[:, None]
    branch_z, gated_low, residual, weight_row, sent = home_forward(
        sample, normed_low, late, own_inner, mixer_out, tokens, gains, router_full, kept_hot, chooser,
    )
    received = to_experts(sent)

    mine = (expert_ids == lax.axis_index("fsdp")).astype(F32)[None, :]
    result, grad_rows, flat_grad, router_grad, acts, grad_pres = expert_pass(
        received, upstream_sent, router_full, mine, ups, downs
    )
    grad_rows, result, received, flat_grad = lax.optimization_barrier((grad_rows, result, received, flat_grad))
    grad_back = back_home(grad_rows)
    matrix_grads = expert_grads(received, flat_grad, grad_pres, acts)
    at_gain, at_decay, at_router = rank + taps + 3, rank + taps + 4, rank + taps + 4 + states
    lane = jnp.arange(LANES)
    router_grads = router_grad.reshape(2, half, devices, own_model).transpose(2, 0, 3, 1).reshape(inner, half)
    extra = jnp.pad(router_grads, ((0, 0), (at_router, LANES - at_router - half)))
    gain_row = gains[:1]
    grad_back, matrix_grads, extra, gain_row, result = lax.optimization_barrier(
        (grad_back, matrix_grads, extra, gain_row, result)
    )
    result = back_home(result)
    up_own, down_own, *others = matrix_grads
    others = [swap(other, "dp", k // 2 + 1) for k, other in enumerate(others)]

    grad_residual, grad_mixer, grad_normed_z, gain_two_grad, *late_terms = home_backward(
        sample, chooser, grad_back.reshape(experts * slots, model), residual, cotangent, gains, late,
        own_inner, branch_z, mixer_out, normed_low, gated_low,
    )
    if not packed:
        blocks = [v.reshape(devices, -1, v.shape[1]) for v in late_terms]
        late_terms = [jnp.concatenate([blocks[0], fold(blocks[1], 2)], axis=1).reshape(-1, inner)]
    late_grads = lax.psum_scatter(late_terms[0], ("dp", "fsdp"), scatter_dimension=0, tiled=True)
    if not packed:
        extra = extra + gains_in(jnp.zeros_like(gain_two_grad), gain_two_grad)
    grad_mixer, others = lax.optimization_barrier((grad_mixer, others))
    mixer_grads = mixer_backward(
        jnp.append(sample, lax.axis_index("dp")), step_size, scan_in, branch_x, grad_mixer, selected, small_full, vectors_first, decay_two,
        states_kept, input_x, tokens, gain_row, grad_normed_z, grad_residual, normed_low, extra,
        gain_two_grad, micro, rank, taps, at_gain, own_model, groups,
    )
    if packed:
        *early_terms, tokens_grad = mixer_grads
        early_terms = [terms.reshape(experts, -1, inner) for terms in early_terms]
    else:
        tokens_grad, input_x_grad, select_grad, step_grad, gain_one_grad = mixer_grads
        step_grad = step_grad + gains_in(gain_one_grad, jnp.zeros_like(gain_one_grad))
        blocks = jnp.concatenate([select_grad, step_grad], axis=1).reshape(devices, own_inner, 2 * LANES)
        blocks = jnp.concatenate([input_x_grad.reshape(devices, own_model, inner), fold(blocks, folds)], axis=1)
        blocks = blocks.reshape(groups, experts, -1, inner)
        me = lax.axis_index("dp")
        early_terms = [lax.dynamic_index_in_dim(blocks, me ^ k, 0, False) for k in range(groups)]
    early_terms, result = lax.optimization_barrier((early_terms, result))
    early_terms = scatter_begin(early_terms)
    early_terms, others, result = lax.optimization_barrier((early_terms, others, result))
    early_parts = lax.all_to_all(early_terms, "fsdp", 0, 0, tiled=True)
    up_grad, down_grad = up_own.astype(F32), down_own.astype(F32)
    for k in range(groups - 1):
        up_grad = up_grad + others[2 * k].astype(F32)
        down_grad = down_grad + others[2 * k + 1].astype(F32)
    block_output = (residual + weight_row * from_experts(result)).astype(BF16)
    if packed:
        in_grad, out_grad, scan_grad, step_grad, conv_grad, decay_grad, router_grad, *vector_grads = finish(
            early_parts, late_grads, own_model, rank, taps, states, half
        )
        conv_grad, decay_grad, router_grad = conv_grad.T, decay_grad.T, router_grad.T
    else:
        early_grads = jnp.sum(early_parts.astype(F32), axis=0)
        late_grads = late_grads.astype(F32)
        in_grad = jnp.concatenate([early_grads[:own_model], late_grads[:own_model]], axis=1)
        out_grad = unfold(late_grads[own_model:], 2)
        small_grads = unfold(early_grads[own_model:], folds)
        scan_grad, step_grad = small_grads[:, : rank + 2 * states], small_grads[:, LANES : LANES + rank]
        small_grads = small_grads[:, LANES:]
        conv_grad = small_grads[:, rank : rank + taps]
        decay_grad = small_grads[:, at_decay : at_decay + states]
        routers = small_grads[:, at_router : at_router + half]
        router_grad = jnp.concatenate([routers[:own_model], routers[own_model:]], axis=1)
        *vector_grads, gain_grads = [small_grads[:, rank + taps + i] for i in range(4)]
        vector_grads += [gain_grads[:own_model], gain_grads[own_model:]]
    conv_bias_grad, step_bias_grad, skip_grad, gain_one_grad, gain_two_grad = vector_grads
    return (
        block_output.reshape(micro, steps, model),
        tokens_grad.reshape(micro, steps, model),
        gain_one_grad,
        in_grad,
        conv_grad,
        conv_bias_grad,
        scan_grad,
        step_grad,
        step_bias_grad,
        decay_grad,
        skip_grad,
        out_grad,
        gain_two_grad,
        router_grad,
        up_grad[None],
        down_grad[None],
    )


def solution(mesh):
    rows3 = P(None, ("dp", "fsdp"), None)
    vector = P(("dp", "fsdp"))
    matrix = P(("dp", "fsdp"), None)
    weights = (
        vector, matrix, matrix, vector, matrix, matrix, vector, matrix, vector, matrix, vector, matrix,
        P("fsdp", None, "dp"), P("fsdp", "dp", None),
    )
    return jax.shard_map(
        body,
        mesh=mesh,
        in_specs=(rows3, rows3, rows3, rows3) + weights,
        out_specs=(rows3, rows3) + weights,
        check_vma=False,
    )
```
